256 devices in a mesh: leaf: 16 (over y, x), top: 16 (over z, core).
Axes of the slice: x: 4, y: 4, z: 8, core: 2. Of those that a mesh axis runs over, the one named last changes fastest.
Arguments:
- rhs: bfloat16 [2, 262144, 256], P(None, ('leaf', 'top')), may hold values from -6 to 6
- diag_blocks: bfloat16 [2, 512, 512, 512], P(None, ('leaf', 'top')), may hold values from -0.1875 to 0.1875
- row_basis: bfloat16 [2, 512, 512, 256], P(None, ('leaf', 'top')), may hold values from -0.125 to 0.125
- col_basis: bfloat16 [2, 512, 512, 256], P(None, ('leaf', 'top')), may hold values from -0.1875 to 0.1875
- local_pair: bfloat16 [2, 256, 2, 256, 256], P(None, ('leaf', 'top')), may hold values from -0.21875 to 0.21875
- local_couple: bfloat16 [2, 256, 256, 256], P(None, ('leaf', 'top')), may hold values from -0.25 to 0.25
- cross_pair: bfloat16 [2, 256, 8, 2, 256, 256], P(None, ('leaf', 'top')), may hold values from -0.21650635 to 0.21650635, as said below
- cross_couple: bfloat16 [2, 256, 8, 256, 256], P(None, ('leaf', 'top')), may hold values from -0.42474313 to 0.42474313, as said below
- leaf_map: int32 [256, 2], P(('leaf', 'top')), may hold values from 0 to 1, each once within a row
Outputs:
- applied: bfloat16 [2, 262144, 256], P(None, ('leaf', 'top'))
The draws below stay inside these ranges and needn't reach their ends.
Inputs may be any that keep to these rules, and one draw needn't show every extreme that they name: `leaf_map`: each row lists the 2 row blocks of one device, each once. `cross_pair`: the slices [:, d, k] of all devices d with the same d // 2^(k+1) are equal. `cross_couple`: the slices [:, d, k] of all devices d with the same d // 2^(k+1) are equal.
All inputs are finite; a program needn't handle non-finite values.
Results may differ from the reference program's by a relative error of at most 0.023.
Values may be sent and summed in bfloat16 or wider, within the bound.
No kernel may reach another device: no remote copies, remote signals or barrier semaphores. Data moves between devices by JAX's collectives and lax.ppermute only.
A program may use at most 64 MiB of HBM per device.

```python
import math
import jax
import jax.numpy as jnp
from jax import lax

LEAF = 512
RANK = 256
NRHS = 256
LEAF_DEV = 2
SPLITS = 256
BITS = 8
LEAVES = 512
ORDER = 262144


def draw_cross_pair(key, part):
    key = jax.random.fold_in(key, 7)
    levels = []
    for height in range(BITS):
        sub_key = jax.random.fold_in(key, height)
        node_count = SPLITS // 2 ** (height + 1)
        values = jnp.clip(jax.random.normal(sub_key, (2, node_count, 1, 2, RANK, RANK), jnp.float32), -6.0, 6.0)
        levels.append(jnp.repeat(values, 2 ** (height + 1), axis=1))
    return (jnp.concatenate(levels, axis=2) / math.sqrt(3.0 * RANK)).astype(jnp.bfloat16)


def draw_cross_couple(key, part):
    key = jax.random.fold_in(key, 9)
    levels_below = LEAF_DEV.bit_length() - 1
    levels = []
    for height in range(BITS):
        sub_key = jax.random.fold_in(key, height)
        node_count = SPLITS // 2 ** (height + 1)
        growth = 1.125 ** ((levels_below + height) / 2.0)
        values = jnp.clip(jax.random.normal(sub_key, (2, node_count, 1, RANK, RANK), jnp.float32), -6.0, 6.0)
        levels.append(jnp.repeat(values * growth, 2 ** (height + 1), axis=1))
    return (jnp.concatenate(levels, axis=2) / math.sqrt(2.0 * RANK)).astype(jnp.bfloat16)


def shard_levels(stream_key, extent, split, least, high):
    gain, own = 1.0, jax.random.fold_in(stream_key, 6)
    for axis_at, blocks in split:
        draws = jnp.exp(jax.random.uniform(jax.random.fold_in(own, axis_at), (blocks,), jnp.float32, least / len(split), high / len(split)))
        gain = gain * jnp.repeat(draws, extent[axis_at] // blocks).reshape([-1 if axis == axis_at else 1 for axis in range(len(extent))])
    return gain


def bell_draw(own_key, dims, width, bound, cuts=(), held_as=jnp.bfloat16):
    drawn = jax.random.normal(own_key, dims, jnp.float32) * width
    if len(cuts) > 0:
        drawn = shard_levels(own_key, dims, cuts, -0.22, 0.18) * drawn
    return jnp.clip(drawn, min=-bound, max=bound).astype(held_as)


def setup_inputs(seed: int = 0) -> dict:
    seeds = jax.random.split(jax.random.key(seed), 10)
    rhs = bell_draw(seeds[0], (2, ORDER, NRHS), 1.0, 6.0, ((1, 256),))
    diag_blocks = bell_draw(seeds[1], (2, LEAVES, LEAF, LEAF), (2 * LEAF) ** -0.5, 0.1875, ((1, 256),))
    row_basis = bell_draw(seeds[2], (2, LEAVES, LEAF, RANK), (8 * RANK) ** -0.5, 0.125, ((1, 256),))
    col_basis = bell_draw(seeds[3], (2, LEAVES, LEAF, RANK), (2 * LEAF) ** -0.5, 0.1875, ((1, 256),))
    local_pair = bell_draw(seeds[4], (2, SPLITS * (LEAF_DEV - 1), 2, RANK, RANK), (3 * RANK) ** -0.5, 0.21875, ((1, 256),))
    local_couple = bell_draw(seeds[5], (2, SPLITS * (LEAF_DEV - 1), RANK, RANK), (2 * RANK) ** -0.5, 0.25, ((1, 256),))
    cross_pair = draw_cross_pair(jax.random.fold_in(seeds[9], 71), 0)
    cross_couple = draw_cross_couple(jax.random.fold_in(seeds[9], 71), 0)
    leaf_map = jax.vmap(lambda own: jax.random.permutation(own, LEAF_DEV))(jax.random.split(seeds[8], SPLITS)).reshape((SPLITS, LEAF_DEV)).astype(jnp.int32)
    return {"rhs": rhs, "diag_blocks": diag_blocks, "row_basis": row_basis, "col_basis": col_basis, "local_pair": local_pair, "local_couple": local_couple, "cross_pair": cross_pair, "cross_couple": cross_couple, "leaf_map": leaf_map}


def complex_dot(first_arg, second_arg):
    real_part = jnp.dot(first_arg[0], second_arg[0], preferred_element_type=jnp.float32) - jnp.dot(first_arg[1], second_arg[1], preferred_element_type=jnp.float32)
    imag_part = jnp.dot(first_arg[0], second_arg[1], preferred_element_type=jnp.float32) + jnp.dot(first_arg[1], second_arg[0], preferred_element_type=jnp.float32)
    return jnp.stack([real_part, imag_part])


def complex_tdot(first_arg, second_arg):
    return complex_dot(jnp.swapaxes(first_arg, 1, 2), second_arg)


def reference(rhs, diag_blocks, row_basis, col_basis, local_pair, local_couple, cross_pair, cross_couple, leaf_map):
    leaf_total = SPLITS * LEAF_DEV
    order_ids = (jnp.arange(SPLITS, dtype=jnp.int32)[:, None] * LEAF_DEV + leaf_map.astype(jnp.int32)).reshape(leaf_total).astype(jnp.int32)
    blocks = rhs.reshape(2, leaf_total, LEAF, NRHS)[:, order_ids]

    def leaf_skeleton(index):
        return complex_tdot(col_basis[:, index], blocks[:, index])

    skeleton = lax.map(leaf_skeleton, jnp.arange(leaf_total, dtype=jnp.int32))
    generators = []
    local_w = local_pair.reshape(2, SPLITS, LEAF_DEV - 1, 2, RANK, RANK)
    local_b = local_couple.reshape(2, SPLITS, LEAF_DEV - 1, RANK, RANK)
    offset = 0
    parents = LEAF_DEV // 2
    for height in range(LEAF_DEV.bit_length() - 1):
        w_pairs = local_w[:, :, offset:offset + parents].reshape(2, SPLITS * parents, 2, RANK, RANK)
        b_mats = local_b[:, :, offset:offset + parents].reshape(2, SPLITS * parents, RANK, RANK)
        generators.append((w_pairs, b_mats))
        offset = offset + parents
        parents = parents // 2
    for height in range(BITS):
        stride = 2 ** (height + 1)
        generators.append((cross_pair[:, ::stride, height], cross_couple[:, ::stride, height]))
    saved = []
    for index in range(len(generators)):
        w_pairs = generators[index][0]
        rounded = skeleton.astype(jnp.bfloat16)
        saved.append(rounded)
        if index + 1 < len(generators):
            def lift(parent, rounded=rounded, w_pairs=w_pairs):
                return complex_tdot(w_pairs[:, parent, 0], rounded[2 * parent]) + complex_tdot(w_pairs[:, parent, 1], rounded[2 * parent + 1])

            skeleton = lax.map(lift, jnp.arange(w_pairs.shape[1], dtype=jnp.int32))
    above_node = jnp.zeros((1, 2, RANK, NRHS), jnp.float32)
    for index in reversed(range(len(generators))):
        w_pairs, b_mats = generators[index]
        rounded = saved[index]

        def lower(parent, rounded=rounded, w_pairs=w_pairs, b_mats=b_mats, above_node=above_node):
            upper_bf = above_node[parent].astype(jnp.bfloat16)
            b_here = b_mats[:, parent]
            first_child = complex_dot(b_here, rounded[2 * parent + 1]) + complex_dot(w_pairs[:, parent, 0], upper_bf)
            second_child = complex_dot(jnp.swapaxes(b_here, 1, 2), rounded[2 * parent]) + complex_dot(w_pairs[:, parent, 1], upper_bf)
            return jnp.stack([first_child, second_child])

        parent_count = w_pairs.shape[1]
        above_node = lax.map(lower, jnp.arange(parent_count, dtype=jnp.int32)).reshape(2 * parent_count, 2, RANK, NRHS)

    def finish(index):
        total = complex_dot(diag_blocks[:, index], blocks[:, index]) + complex_dot(row_basis[:, index], above_node[index].astype(jnp.bfloat16))
        return total.astype(jnp.bfloat16)

    result = lax.map(finish, jnp.arange(leaf_total, dtype=jnp.int32))
    result = jnp.moveaxis(result, 0, 1)
    placed = jnp.zeros_like(result).at[:, order_ids].set(result)
    return placed.reshape(2, leaf_total * LEAF, NRHS)
```

```python
import jax
import jax.numpy as jnp
from jax import lax
from jax.experimental import pallas as pl
from jax.experimental.pallas import tpu as pltpu
from jax.sharding import PartitionSpec as P

BF = jnp.bfloat16
F32 = jnp.float32
NN = (((1,), (0,)), ((), ()))
NT = (((1,), (1,)), ((), ()))


def dot(a, b, dims=NN):
    return lax.dot_general(a, b, dims, preferred_element_type=F32)


def cmul(a, w_re, w_im, dims=NN):
    half = a.shape[0] // 2
    p = dot(a, w_re, dims)
    q = dot(a, w_im, dims)
    return jnp.concatenate([p[:half] - q[half:], p[half:] + q[:half]], axis=0)


def rows(ref, *at):
    return jnp.concatenate([ref[(0,) + at], ref[(1,) + at]], axis=0)


def put(ref, value, *at):
    half = value.shape[0] // 2
    ref[(0,) + at] = value[:half].astype(ref.dtype)
    ref[(1,) + at] = value[half:].astype(ref.dtype)


def lift(q, w, level, child):
    return cmul(q, w[0, level, child], w[1, level, child])


def lower(h, w, level, child):
    return cmul(h, w[0, level, child], w[1, level, child], NT)


def couple_left(q_right, b, level):
    return cmul(q_right, b[0, level], b[1, level], NT)


def couple_right(q_left, b, level):
    return cmul(q_left, b[0, level], b[1, level], NN)


def couple(q_other, b, level, child):
    return lax.cond(
        child == 0,
        lambda: couple_left(q_other, b, level),
        lambda: couple_right(q_other, b, level),
    )


def couple_both(q_own, q_other, b, level, child):
    q_left = jnp.where(child == 0, q_own, q_other)
    q_right = jnp.where(child == 0, q_other, q_own)
    left = couple_left(q_right, b, level)
    right = couple_right(q_left, b, level)
    return jnp.where(child == 0, left, right), jnp.where(child == 0, right, left)


def leaf_kernel(pos, order, x, u, wl, w, qleaf, q0, out, order_s, x_v, u_v, wl_v, w_v, sems):
    copies = [
        pltpu.make_async_copy(order, order_s, sems.at[0]),
        pltpu.make_async_copy(x.at[:], x_v.at[:], sems.at[1]),
        pltpu.make_async_copy(u.at[:, 0], u_v.at[:, 0], sems.at[2]),
        pltpu.make_async_copy(u.at[:, 1], u_v.at[:, 1], sems.at[3]),
        pltpu.make_async_copy(wl.at[:, 0], wl_v.at[:], sems.at[4]),
        pltpu.make_async_copy(w.at[:, 0], w_v.at[:], sems.at[5]),
    ]
    for copy in copies:
        copy.start()
    copies[0].wait()
    copies[1].wait()
    size = u.shape[2]
    for leaf in range(2):
        at = pl.ds(pl.multiple_of(order_s[0, leaf] * size, size), size)
        xt = jnp.concatenate([x_v[0, at].T, x_v[1, at].T], axis=0)
        copies[2 + leaf].wait()
        qleaf[leaf] = cmul(xt, u_v[0, leaf], u_v[1, leaf]).astype(BF)
    copies[4].wait()
    q = cmul(qleaf[0], wl_v[0, 0], wl_v[1, 0]) + cmul(qleaf[1], wl_v[0, 1], wl_v[1, 1])
    q = q.astype(BF)
    put(q0, q)
    copies[5].wait()
    bit = pos[0] & 1
    spread(out, cmul(q, w_v[0, bit], w_v[1, bit]).astype(BF))


def spread(out, value):
    blocks, _, part, _ = out.shape
    for i in range(blocks):
        for c in range(2):
            at = (c * blocks + i) * part
            out[i, c] = value[at : at + part]


def pick(got, i):
    return rows(got.at[i]).astype(F32)


def mid_kernel(pos, got, w, q_own, q_oth, q_up, out):
    digit = pos[0] & 3
    qa = (pick(got, digit) + pick(got, digit ^ 1)).astype(BF)
    qb = (pick(got, digit ^ 2) + pick(got, digit ^ 3)).astype(BF)
    put(q_own, qa)
    put(q_oth, qb)
    bit = digit >> 1
    up = (lift(qa, w, 1, bit) + lift(qb, w, 1, 1 - bit)).astype(BF)
    put(q_up, up)
    spread(out, lift(up, w, 2, (pos[0] >> 2) & 1).astype(BF))


def mid_last_kernel(pos, got, w, q_own, q_oth, out):
    digit = (pos[0] >> 2) & 3
    qa = (pick(got, digit) + pick(got, digit ^ 1)).astype(BF)
    qb = (pick(got, digit ^ 2) + pick(got, digit ^ 3)).astype(BF)
    put(q_own, qa)
    put(q_oth, qb)
    bit = digit >> 1
    part = (lift(qa, w, 3, bit) + lift(qb, w, 3, 1 - bit)).astype(BF)
    leaf = pos[0] >> 4
    put(out.at[leaf], part)
    for level in range(4):
        if level > 0:
            part = lift(part, w, 3 + level, (leaf >> (level - 1)) & 1).astype(BF)
        for flip in range(2**level, 2 ** (level + 1)):
            put(out.at[leaf ^ flip], part)


def store_both(out, digit, own, oth):
    for flip, value in enumerate((own, own, oth, oth)):
        put(out.at[digit ^ flip], value)


def top_kernel(pos, got, q_own3, q_oth3, w, b, out):
    def bit(level):
        return (pos[0] >> level) & 1

    leaf = pos[0] >> 4
    own3, oth3 = couple_both(rows(q_own3), rows(q_oth3), b, 3, bit(3))
    h = None
    for level in reversed(range(4)):
        q_sib = pick(got, leaf ^ 2**level)
        for flip in range(2**level + 1, 2 ** (level + 1)):
            q_sib = q_sib + pick(got, leaf ^ flip)
        c = couple(q_sib.astype(BF), b, 4 + level, bit(4 + level))
        h = c if h is None else c + lower(h.astype(BF), w, 4 + level, bit(4 + level))
    h = h.astype(BF)
    store_both(
        out,
        (pos[0] >> 2) & 3,
        (own3 + lower(h, w, 3, bit(3))).astype(BF),
        (oth3 + lower(h, w, 3, 1 - bit(3))).astype(BF),
    )


def gather(got):
    blocks = got.shape[0]
    return jnp.concatenate([got[i, c] for c in range(2) for i in range(blocks)], axis=0)


def down_kernel(pos, got, c2, c1_own, c1_oth, w, out):
    def bit(level):
        return (pos[0] >> level) & 1

    h = (rows(c2) + lower(gather(got), w, 2, bit(2))).astype(BF)
    store_both(
        out,
        pos[0] & 3,
        (rows(c1_own) + lower(h, w, 1, bit(1))).astype(BF),
        (rows(c1_oth) + lower(h, w, 1, 1 - bit(1))).astype(BF),
    )


def couple_kernel(pos, q_sib2, q_own1, q_oth1, b, c2, c1_own, c1_oth):
    put(c2, couple(rows(q_sib2), b, 2, (pos[0] >> 2) & 1))
    own, oth = couple_both(rows(q_own1), rows(q_oth1), b, 1, (pos[0] >> 1) & 1)
    put(c1_own, own)
    put(c1_oth, oth)


def low_couple_kernel(pos, q_sib0, qleaf, bl, b, c0, cleaf):
    put(c0, couple(rows(q_sib0), b, 0, pos[0] & 1))
    cleaf[0] = couple_left(qleaf[1], bl, 0)
    cleaf[1] = couple_right(qleaf[0], bl, 0)


def direct_kernel(order, x, d, out):
    size = d.shape[2]
    n = x.shape[2]
    tile = 128
    for leaf in range(2):
        start = pl.multiple_of(order[0, leaf] * size, size)
        xs = jnp.concatenate([x[0, pl.ds(start, size)], x[1, pl.ds(start, size)]], axis=1)

        def body(step, carry):
            at = pl.ds(pl.multiple_of(step * tile, tile), tile)
            to = pl.ds(pl.multiple_of(start + step * tile, tile), tile)
            p = dot(d[0, leaf, at], xs)
            q = dot(d[1, leaf, at], xs)
            out[0, to] = p[:, :n] - q[:, n:]
            out[1, to] = p[:, n:] + q[:, :n]
            return carry

        lax.fori_loop(0, size // tile, body, 0)


def last_kernel(pos, order, got, c0, cleaf, direct, w, wl, r, out):
    size = r.shape[2]
    n = out.shape[2]
    h = (rows(c0) + lower(gather(got), w, 0, pos[0] & 1)).astype(BF)
    tile = 256
    for leaf in range(2):
        hl = (cleaf[leaf] + lower(h, wl, 0, leaf)).astype(BF)
        start = pl.multiple_of(order[0, leaf] * size, size)
        for step in range(size // tile):
            at = pl.ds(step * tile, tile)
            to = pl.ds(pl.multiple_of(start + step * tile, tile), tile)
            p = dot(r[0, leaf, at], hl, NT)
            q = dot(r[1, leaf, at], hl, NT)
            out[0, to] = (direct[0, to] + (p[:, :n] - q[:, n:])).astype(BF)
            out[1, to] = (direct[1, to] + (p[:, n:] + q[:, :n])).astype(BF)


VMEM = pl.BlockSpec(memory_space=pltpu.VMEM)
SMEM = pl.BlockSpec(memory_space=pltpu.SMEM)
HBM = pl.BlockSpec(memory_space=pltpu.HBM)
GRANT = 20 * 2**20


def call(kernel, ins, outs, *args, scratch=(), flops=0, name=None):
    specs = {"s": SMEM, "v": VMEM, "a": HBM}
    moved = sum(a.size * a.dtype.itemsize for a in args)
    return pl.pallas_call(
        kernel,
        out_shape=[jax.ShapeDtypeStruct(shape, dtype) for shape, dtype in outs],
        in_specs=[specs[kind] for kind in ins],
        out_specs=[VMEM] * len(outs),
        scratch_shapes=list(scratch),
        compiler_params=pltpu.CompilerParams(vmem_limit_bytes=GRANT),
        cost_estimate=pl.CostEstimate(flops=flops, bytes_accessed=moved, transcendentals=0),
        name=name,
    )(*args)


def shards(rhs, diag, row_basis, col_basis, wl, bl, cross_w, cross_b, order):
    n = rhs.shape[2]
    rank = col_basis.shape[3]
    top = lax.axis_index("top")
    leaf = lax.axis_index("leaf")
    pos = (leaf * lax.axis_size("top") + top).astype(jnp.int32).reshape(1)
    w = cross_w[:, 0]
    b = cross_b[:, 0]

    def swap(value, flip):
        return lax.ppermute(value, "top", [(i, i ^ flip) for i in range(lax.axis_size("top"))])

    def exchange(value, axis, group):
        return lax.all_to_all(value, axis, 0, 0, axis_index_groups=group, tiled=True)

    near = [[4 * i + j for j in range(4)] for i in range(4)]
    far = [[i + 4 * j for j in range(4)] for i in range(4)]
    full, quarter, part = (2, n, rank), (2, n // 4, rank), (2, n // 16, rank)
    mac = 8 * rank * rank
    hbm = [pltpu.with_memory_space_constraint(a, pltpu.HBM) for a in (order, rhs, col_basis, wl, w)]
    qleaf, q0, out = call(
        leaf_kernel, "saaaaa",
        [((2, 2 * n, rank), BF), (full, BF), ((4,) + quarter, BF)],
        pos, *hbm,
        scratch=(
            pltpu.SMEM(order.shape, jnp.int32),
            pltpu.VMEM(rhs.shape, BF),
            pltpu.VMEM(col_basis.shape, BF),
            pltpu.VMEM((2, 2, rank, rank), BF),
            pltpu.VMEM((2, 2, rank, rank), BF),
            pltpu.SemaphoreType.DMA((6,)),
        ),
        flops=mac * n * 7, name="leaf_skeletons",
    )
    got = exchange(out, "top", near)
    q_sib0 = swap(q0, 1)
    q_own1, q_oth1, q2, out = call(
        mid_kernel, "svv",
        [(quarter, BF), (quarter, BF), (quarter, BF), ((4,) + part, BF)],
        pos, got, w, flops=mac * n, name="levels_0_1",
    )
    got = exchange(out, "top", far)
    q_sib2 = swap(q2, 4)
    q_own3, q_oth3, out = call(
        mid_last_kernel, "svv", [(part, BF), (part, BF), ((16,) + part, BF)],
        pos, got, w, flops=mac * n // 4, name="levels_2_5",
    )
    got = exchange(out, "leaf", None)
    (direct,) = call(
        direct_kernel, "svv", [(rhs.shape, F32)], order, rhs, diag,
        flops=mac * n * 8, name="direct",
    )
    c0, cleaf = call(
        low_couple_kernel, "svvvv", [(full, F32), (qleaf.shape, F32)],
        pos, q_sib0, qleaf, bl, b, flops=mac * n * 3, name="low_coupled",
    )
    c2, c1_own, c1_oth = call(
        couple_kernel, "svvvv", [(quarter, F32), (quarter, F32), (quarter, F32)],
        pos, q_sib2, q_own1, q_oth1, b, flops=mac * n, name="mid_coupled",
    )
    (out,) = call(
        top_kernel, "svvvvv", [((4,) + part, BF)],
        pos, got, q_own3, q_oth3, w, b, flops=mac * n // 2, name="top",
    )
    got = exchange(out, "top", far)
    (out,) = call(
        down_kernel, "svvvvv", [((4,) + quarter, BF)],
        pos, got, c2, c1_own, c1_oth, w, flops=mac * n, name="down",
    )
    got = exchange(out, "top", near)
    (out,) = call(
        last_kernel, "ssvvvvvvv", [(rhs.shape, BF)],
        pos, order, got, c0, cleaf, direct, w, wl, row_basis,
        flops=mac * n * 7, name="last",
    )
    return out


def solution(mesh):
    return jax.shard_map(
        shards,
        mesh=mesh,
        in_specs=(
            P(None, ("leaf", "top"), None),
            P(None, ("leaf", "top"), None, None),
            P(None, ("leaf", "top"), None, None),
            P(None, ("leaf", "top"), None, None),
            P(None, ("leaf", "top"), None, None, None),
            P(None, ("leaf", "top"), None, None),
            P(None, ("leaf", "top"), None, None, None, None),
            P(None, ("leaf", "top"), None, None, None),
            P(("leaf", "top"), None),
        ),
        out_specs=P(None, ("leaf", "top"), None),
        check_vma=False,
    )
```

```python
import jax
import jax.numpy as jnp
from jax import lax
from jax.experimental import pallas as pl
from jax.experimental.pallas import tpu as pltpu
from jax.sharding import PartitionSpec as P

BF = jnp.bfloat16
F32 = jnp.float32
NN = (((1,), (0,)), ((), ()))
NT = (((1,), (1,)), ((), ()))


def dot(a, b, dims=NN):
    return lax.dot_general(a, b, dims, preferred_element_type=F32)


def widen(a):
    half = a.shape[0] // 2
    re, im = a[:half], a[half:]
    return jnp.concatenate(
        [jnp.concatenate([re, -im], axis=1), jnp.concatenate([im, re], axis=1)], axis=0
    )


def times(a, w_re, w_im):
    return dot(widen(a), jnp.concatenate([w_re, w_im], axis=0))


def times_t(a, w_re, w_im):
    return dot(widen(a), jnp.concatenate([w_re, w_im], axis=1), NT)


def rows(ref):
    return jnp.concatenate([ref[0], ref[1]], axis=0)


def put(ref, value):
    half = value.shape[0] // 2
    ref[0] = value[:half].astype(ref.dtype)
    ref[1] = value[half:].astype(ref.dtype)


def bit(pos, level):
    return (pos[0] >> level) & 1


def lift(q, w, pos, level, flip=0):
    child = bit(pos, level) ^ flip
    return times(q, w[0, level, child], w[1, level, child])


def lower(h, w, pos, level, flip=0):
    child = bit(pos, level) ^ flip
    return times_t(h, w[0, level, child], w[1, level, child])


def couple(q, b, pos, level, flip=0):
    return lax.cond(
        (bit(pos, level) ^ flip) == 0,
        lambda: times_t(q, b[0, level], b[1, level]),
        lambda: times(q, b[0, level], b[1, level]),
    )


def split(value, side, keep, send):
    half = value.shape[0] // 2
    part = half // 2
    for c in range(2):
        low = value[c * half : c * half + part]
        high = value[c * half + part : (c + 1) * half]
        keep[c] = jnp.where(side == 0, low, high)
        send[c] = jnp.where(side == 0, high, low)


def join(own, got, side):
    parts = []
    for c in range(2):
        parts.append(jnp.where(side == 0, own[c], got[c]))
        parts.append(jnp.where(side == 0, got[c], own[c]))
    return jnp.concatenate(parts, axis=0)


def leaf_kernel(pos, order, x, u, wl, w, qleaf, keep, send, own, order_s, x_v, u_v, wl_v, w_v, sems):
    size = u.shape[2]
    copies = [
        pltpu.make_async_copy(order, order_s, sems.at[0]),
        pltpu.make_async_copy(x.at[:, pl.ds(0, size)], x_v.at[:, pl.ds(0, size)], sems.at[1]),
        pltpu.make_async_copy(u, u_v, sems.at[2]),
        pltpu.make_async_copy(x.at[:, pl.ds(size, size)], x_v.at[:, pl.ds(size, size)], sems.at[3]),
        pltpu.make_async_copy(wl.at[:, 0], wl_v, sems.at[4]),
        pltpu.make_async_copy(w.at[:, 0], w_v.at[:, 0], sems.at[5]),
    ]
    for copy in copies:
        copy.start()
    copies[0].wait()
    first = order_s[0, 0]
    for block in range(2):
        copies[1 + 2 * block].wait()
        at = pl.ds(block * size, size)
        xt = jnp.concatenate([x_v[0, at].T, x_v[1, at].T], axis=0)
        if block == 0:
            copies[2].wait()
        leaf = first ^ block
        qleaf[leaf] = times(xt, u_v[0, leaf], u_v[1, leaf]).astype(BF)
    copies[4].wait()
    q = times(qleaf[0], wl_v[0, 0], wl_v[1, 0]) + times(qleaf[1], wl_v[0, 1], wl_v[1, 1])
    split(q.astype(BF), bit(pos, 0), keep, send)
    copies[5].wait()
    put(own, lift(rows(keep), w_v, pos, 0))


def climb_kernel(level):
    def kernel(pos, got, own, w, *outs):
        q = (rows(own) + lift(rows(got), w, pos, level, 1)).astype(BF)
        if len(outs) == 2:
            split(q, bit(pos, level + 1), *outs)
        else:
            put(outs[0], q)

    return kernel


def direct(order, block, x, d, out):
    size = d.shape[2]
    leaf = order[0, 0] ^ block
    at = pl.ds(block * size, size)
    xs = jnp.concatenate([x[0, at], x[1, at]], axis=0)
    re, im = d[0, leaf], d[1, leaf]
    out[0] = dot(jnp.concatenate([re, -im], axis=1), xs)
    out[1] = dot(jnp.concatenate([im, re], axis=1), xs)


def shadow_1(pos, order, keep, w, x, d, own, part):
    put(own, lift(rows(keep), w, pos, 1))
    direct(order, 0, x, d, part)


def shadow_2(pos, order, keep, w, x, d, own, part):
    put(own, lift(rows(keep), w, pos, 2))
    direct(order, 1, x, d, part)


def shadow_3(pos, q3, w, b, bl, qleaf, keep0, got0, keep1, got1, keep2, got2, own, cleaf, *coupled):
    put(own, lift(rows(q3), w, pos, 3))
    cleaf[0] = times_t(qleaf[1], bl[0, 0], bl[1, 0]).astype(BF)
    cleaf[1] = times(qleaf[0], bl[0, 0], bl[1, 0]).astype(BF)
    for level, (keep, got) in enumerate(((keep0, got0), (keep1, got1), (keep2, got2))):
        put(coupled[2 * level], couple(rows(got), b, pos, level))
        put(coupled[2 * level + 1], couple(rows(keep), b, pos, level, 1))


def shadow_4(pos, order, q4, got3, w, b, r, cleaf, part_0, part_1, own, top, base):
    put(own, lift(rows(q4), w, pos, 4))
    put(top, couple(rows(got3), b, pos, 3))
    n = part_0.shape[2]
    size = r.shape[2]
    first = order[0, 0]
    for block, part in enumerate((part_0, part_1)):
        leaf = first ^ block
        add = dot(jnp.concatenate([r[0, leaf], r[1, leaf]], axis=1), widen(cleaf[leaf]), NT)
        for c in range(2):
            for half in range(2):
                lanes = slice(half * n // 2, (half + 1) * n // 2)
                base[half, c, pl.ds(block * size, size)] = (
                    part[c, :, lanes] + add[:, c * n + lanes.start : c * n + lanes.stop]
                )


def product(r, wl, leaf, out):
    put(out, times(jnp.concatenate([r[0, leaf], r[1, leaf]], axis=0), wl[0, 0, leaf], wl[1, 0, leaf]))


def shadow_5(pos, q5, got4, w, b, r, wl, top, own, top_out, path, rw):
    put(own, lift(rows(q5), w, pos, 5))
    c4 = couple(rows(got4), b, pos, 4).astype(BF)
    put(top_out, rows(top) + lower(c4, w, pos, 3))
    w3 = bit(pos, 3)
    put(path, lift(jnp.concatenate([w[0, 3, w3], w[1, 3, w3]], axis=0), w, pos, 4))
    product(r, wl, 0, rw)


def shadow_6(pos, q6, got5, w, b, r, wl, top, path, own, top_out, path_out, rw):
    put(own, lift(rows(q6), w, pos, 6))
    c5 = couple(rows(got5), b, pos, 5).astype(BF)
    put(top_out, rows(top) + times_t(c5, path[0], path[1]))
    put(path_out, lift(rows(path), w, pos, 5))
    product(r, wl, 1, rw)


def shadow_7(pos, got6, w, b, top, path, top_out, path_out):
    c6 = couple(rows(got6), b, pos, 6).astype(BF)
    put(top_out, rows(top) + times_t(c6, path[0], path[1]))
    longer = lift(rows(path), w, pos, 6).astype(BF)
    put(path_out, couple_path(longer, b, pos))


def couple_path(path, b, pos):
    return lax.cond(
        bit(pos, 7) == 0,
        lambda: times(path, b[0, 7], b[1, 7]),
        lambda: times_t(path, b[0, 7], b[1, 7]),
    )


def top_kernel(pos, got, top, path, c_own, c_oth, w, own, send):
    h = (rows(top) + times_t(rows(got), path[0], path[1])).astype(BF)
    put(own, rows(c_own) + lower(h, w, pos, 2))
    put(send, rows(c_oth) + lower(h, w, pos, 2, 1))


def down_kernel(level):
    def kernel(pos, mine, got, c_own, c_oth, w, own, send):
        h = join(mine, got, bit(pos, level + 1))
        put(own, rows(c_own) + lower(h, w, pos, level))
        put(send, rows(c_oth) + lower(h, w, pos, level, 1))

    return kernel


def finish(order, h, base, half, rws, emit):
    hw = widen(rows(h))
    n = h.shape[1]
    first = order[0, 0]
    for leaf, rw in enumerate(rws):
        size = rw.shape[1]
        at = pl.ds(pl.multiple_of((first ^ leaf) * size, size), size)
        add = dot(jnp.concatenate([rw[0], rw[1]], axis=1), hw, NT)
        for c in range(2):
            emit(c, at, (base[half, c, at] + add[:, c * n : (c + 1) * n]).astype(BF))


def own_kernel(pos, order, h, base, rw0, rw1, out):
    def emit(c, at, value):
        out[c, at] = value

    finish(order, h, base, bit(pos, 0), (rw0, rw1), emit)


def last_kernel(pos, order, h, base, rw0, rw1, done, out):
    side = bit(pos, 0)
    n = h.shape[1]
    at_own = pl.ds(pl.multiple_of(side * n, n), n)
    at_oth = pl.ds(pl.multiple_of((1 - side) * n, n), n)
    out[:, :, at_own] = done[...]

    def emit(c, at, value):
        out[c, at, at_oth] = value

    finish(order, h, base, 1 - side, (rw0, rw1), emit)


VMEM = pl.BlockSpec(memory_space=pltpu.VMEM)
SMEM = pl.BlockSpec(memory_space=pltpu.SMEM)
HBM = pl.BlockSpec(memory_space=pltpu.HBM)
GRANT = 20 * 2**20


def call(name, kernel, ins, outs, *args, scratch=(), flops=0):
    specs = {"s": SMEM, "v": VMEM, "h": HBM}
    moved = sum(a.size * a.dtype.itemsize for a in args)
    return pl.pallas_call(
        kernel,
        out_shape=[jax.ShapeDtypeStruct(shape, dtype) for shape, dtype in outs],
        in_specs=[specs[kind] for kind in ins],
        out_specs=[VMEM] * len(outs),
        scratch_shapes=list(scratch),
        compiler_params=pltpu.CompilerParams(vmem_limit_bytes=GRANT),
        cost_estimate=pl.CostEstimate(flops=flops, bytes_accessed=moved, transcendentals=0),
        name=name,
    )(*args)


def shards(rhs, diag, row_basis, col_basis, wl, bl, cross_w, cross_b, order):
    n = rhs.shape[2]
    rank = col_basis.shape[3]
    size = col_basis.shape[2]
    top_size = lax.axis_size("top")
    pos = (lax.axis_index("leaf") * top_size + lax.axis_index("top")).astype(jnp.int32).reshape(1)
    w = cross_w[:, 0]
    b = cross_b[:, 0]

    def swap(value, level):
        flip = 2**level
        axis, mask = ("top", flip) if flip < top_size else ("leaf", flip // top_size)
        return lax.ppermute(value, axis, [(i, i ^ mask) for i in range(lax.axis_size(axis))])

    def block(columns, dtype=BF):
        return ((2, columns, rank), dtype)

    mac = 8 * rank * rank
    hbm = [pltpu.with_memory_space_constraint(a, pltpu.HBM) for a in (order, rhs, col_basis, wl, w)]
    half, quarter, eighth = n // 2, n // 4, n // 8
    qleaf, keep0, send, own = call(
        "leaf_skeletons", leaf_kernel, "shhhhh",
        [((2, 2 * n, rank), BF), block(half), block(half), block(half, F32)], pos, *hbm,
        scratch=(
            pltpu.SMEM(order.shape, jnp.int32),
            pltpu.VMEM(rhs.shape, BF),
            pltpu.VMEM(col_basis.shape, BF),
            pltpu.VMEM((2, 2, rank, rank), BF),
            pltpu.VMEM((2, 1, 2, rank, rank), BF),
            pltpu.SemaphoreType.DMA((6,)),
        ),
        flops=mac * n * 6,
    )
    got0 = swap(send, 0)
    keep1, send = call(
        "climb_0", climb_kernel(0), "svvv", [block(quarter), block(quarter)],
        pos, got0, own, w, flops=mac * half,
    )
    got1 = swap(send, 1)
    own, part_0 = call(
        "shadow_1", shadow_1, "ssvvvv", [block(quarter, F32), ((2, size, n), F32)],
        pos, order, keep1, w, rhs, diag, flops=mac * n * 5,
    )
    keep2, send = call(
        "climb_1", climb_kernel(1), "svvv", [block(eighth), block(eighth)],
        pos, got1, own, w, flops=mac * quarter,
    )
    got2 = swap(send, 2)
    own, part_1 = call(
        "shadow_2", shadow_2, "ssvvvv", [block(eighth, F32), ((2, size, n), F32)],
        pos, order, keep2, w, rhs, diag, flops=mac * n * 5,
    )
    (q3,) = call("climb_2", climb_kernel(2), "svvv", [block(eighth)], pos, got2, own, w, flops=mac * eighth)
    got3 = swap(q3, 3)
    own, cleaf, c0, c0_oth, c1, c1_oth, c2, c2_oth = call(
        "shadow_3", shadow_3, "s" + "v" * 11,
        [block(eighth, F32), ((2, 2 * n, rank), BF)]
        + [block(half, F32)] * 2 + [block(quarter, F32)] * 2 + [block(eighth, F32)] * 2,
        pos, q3, w, b, bl, qleaf, keep0, got0, keep1, got1, keep2, got2, flops=mac * n * 4,
    )
    (q4,) = call("climb_3", climb_kernel(3), "svvv", [block(eighth)], pos, got3, own, w, flops=mac * eighth)
    got4 = swap(q4, 4)
    own, top, base = call(
        "shadow_4", shadow_4, "ss" + "v" * 8,
        [block(eighth, F32), block(eighth, F32), ((2, 2, 2 * size, half), F32)],
        pos, order, q4, got3, w, b, row_basis, cleaf, part_0, part_1, flops=mac * n * 4,
    )
    (q5,) = call("climb_4", climb_kernel(4), "svvv", [block(eighth)], pos, got4, own, w, flops=mac * eighth)
    got5 = swap(q5, 5)
    own, top, path, rw0 = call(
        "shadow_5", shadow_5, "s" + "v" * 7,
        [block(eighth, F32), block(eighth, F32), block(rank), block(size)],
        pos, q5, got4, w, b, row_basis, wl, top, flops=mac * n * 3,
    )
    (q6,) = call("climb_5", climb_kernel(5), "svvv", [block(eighth)], pos, got5, own, w, flops=mac * eighth)
    got6 = swap(q6, 6)
    own, top, path, rw1 = call(
        "shadow_6", shadow_6, "s" + "v" * 8,
        [block(eighth, F32), block(eighth, F32), block(rank), block(size)],
        pos, q6, got5, w, b, row_basis, wl, top, path, flops=mac * n * 3,
    )
    (q7,) = call("climb_6", climb_kernel(6), "svvv", [block(eighth)], pos, got6, own, w, flops=mac * eighth)
    got7 = swap(q7, 7)
    top, path = call(
        "shadow_7", shadow_7, "s" + "v" * 5, [block(eighth, F32), block(rank)],
        pos, got6, w, b, top, path, flops=mac * n * 2,
    )
    mine, send = call(
        "top", top_kernel, "s" + "v" * 6, [block(eighth), block(eighth)],
        pos, got7, top, path, c2, c2_oth, w, flops=mac * eighth * 3,
    )
    got = swap(send, 2)
    mine, send = call(
        "down_1", down_kernel(1), "s" + "v" * 5, [block(quarter), block(quarter)],
        pos, mine, got, c1, c1_oth, w, flops=mac * quarter * 2,
    )
    got = swap(send, 1)
    mine, send = call(
        "down_0", down_kernel(0), "s" + "v" * 5, [block(half), block(half)],
        pos, mine, got, c0, c0_oth, w, flops=mac * half * 2,
    )
    got = swap(send, 0)
    (done,) = call(
        "own_columns", own_kernel, "ss" + "v" * 4, [((2, 2 * size, half), BF)],
        pos, order, mine, base, rw0, rw1, flops=mac * n * 2,
    )
    (out,) = call(
        "other_columns", last_kernel, "ss" + "v" * 5, [(rhs.shape, BF)],
        pos, order, got, base, rw0, rw1, done, flops=mac * n * 2,
    )
    return out


def solution(mesh):
    return jax.shard_map(
        shards,
        mesh=mesh,
        in_specs=(
            P(None, ("leaf", "top"), None),
            P(None, ("leaf", "top"), None, None),
            P(None, ("leaf", "top"), None, None),
            P(None, ("leaf", "top"), None, None),
            P(None, ("leaf", "top"), None, None, None),
            P(None, ("leaf", "top"), None, None),
            P(None, ("leaf", "top"), None, None, None, None),
            P(None, ("leaf", "top"), None, None, None),
            P(("leaf", "top"), None),
        ),
        out_specs=P(None, ("leaf", "top"), None),
        check_vma=False,
    )
```

```python
import jax
import jax.numpy as jnp
from jax import lax
from jax.experimental import pallas as pl
from jax.experimental.pallas import tpu as pltpu
from jax.sharding import PartitionSpec as P

BF = jnp.bfloat16
F32 = jnp.float32
NN = (((1,), (0,)), ((), ()))
NT = (((1,), (1,)), ((), ()))


def dot(a, b, dims=NN):
    return lax.dot_general(a, b, dims, preferred_element_type=F32)


def widen(a):
    half = a.shape[0] // 2
    re, im = a[:half], a[half:]
    return jnp.concatenate(
        [jnp.concatenate([re, -im], axis=1), jnp.concatenate([im, re], axis=1)], axis=0
    )


def times(a, w_re, w_im):
    return dot(widen(a), jnp.concatenate([w_re, w_im], axis=0))


def times_t(a, w_re, w_im):
    return dot(widen(a), jnp.concatenate([w_re, w_im], axis=1), NT)


def rows(ref):
    return jnp.concatenate([ref[0], ref[1]], axis=0)


def put(ref, value):
    half = value.shape[0] // 2
    ref[0] = value[:half].astype(ref.dtype)
    ref[1] = value[half:].astype(ref.dtype)


def bit(pos, level):
    return (pos[0] >> level) & 1


def lift(q, w, pos, level, flip=0):
    child = bit(pos, level) ^ flip
    return times(q, w[0, level, child], w[1, level, child])


def lower(h, w, pos, level, flip=0):
    child = bit(pos, level) ^ flip
    return times_t(h, w[0, level, child], w[1, level, child])


def couple(q, b, pos, level, flip=0):
    return lax.cond(
        (bit(pos, level) ^ flip) == 0,
        lambda: times_t(q, b[0, level], b[1, level]),
        lambda: times(q, b[0, level], b[1, level]),
    )


def split(value, side, keep, send):
    half = value.shape[0] // 2
    part = half // 2
    for c in range(2):
        low = value[c * half : c * half + part]
        high = value[c * half + part : (c + 1) * half]
        keep[c] = jnp.where(side == 0, low, high)
        send[c] = jnp.where(side == 0, high, low)


def join(own, got, side):
    parts = []
    for c in range(2):
        parts.append(jnp.where(side == 0, own[c], got[c]))
        parts.append(jnp.where(side == 0, got[c], own[c]))
    return jnp.concatenate(parts, axis=0)


def leaf_kernel(pos, order, x, u, wl, w, qleaf, q0, w0, order_s, x_v, u_v, wl_v, sems):
    size = u.shape[2]
    copies = [
        pltpu.make_async_copy(order, order_s, sems.at[0]),
        pltpu.make_async_copy(x.at[:, pl.ds(0, size)], x_v.at[:, pl.ds(0, size)], sems.at[1]),
        pltpu.make_async_copy(u, u_v, sems.at[2]),
        pltpu.make_async_copy(x.at[:, pl.ds(size, size)], x_v.at[:, pl.ds(size, size)], sems.at[3]),
        pltpu.make_async_copy(wl.at[:, 0], wl_v, sems.at[4]),
        pltpu.make_async_copy(w.at[:, 0], w0.at[:, 0], sems.at[5]),
    ]
    for copy in copies:
        copy.start()
    copies[0].wait()
    first = order_s[0, 0]
    for block in range(2):
        copies[1 + 2 * block].wait()
        at = pl.ds(block * size, size)
        xt = jnp.concatenate([x_v[0, at].T, x_v[1, at].T], axis=0)
        if block == 0:
            copies[2].wait()
        leaf = first ^ block
        qleaf[leaf] = times(xt, u_v[0, leaf], u_v[1, leaf]).astype(BF)
    copies[4].wait()
    put(q0, times(qleaf[0], wl_v[0, 0], wl_v[1, 0]) + times(qleaf[1], wl_v[0, 1], wl_v[1, 1]))
    copies[5].wait()


def side(pos, level):
    return bit(pos, level) ^ bit(pos, level + 1) if level == 2 else bit(pos, level)


def climb_kernel(level):
    def kernel(pos, got, own, w, *outs):
        q = (rows(own) + lift(rows(got), w, pos, level, 1)).astype(BF)
        if len(outs) == 2:
            split(q, side(pos, level + 1), *outs)
        else:
            put(outs[0], q)

    return kernel


def direct(order, block, x, d, out):
    size = d.shape[2]
    leaf = order[0, 0] ^ block
    at = pl.ds(block * size, size)
    xs = jnp.concatenate([x[0, at], x[1, at]], axis=0)
    re, im = d[0, leaf], d[1, leaf]
    out[0] = dot(jnp.concatenate([re, -im], axis=1), xs)
    out[1] = dot(jnp.concatenate([im, re], axis=1), xs)


def shadow_0(pos, q0, w, own):
    put(own, lift(rows(q0), w, pos, 0))


def shadow_1(pos, order, keep, w, x, d, own, part):
    put(own, lift(rows(keep), w, pos, 1))
    direct(order, 0, x, d, part)


def shadow_2(pos, order, keep, w, x, d, own, part):
    put(own, lift(rows(keep), w, pos, 2))
    direct(order, 1, x, d, part)


def shadow_3(pos, q3, w, w0, b, bl, wl, qleaf, got0, keep2, got2, own, cleaf, c2, c2_oth):
    put(own, lift(rows(q3), w, pos, 3))
    c0 = couple(rows(got0), b, pos, 0).astype(BF)
    left = times_t(qleaf[1], bl[0, 0], bl[1, 0])
    right = times(qleaf[0], bl[0, 0], bl[1, 0])
    cleaf[0] = (left + times_t(c0, wl[0, 0, 0], wl[1, 0, 0])).astype(BF)
    cleaf[1] = (right + times_t(c0, wl[0, 0, 1], wl[1, 0, 1])).astype(BF)
    put(c2, couple(rows(got2), b, pos, 2))
    put(c2_oth, couple(rows(keep2), b, pos, 2, 1))


def shadow_4(pos, order, q4, got3, w, b, r, cleaf, part_0, part_1, own, top, base):
    put(own, lift(rows(q4), w, pos, 4))
    put(top, couple(rows(got3), b, pos, 3))
    n = part_0.shape[2]
    size = r.shape[2]
    first = order[0, 0]
    for block, part in enumerate((part_0, part_1)):
        leaf = first ^ block
        add = dot(jnp.concatenate([r[0, leaf], r[1, leaf]], axis=1), widen(cleaf[leaf]), NT)
        for c in range(2):
            for half in range(2):
                lanes = slice(half * n // 2, (half + 1) * n // 2)
                base[half, c, pl.ds(block * size, size)] = (
                    part[c, :, lanes] + add[:, c * n + lanes.start : c * n + lanes.stop]
                )


def product(r, wl, leaf, out):
    put(out, times(jnp.concatenate([r[0, leaf], r[1, leaf]], axis=0), wl[0, 0, leaf], wl[1, 0, leaf]))


def shadow_5(pos, q5, got4, w, b, r, wl, top, own, top_out, path, rw):
    put(own, lift(rows(q5), w, pos, 5))
    c4 = couple(rows(got4), b, pos, 4).astype(BF)
    put(top_out, rows(top) + lower(c4, w, pos, 3))
    w3 = bit(pos, 3)
    put(path, lift(jnp.concatenate([w[0, 3, w3], w[1, 3, w3]], axis=0), w, pos, 4))
    product(r, wl, 0, rw)


def shadow_6(pos, q6, got5, w, b, r, wl, top, path, own, top_out, path_out, rw):
    put(own, lift(rows(q6), w, pos, 6))
    c5 = couple(rows(got5), b, pos, 5).astype(BF)
    put(top_out, rows(top) + times_t(c5, path[0], path[1]))
    put(path_out, lift(rows(path), w, pos, 5))
    product(r, wl, 1, rw)


def shadow_7(pos, got6, w, b, top, path, top_out, path_out):
    c6 = couple(rows(got6), b, pos, 6).astype(BF)
    put(top_out, rows(top) + times_t(c6, path[0], path[1]))
    longer = lift(rows(path), w, pos, 6).astype(BF)
    put(path_out, couple_path(longer, b, pos))


def couple_path(path, b, pos):
    return lax.cond(
        bit(pos, 7) == 0,
        lambda: times(path, b[0, 7], b[1, 7]),
        lambda: times_t(path, b[0, 7], b[1, 7]),
    )


def top_kernel(pos, got, top, path, c_own, c_oth, w, own, send):
    h = (rows(top) + times_t(rows(got), path[0], path[1])).astype(BF)
    put(own, rows(c_own) + lower(h, w, pos, 2))
    put(send, rows(c_oth) + lower(h, w, pos, 2, 1))


def shadow_8(pos, mine, keep1, got1, b, w0, rw0, rw1, c1, c1_oth, g0, g1):
    put(c1, couple(rows(got1), b, pos, 1))
    put(c1_oth, couple(rows(keep1), b, pos, 1, 1))
    put(g0, lift(rows(rw0), w0, pos, 0))
    put(g1, lift(rows(rw1), w0, pos, 0))


def down_kernel(pos, mine, got, c_own, c_oth, w, own, send):
    h = join(mine, got, side(pos, 2))
    put(own, rows(c_own) + lower(h, w, pos, 1))
    put(send, rows(c_oth) + lower(h, w, pos, 1, 1))


def finish(pos, order, h_hub, h_other, base, gs, half, out, buf, sems):
    h = jnp.where(bit(pos, 0) == 1, rows(h_hub), rows(h_other))
    hw = widen(h)
    n = h_hub.shape[1]
    lanes = pl.ds(pl.multiple_of(half * n, n), n)
    copies = []
    for leaf, g in enumerate(gs):
        size = g.shape[1]
        at = pl.ds(pl.multiple_of((order[0, 0] ^ leaf) * size, size), size)
        add = dot(jnp.concatenate([g[0], g[1]], axis=1), hw, NT)
        for c in range(2):
            buf[leaf, c] = (base[half, c, at] + add[:, c * n : (c + 1) * n]).astype(BF)
            copies.append(
                pltpu.make_async_copy(buf.at[leaf, c], out.at[c, at, lanes], sems.at[leaf, c])
            )
            copies[-1].start()
    for copy in copies:
        copy.wait()


def own_kernel(pos, order, h_hub, h_other, base, g0, g1, out, buf, sems):
    finish(pos, order, h_hub, h_other, base, (g0, g1), bit(pos, 1), out, buf, sems)


def last_kernel(pos, order, h_hub, h_other, base, g0, g1, done, out, buf, sems):
    finish(pos, order, h_hub, h_other, base, (g0, g1), 1 - bit(pos, 1), out, buf, sems)


VMEM = pl.BlockSpec(memory_space=pltpu.VMEM)
SMEM = pl.BlockSpec(memory_space=pltpu.SMEM)
HBM = pl.BlockSpec(memory_space=pltpu.HBM)
GRANT = 20 * 2**20


def call(name, kernel, ins, outs, *args, scratch=(), flops=0, aliases=None, out_spec=VMEM):
    specs = {"s": SMEM, "v": VMEM, "h": HBM}
    moved = sum(a.size * a.dtype.itemsize for a in args)
    return pl.pallas_call(
        kernel,
        out_shape=[jax.ShapeDtypeStruct(shape, dtype) for shape, dtype in outs],
        in_specs=[specs[kind] for kind in ins],
        out_specs=[out_spec] * len(outs),
        scratch_shapes=list(scratch),
        input_output_aliases=aliases or {},
        compiler_params=pltpu.CompilerParams(vmem_limit_bytes=GRANT),
        cost_estimate=pl.CostEstimate(flops=flops, bytes_accessed=moved, transcendentals=0),
        name=name,
    )(*args)


def shards(rhs, diag, row_basis, col_basis, wl, bl, cross_w, cross_b, order):
    n = rhs.shape[2]
    rank = col_basis.shape[3]
    size = col_basis.shape[2]
    axes = ("leaf", "top")
    devices = lax.axis_size("leaf") * lax.axis_size("top")
    pos = lax.axis_index(axes).astype(jnp.int32).reshape(1)
    w = cross_w[:, 0]
    b = cross_b[:, 0]

    def hubs(value, flip):
        return lax.ppermute(value, axes, [(i, i ^ flip) for i in range(devices) if i & 1])

    def block(columns, dtype=BF):
        return ((2, columns, rank), dtype)

    mac = 8 * rank * rank
    hbm = [pltpu.with_memory_space_constraint(a, pltpu.HBM) for a in (order, rhs, col_basis, wl, w)]
    half, quarter = n // 2, n // 4
    qleaf, q0, w0 = call(
        "leaf_skeletons", leaf_kernel, "shhhhh",
        [((2, 2 * n, rank), BF), block(n), ((2, 1, 2, rank, rank), BF)], pos, *hbm,
        scratch=(
            pltpu.SMEM(order.shape, jnp.int32),
            pltpu.VMEM(rhs.shape, BF),
            pltpu.VMEM(col_basis.shape, BF),
            pltpu.VMEM((2, 2, rank, rank), BF),
            pltpu.SemaphoreType.DMA((6,)),
        ),
        flops=mac * n * 6,
    )
    got0 = lax.ppermute(q0, axes, [(i, i ^ 1) for i in range(devices)])
    (own,) = call("shadow_0", shadow_0, "svv", [block(n, F32)], pos, q0, w0, flops=mac * n)
    keep1, send = call(
        "climb_0", climb_kernel(0), "svvv", [block(half), block(half)],
        pos, got0, own, w0, flops=mac * n,
    )
    got1 = hubs(send, 2)
    own, part_0 = call(
        "shadow_1", shadow_1, "ssvvvv", [block(half, F32), ((2, size, n), F32)],
        pos, order, keep1, w, rhs, diag, flops=mac * n * 5,
    )
    keep2, send = call(
        "climb_1", climb_kernel(1), "svvv", [block(quarter), block(quarter)],
        pos, got1, own, w, flops=mac * half,
    )
    got2 = hubs(send, 4)
    own, part_1 = call(
        "shadow_2", shadow_2, "ssvvvv", [block(quarter, F32), ((2, size, n), F32)],
        pos, order, keep2, w, rhs, diag, flops=mac * n * 5,
    )
    (q3,) = call("climb_2", climb_kernel(2), "svvv", [block(quarter)], pos, got2, own, w, flops=mac * quarter)
    got3 = hubs(q3, 12)
    own, cleaf, c2, c2_oth = call(
        "shadow_3", shadow_3, "s" + "v" * 10,
        [block(quarter, F32), ((2, 2 * n, rank), BF), block(quarter, F32), block(quarter, F32)],
        pos, q3, w, w0, b, bl, wl, qleaf, got0, keep2, got2, flops=mac * n * 6,
    )
    (q4,) = call("climb_3", climb_kernel(3), "svvv", [block(quarter)], pos, got3, own, w, flops=mac * quarter)
    got4 = hubs(q4, 16)
    own, top, base = call(
        "shadow_4", shadow_4, "ss" + "v" * 8,
        [block(quarter, F32), block(quarter, F32), ((2, 2, 2 * size, half), F32)],
        pos, order, q4, got3, w, b, row_basis, cleaf, part_0, part_1, flops=mac * n * 4,
    )
    (q5,) = call("climb_4", climb_kernel(4), "svvv", [block(quarter)], pos, got4, own, w, flops=mac * quarter)
    got5 = hubs(q5, 48)
    own, top, path, rw0 = call(
        "shadow_5", shadow_5, "s" + "v" * 7,
        [block(quarter, F32), block(quarter, F32), block(rank), block(size)],
        pos, q5, got4, w, b, row_basis, wl, top, flops=mac * n * 3,
    )
    (q6,) = call("climb_5", climb_kernel(5), "svvv", [block(quarter)], pos, got5, own, w, flops=mac * quarter)
    got6 = hubs(q6, 64)
    own, top, path, rw1 = call(
        "shadow_6", shadow_6, "s" + "v" * 8,
        [block(quarter, F32), block(quarter, F32), block(rank), block(size)],
        pos, q6, got5, w, b, row_basis, wl, top, path, flops=mac * n * 3,
    )
    (q7,) = call("climb_6", climb_kernel(6), "svvv", [block(quarter)], pos, got6, own, w, flops=mac * quarter)
    got7 = hubs(q7, 192)
    top, path = call(
        "shadow_7", shadow_7, "s" + "v" * 5, [block(quarter, F32), block(rank)],
        pos, got6, w, b, top, path, flops=mac * n * 2,
    )
    mine, send = call(
        "top", top_kernel, "s" + "v" * 6, [block(quarter), block(quarter)],
        pos, got7, top, path, c2, c2_oth, w, flops=mac * quarter * 3,
    )
    got = hubs(send, 4)
    c1, c1_oth, g0, g1 = call(
        "shadow_8", shadow_8, "s" + "v" * 7,
        [block(half, F32), block(half, F32), block(size), block(size)],
        pos, mine, keep1, got1, b, w0, rw0, rw1, flops=mac * n * 5,
    )
    mine, send = call(
        "down", down_kernel, "s" + "v" * 5, [block(half), block(half)],
        pos, mine, got, c1, c1_oth, w, flops=mac * half * 2,
    )
    got = hubs(send, 2)

    def inward(value):
        return lax.ppermute(value, axes, [(i, i ^ 1) for i in range(devices) if i & 1])

    def output(name, kernel, h, *args, aliases=None):
        return call(
            name, kernel, "ss" + "v" * 5 + "h" * (len(args)), [(rhs.shape, BF)],
            pos, order, h, inward(h), base, g0, g1, *args,
            scratch=(
                pltpu.VMEM((2, 2, size, half), BF),
                pltpu.SemaphoreType.DMA((2, 2)),
            ),
            flops=mac * n * 2, aliases=aliases, out_spec=HBM,
        )[0]

    done = output("own_columns", own_kernel, mine)
    return output("other_columns", last_kernel, got, done, aliases={7: 0})


def solution(mesh):
    return jax.shard_map(
        shards,
        mesh=mesh,
        in_specs=(
            P(None, ("leaf", "top"), None),
            P(None, ("leaf", "top"), None, None),
            P(None, ("leaf", "top"), None, None),
            P(None, ("leaf", "top"), None, None),
            P(None, ("leaf", "top"), None, None, None),
            P(None, ("leaf", "top"), None, None),
            P(None, ("leaf", "top"), None, None, None, None),
            P(None, ("leaf", "top"), None, None, None),
            P(("leaf", "top"), None),
        ),
        out_specs=P(None, ("leaf", "top"), None),
        check_vma=False,
    )
```

```python
import jax
import jax.numpy as jnp
from jax import lax
from jax.experimental import pallas as pl
from jax.experimental.pallas import tpu as pltpu
from jax.sharding import PartitionSpec as P

BF = jnp.bfloat16
F32 = jnp.float32
NN = (((1,), (0,)), ((), ()))
NT = (((1,), (1,)), ((), ()))


def dot(a, b, dims=NN):
    return lax.dot_general(a, b, dims, preferred_element_type=F32)


def widen(a):
    half = a.shape[0] // 2
    re, im = a[:half], a[half:]
    return jnp.concatenate(
        [jnp.concatenate([re, -im], axis=1), jnp.concatenate([im, re], axis=1)], axis=0
    )


def times(a, w_re, w_im):
    return dot(widen(a), jnp.concatenate([w_re, w_im], axis=0))


def times_t(a, w_re, w_im):
    return dot(widen(a), jnp.concatenate([w_re, w_im], axis=1), NT)


def rows(ref):
    return jnp.concatenate([ref[0], ref[1]], axis=0)


def put(ref, value):
    half = value.shape[0] // 2
    ref[0] = value[:half].astype(ref.dtype)
    ref[1] = value[half:].astype(ref.dtype)


def bit(pos, level):
    return (pos[0] >> level) & 1


def lift(q, w, pos, level, flip=0):
    child = bit(pos, level) ^ flip
    return times(q, w[0, level, child], w[1, level, child])


def lower(h, w, pos, level, flip=0):
    child = bit(pos, level) ^ flip
    return times_t(h, w[0, level, child], w[1, level, child])


def couple(q, b, pos, level, flip=0):
    return lax.cond(
        (bit(pos, level) ^ flip) == 0,
        lambda: times_t(q, b[0, level], b[1, level]),
        lambda: times(q, b[0, level], b[1, level]),
    )


def split(value, side, keep, send):
    half = value.shape[0] // 2
    part = half // 2
    for c in range(2):
        low = value[c * half : c * half + part]
        high = value[c * half + part : (c + 1) * half]
        keep[c] = jnp.where(side == 0, low, high)
        send[c] = jnp.where(side == 0, high, low)


def join(own, got, side):
    parts = []
    for c in range(2):
        parts.append(jnp.where(side == 0, own[c], got[c]))
        parts.append(jnp.where(side == 0, got[c], own[c]))
    return jnp.concatenate(parts, axis=0)


def leaf_kernel(pos, order, x, u, wl, w, qleaf, q0, w0, order_s, x_v, u_v, wl_v, sems):
    size = u.shape[2]
    copies = [
        pltpu.make_async_copy(order, order_s, sems.at[0]),
        pltpu.make_async_copy(x.at[:, pl.ds(0, size)], x_v.at[:, pl.ds(0, size)], sems.at[1]),
        pltpu.make_async_copy(u, u_v, sems.at[2]),
        pltpu.make_async_copy(x.at[:, pl.ds(size, size)], x_v.at[:, pl.ds(size, size)], sems.at[3]),
        pltpu.make_async_copy(wl.at[:, 0], wl_v, sems.at[4]),
        pltpu.make_async_copy(w.at[:, 0], w0.at[:, 0], sems.at[5]),
    ]
    for copy in copies:
        copy.start()
    copies[0].wait()
    first = order_s[0, 0]
    for block in range(2):
        copies[1 + 2 * block].wait()
        at = pl.ds(block * size, size)
        xt = jnp.concatenate([x_v[0, at].T, x_v[1, at].T], axis=0)
        if block == 0:
            copies[2].wait()
        leaf = first ^ block
        qleaf[leaf] = times(xt, u_v[0, leaf], u_v[1, leaf]).astype(BF)
    copies[4].wait()
    put(q0, times(qleaf[0], wl_v[0, 0], wl_v[1, 0]) + times(qleaf[1], wl_v[0, 1], wl_v[1, 1]))
    copies[5].wait()


def side(pos, level):
    return bit(pos, level) ^ bit(pos, level + 1) if level == 2 else bit(pos, level)


def climb_kernel(level):
    def kernel(pos, got, own, w, *outs):
        q = (rows(own) + lift(rows(got), w, pos, level, 1)).astype(BF)
        if len(outs) == 2:
            split(q, side(pos, level + 1), *outs)
        else:
            put(outs[0], q)

    return kernel


def direct(order, block, x, d, out):
    size = d.shape[2]
    leaf = order[0, 0] ^ block
    at = pl.ds(block * size, size)
    xs = jnp.concatenate([x[0, at], x[1, at]], axis=0)
    re, im = d[0, leaf], d[1, leaf]
    out[0] = dot(jnp.concatenate([re, -im], axis=1), xs)
    out[1] = dot(jnp.concatenate([im, re], axis=1), xs)


def shadow_0(pos, q0, w, own):
    put(own, lift(rows(q0), w, pos, 0))


def shadow_1(pos, order, keep, w, x, d, own, part):
    put(own, lift(rows(keep), w, pos, 1))
    direct(order, 0, x, d, part)


def shadow_2(pos, order, keep, w, x, d, own, part):
    put(own, lift(rows(keep), w, pos, 2))
    direct(order, 1, x, d, part)


def shadow_3(pos, q3, w, w0, b, bl, wl, qleaf, got0, keep2, got2, own, cleaf, c2, c2_oth):
    put(own, lift(rows(q3), w, pos, 3))
    c0 = couple(rows(got0), b, pos, 0).astype(BF)
    left = times_t(qleaf[1], bl[0, 0], bl[1, 0])
    right = times(qleaf[0], bl[0, 0], bl[1, 0])
    cleaf[0] = (left + times_t(c0, wl[0, 0, 0], wl[1, 0, 0])).astype(BF)
    cleaf[1] = (right + times_t(c0, wl[0, 0, 1], wl[1, 0, 1])).astype(BF)
    put(c2, couple(rows(got2), b, pos, 2))
    put(c2_oth, couple(rows(keep2), b, pos, 2, 1))


def shadow_4(pos, order, q4, got3, w, b, r, cleaf, part_0, part_1, own, top, base):
    put(own, lift(rows(q4), w, pos, 4))
    put(top, couple(rows(got3), b, pos, 3))
    n = part_0.shape[2]
    size = r.shape[2]
    first = order[0, 0]
    for block, part in enumerate((part_0, part_1)):
        leaf = first ^ block
        add = dot(jnp.concatenate([r[0, leaf], r[1, leaf]], axis=1), widen(cleaf[leaf]), NT)
        for c in range(2):
            for half in range(2):
                lanes = slice(half * n // 2, (half + 1) * n // 2)
                base[half, c, pl.ds(block * size, size)] = (
                    part[c, :, lanes] + add[:, c * n + lanes.start : c * n + lanes.stop]
                )


def product(r, wl, leaf, out):
    put(out, times(jnp.concatenate([r[0, leaf], r[1, leaf]], axis=0), wl[0, 0, leaf], wl[1, 0, leaf]))


def shadow_5(pos, q5, got4, w, b, r, wl, top, own, top_out, path, rw):
    put(own, lift(rows(q5), w, pos, 5))
    c4 = couple(rows(got4), b, pos, 4).astype(BF)
    put(top_out, rows(top) + lower(c4, w, pos, 3))
    w3 = bit(pos, 3)
    put(path, lift(jnp.concatenate([w[0, 3, w3], w[1, 3, w3]], axis=0), w, pos, 4))
    product(r, wl, 0, rw)


def shadow_6(pos, q6, got5, w, b, r, wl, top, path, own, top_out, path_out, rw):
    put(own, lift(rows(q6), w, pos, 6))
    c5 = couple(rows(got5), b, pos, 5).astype(BF)
    put(top_out, rows(top) + times_t(c5, path[0], path[1]))
    put(path_out, lift(rows(path), w, pos, 5))
    product(r, wl, 1, rw)


def shadow_7(pos, got6, w, b, top, path, top_out, path_out):
    c6 = couple(rows(got6), b, pos, 6).astype(BF)
    put(top_out, rows(top) + times_t(c6, path[0], path[1]))
    longer = lift(rows(path), w, pos, 6).astype(BF)
    put(path_out, couple_path(longer, b, pos))


def couple_path(path, b, pos):
    return lax.cond(
        bit(pos, 7) == 0,
        lambda: times(path, b[0, 7], b[1, 7]),
        lambda: times_t(path, b[0, 7], b[1, 7]),
    )


def top_kernel(pos, got, top, path, c_own, c_oth, w, own, send):
    h = (rows(top) + times_t(rows(got), path[0], path[1])).astype(BF)
    put(own, rows(c_own) + lower(h, w, pos, 2))
    put(send, rows(c_oth) + lower(h, w, pos, 2, 1))


def shadow_8(pos, mine, keep1, got1, b, w0, rw0, rw1, c1, c1_oth, g0, g1):
    put(c1, couple(rows(got1), b, pos, 1))
    put(c1_oth, couple(rows(keep1), b, pos, 1, 1))
    put(g0, lift(rows(rw0), w0, pos, 0))
    put(g1, lift(rows(rw1), w0, pos, 0))


def down_kernel(pos, mine, got, c_own, c_oth, w, own, send):
    h = join(mine, got, side(pos, 2))
    put(own, rows(c_own) + lower(h, w, pos, 1))
    put(send, rows(c_oth) + lower(h, w, pos, 1, 1))


def finish(pos, order, h_hub, h_other, base, gs, half, out, buf, sems):
    h = jnp.where(bit(pos, 0) == 1, rows(h_hub), rows(h_other))
    hw = widen(h)
    n = h_hub.shape[1]
    lanes = pl.ds(pl.multiple_of(half * n, n), n)
    copies = []
    for leaf, g in enumerate(gs):
        size = g.shape[1]
        at = pl.ds(pl.multiple_of((order[0, 0] ^ leaf) * size, size), size)
        add = dot(jnp.concatenate([g[0], g[1]], axis=1), hw, NT)
        for c in range(2):
            buf[leaf, c] = (base[half, c, at] + add[:, c * n : (c + 1) * n]).astype(BF)
            copies.append(
                pltpu.make_async_copy(buf.at[leaf, c], out.at[c, at, lanes], sems.at[leaf, c])
            )
            copies[-1].start()
    for copy in copies:
        copy.wait()


def own_kernel(pos, order, h_hub, h_other, base, g0, g1, out, buf, sems):
    finish(pos, order, h_hub, h_other, base, (g0, g1), bit(pos, 1), out, buf, sems)


def last_kernel(pos, order, h_hub, h_other, base, g0, g1, done, out, buf, sems):
    finish(pos, order, h_hub, h_other, base, (g0, g1), 1 - bit(pos, 1), out, buf, sems)


VMEM = pl.BlockSpec(memory_space=pltpu.VMEM)
SMEM = pl.BlockSpec(memory_space=pltpu.SMEM)
HBM = pl.BlockSpec(memory_space=pltpu.HBM)
GRANT = 20 * 2**20


def call(name, kernel, ins, outs, *args, scratch=(), flops=0, aliases=None, out_spec=VMEM):
    specs = {"s": SMEM, "v": VMEM, "h": HBM}
    moved = sum(a.size * a.dtype.itemsize for a in args)
    return pl.pallas_call(
        kernel,
        out_shape=[jax.ShapeDtypeStruct(shape, dtype) for shape, dtype in outs],
        in_specs=[specs[kind] for kind in ins],
        out_specs=[out_spec] * len(outs),
        scratch_shapes=list(scratch),
        input_output_aliases=aliases or {},
        compiler_params=pltpu.CompilerParams(vmem_limit_bytes=GRANT),
        cost_estimate=pl.CostEstimate(flops=flops, bytes_accessed=moved, transcendentals=0),
        name=name,
    )(*args)


def shards(rhs, diag, row_basis, col_basis, wl, bl, cross_w, cross_b, order):
    n = rhs.shape[2]
    rank = col_basis.shape[3]
    size = col_basis.shape[2]
    axes = ("leaf", "top")
    devices = lax.axis_size("leaf") * lax.axis_size("top")
    pos = lax.axis_index(axes).astype(jnp.int32).reshape(1)
    w = cross_w[:, 0]
    b = cross_b[:, 0]

    def hubs(value, flip):
        return lax.ppermute(value, axes, [(i, i ^ flip if i & 1 else i) for i in range(devices)])

    def swap(value):
        return lax.ppermute(value, axes, [(i, i ^ 1) for i in range(devices)])

    def block(columns, dtype=BF):
        return ((2, columns, rank), dtype)

    mac = 8 * rank * rank
    hbm = [pltpu.with_memory_space_constraint(a, pltpu.HBM) for a in (order, rhs, col_basis, wl, w)]
    half, quarter = n // 2, n // 4
    qleaf, q0, w0 = call(
        "leaf_skeletons", leaf_kernel, "shhhhh",
        [((2, 2 * n, rank), BF), block(n), ((2, 1, 2, rank, rank), BF)], pos, *hbm,
        scratch=(
            pltpu.SMEM(order.shape, jnp.int32),
            pltpu.VMEM(rhs.shape, BF),
            pltpu.VMEM(col_basis.shape, BF),
            pltpu.VMEM((2, 2, rank, rank), BF),
            pltpu.SemaphoreType.DMA((6,)),
        ),
        flops=mac * n * 6,
    )
    got0 = swap(q0)
    (own,) = call("shadow_0", shadow_0, "svv", [block(n, F32)], pos, q0, w0, flops=mac * n)
    keep1, send = call(
        "climb_0", climb_kernel(0), "svvv", [block(half), block(half)],
        pos, got0, own, w0, flops=mac * n,
    )
    got1 = hubs(send, 2)
    own, part_0 = call(
        "shadow_1", shadow_1, "ssvvvv", [block(half, F32), ((2, size, n), F32)],
        pos, order, keep1, w, rhs, diag, flops=mac * n * 5,
    )
    keep2, send = call(
        "climb_1", climb_kernel(1), "svvv", [block(quarter), block(quarter)],
        pos, got1, own, w, flops=mac * half,
    )
    got2 = hubs(send, 4)
    own, part_1 = call(
        "shadow_2", shadow_2, "ssvvvv", [block(quarter, F32), ((2, size, n), F32)],
        pos, order, keep2, w, rhs, diag, flops=mac * n * 5,
    )
    (q3,) = call("climb_2", climb_kernel(2), "svvv", [block(quarter)], pos, got2, own, w, flops=mac * quarter)
    got3 = hubs(q3, 12)
    own, cleaf, c2, c2_oth = call(
        "shadow_3", shadow_3, "s" + "v" * 10,
        [block(quarter, F32), ((2, 2 * n, rank), BF), block(quarter, F32), block(quarter, F32)],
        pos, q3, w, w0, b, bl, wl, qleaf, got0, keep2, got2, flops=mac * n * 6,
    )
    (q4,) = call("climb_3", climb_kernel(3), "svvv", [block(quarter)], pos, got3, own, w, flops=mac * quarter)
    got4 = hubs(q4, 16)
    own, top, base = call(
        "shadow_4", shadow_4, "ss" + "v" * 8,
        [block(quarter, F32), block(quarter, F32), ((2, 2, 2 * size, half), F32)],
        pos, order, q4, got3, w, b, row_basis, cleaf, part_0, part_1, flops=mac * n * 4,
    )
    (q5,) = call("climb_4", climb_kernel(4), "svvv", [block(quarter)], pos, got4, own, w, flops=mac * quarter)
    got5 = hubs(q5, 48)
    own, top, path, rw0 = call(
        "shadow_5", shadow_5, "s" + "v" * 7,
        [block(quarter, F32), block(quarter, F32), block(rank), block(size)],
        pos, q5, got4, w, b, row_basis, wl, top, flops=mac * n * 3,
    )
    (q6,) = call("climb_5", climb_kernel(5), "svvv", [block(quarter)], pos, got5, own, w, flops=mac * quarter)
    got6 = hubs(q6, 64)
    own, top, path, rw1 = call(
        "shadow_6", shadow_6, "s" + "v" * 8,
        [block(quarter, F32), block(quarter, F32), block(rank), block(size)],
        pos, q6, got5, w, b, row_basis, wl, top, path, flops=mac * n * 3,
    )
    (q7,) = call("climb_6", climb_kernel(6), "svvv", [block(quarter)], pos, got6, own, w, flops=mac * quarter)
    got7 = hubs(q7, 192)
    top, path = call(
        "shadow_7", shadow_7, "s" + "v" * 5, [block(quarter, F32), block(rank)],
        pos, got6, w, b, top, path, flops=mac * n * 2,
    )
    mine, send = call(
        "top", top_kernel, "s" + "v" * 6, [block(quarter), block(quarter)],
        pos, got7, top, path, c2, c2_oth, w, flops=mac * quarter * 3,
    )
    got = hubs(send, 4)
    c1, c1_oth, g0, g1 = call(
        "shadow_8", shadow_8, "s" + "v" * 7,
        [block(half, F32), block(half, F32), block(size), block(size)],
        pos, mine, keep1, got1, b, w0, rw0, rw1, flops=mac * n * 5,
    )
    mine, send = call(
        "down", down_kernel, "s" + "v" * 5, [block(half), block(half)],
        pos, mine, got, c1, c1_oth, w, flops=mac * half * 2,
    )
    got = hubs(send, 2)

    def output(name, kernel, h, *args, aliases=None):
        return call(
            name, kernel, "ss" + "v" * 5 + "h" * (len(args)), [(rhs.shape, BF)],
            pos, order, h, swap(h), base, g0, g1, *args,
            scratch=(
                pltpu.VMEM((2, 2, size, half), BF),
                pltpu.SemaphoreType.DMA((2, 2)),
            ),
            flops=mac * n * 2, aliases=aliases, out_spec=HBM,
        )[0]

    done = output("own_columns", own_kernel, mine)
    got, done = lax.optimization_barrier((got, done))
    return output("other_columns", last_kernel, got, done, aliases={7: 0})


def solution(mesh):
    return jax.shard_map(
        shards,
        mesh=mesh,
        in_specs=(
            P(None, ("leaf", "top"), None),
            P(None, ("leaf", "top"), None, None),
            P(None, ("leaf", "top"), None, None),
            P(None, ("leaf", "top"), None, None),
            P(None, ("leaf", "top"), None, None, None),
            P(None, ("leaf", "top"), None, None),
            P(None, ("leaf", "top"), None, None, None, None),
            P(None, ("leaf", "top"), None, None, None),
            P(("leaf", "top"), None),
        ),
        out_specs=P(None, ("leaf", "top"), None),
        check_vma=False,
    )
```

```python
import jax
import jax.numpy as jnp
from jax import lax
from jax.experimental import pallas as pl
from jax.experimental.pallas import tpu as pltpu
from jax.sharding import PartitionSpec as P

BF = jnp.bfloat16
F32 = jnp.float32
NN = (((1,), (0,)), ((), ()))
NT = (((1,), (1,)), ((), ()))


def dot(a, b, dims=NN):
    return lax.dot_general(a, b, dims, preferred_element_type=F32)


def widen(a):
    half = a.shape[0] // 2
    re, im = a[:half], a[half:]
    return jnp.concatenate(
        [jnp.concatenate([re, -im], axis=1), jnp.concatenate([im, re], axis=1)], axis=0
    )


def times(a, w_re, w_im):
    return dot(widen(a), jnp.concatenate([w_re, w_im], axis=0))


def times_t(a, w_re, w_im):
    return dot(widen(a), jnp.concatenate([w_re, w_im], axis=1), NT)


def rows(ref):
    return jnp.concatenate([ref[0], ref[1]], axis=0)


def put(ref, value):
    half = value.shape[0] // 2
    ref[0] = value[:half].astype(ref.dtype)
    ref[1] = value[half:].astype(ref.dtype)


def bit(pos, level):
    return (pos[0] >> level) & 1


def lift(q, w, pos, level, flip=0):
    child = bit(pos, level) ^ flip
    return times(q, w[0, level, child], w[1, level, child])


def lower(h, w, pos, level, flip=0):
    child = bit(pos, level) ^ flip
    return times_t(h, w[0, level, child], w[1, level, child])


def couple(q, b, pos, level, flip=0):
    return lax.cond(
        (bit(pos, level) ^ flip) == 0,
        lambda: times_t(q, b[0, level], b[1, level]),
        lambda: times(q, b[0, level], b[1, level]),
    )


def split(value, side, keep, send):
    half = value.shape[0] // 2
    part = half // 2
    for c in range(2):
        low = value[c * half : c * half + part]
        high = value[c * half + part : (c + 1) * half]
        keep[c] = jnp.where(side == 0, low, high)
        send[c] = jnp.where(side == 0, high, low)


def join(own, got, side):
    parts = []
    for c in range(2):
        parts.append(jnp.where(side == 0, own[c], got[c]))
        parts.append(jnp.where(side == 0, got[c], own[c]))
    return jnp.concatenate(parts, axis=0)


def side(pos, level):
    if level == 0:
        return (pos[0] ^ (pos[0] >> 1) ^ (pos[0] >> 2) ^ (pos[0] >> 4) ^ (pos[0] >> 6)) & 1
    if level == 1:
        return bit(pos, 1)
    return bit(pos, 2) ^ bit(pos, 3)


def half_lanes(half, n):
    return pl.ds(pl.multiple_of(half * n, n), n)


def skeletons(first, half, x, u, wl, qleaf, ready):
    size = u.shape[2]
    lanes = half_lanes(half, x.shape[2] // 2)
    for block in range(2):
        ready(block)
        at = pl.ds(block * size, size)
        xt = jnp.concatenate([x[0, at, lanes].T, x[1, at, lanes].T], axis=0)
        leaf = first ^ block
        qleaf[leaf] = times(xt, u[0, leaf], u[1, leaf]).astype(BF)
    ready(2)
    q = times(qleaf[0], wl[0, 0, 0], wl[1, 0, 0]) + times(qleaf[1], wl[0, 0, 1], wl[1, 0, 1])
    return q.astype(BF)


def send_kernel(pos, order, x, u, wl, w, qleaf, send, x_v, u_v, wl_v, w0, order_s, sems):
    size = u.shape[2]
    copies = [
        pltpu.make_async_copy(order, order_s, sems.at[0]),
        pltpu.make_async_copy(x.at[:, pl.ds(0, size)], x_v.at[:, pl.ds(0, size)], sems.at[1]),
        pltpu.make_async_copy(u, u_v, sems.at[2]),
        pltpu.make_async_copy(x.at[:, pl.ds(size, size)], x_v.at[:, pl.ds(size, size)], sems.at[3]),
        pltpu.make_async_copy(wl, wl_v, sems.at[4]),
        pltpu.make_async_copy(w.at[:, 0], w0.at[:, 0], sems.at[5]),
    ]
    for copy in copies:
        copy.start()

    copies[0].wait()
    first = order_s[0, 0]

    def ready(step):
        for i in ((1, 2), (3,), (4,))[step]:
            copies[i].wait()

    put(send, skeletons(first, 1 - side(pos, 0), x_v, u_v, wl_v, qleaf, ready))
    copies[5].wait()


def keep_kernel(pos, order, x, u, wl, w0, qleaf, keep, own):
    q = skeletons(order[0, 0], side(pos, 0), x, u, wl, qleaf, lambda step: None)
    put(keep, q)
    put(own, lift(q, w0, pos, 0))


def climb_kernel(level):
    def kernel(pos, got, own, w, *outs):
        q = (rows(own) + lift(rows(got), w, pos, level, 1)).astype(BF)
        if len(outs) == 2:
            split(q, side(pos, level + 1), *outs)
        else:
            put(outs[0], q)

    return kernel


def direct(order, block, x, d, out):
    size = d.shape[2]
    leaf = order[0, 0] ^ block
    at = pl.ds(block * size, size)
    xs = jnp.concatenate([x[0, at], x[1, at]], axis=0)
    re, im = d[0, leaf], d[1, leaf]
    out[0] = dot(jnp.concatenate([re, -im], axis=1), xs)
    out[1] = dot(jnp.concatenate([im, re], axis=1), xs)


def shadow_1(pos, order, keep, w, x, d, own, part):
    put(own, lift(rows(keep), w, pos, 1))
    direct(order, 0, x, d, part)


def shadow_2(pos, order, keep, w, x, d, own, part):
    put(own, lift(rows(keep), w, pos, 2))
    direct(order, 1, x, d, part)


def shadow_3(
    pos, q3, w, b, bl, wl, q_mine, q_other, got0, got0_other, keep2, got2, own, cleaf, c2, c2_oth
):
    put(own, lift(rows(q3), w, pos, 3))
    for part, (q, got) in enumerate(((q_mine, got0), (q_other, got0_other))):
        c0 = couple(rows(got), b, pos, 0).astype(BF)
        left = times_t(q[1], bl[0, 0], bl[1, 0])
        right = times(q[0], bl[0, 0], bl[1, 0])
        cleaf[0, part] = (left + times_t(c0, wl[0, 0, 0], wl[1, 0, 0])).astype(BF)
        cleaf[1, part] = (right + times_t(c0, wl[0, 0, 1], wl[1, 0, 1])).astype(BF)
    put(c2, couple(rows(got2), b, pos, 2))
    put(c2_oth, couple(rows(keep2), b, pos, 2, 1))


def shadow_4(pos, order, q4, got3, w, b, r, cleaf, part_0, part_1, own, top, base):
    put(own, lift(rows(q4), w, pos, 4))
    put(top, couple(rows(got3), b, pos, 3))
    n = part_0.shape[2] // 2
    size = r.shape[2]
    first = order[0, 0]
    for block, direct_part in enumerate((part_0, part_1)):
        leaf = first ^ block
        basis = jnp.concatenate([r[0, leaf], r[1, leaf]], axis=1)
        for part in range(2):
            add = dot(basis, widen(cleaf[leaf, part]), NT)
            lanes = half_lanes(side(pos, 0) ^ part, n)
            for c in range(2):
                base[part, c, pl.ds(block * size, size)] = (
                    direct_part[c, :, lanes] + add[:, c * n : (c + 1) * n]
                )


def product(r, wl, leaf, out):
    put(out, times(jnp.concatenate([r[0, leaf], r[1, leaf]], axis=0), wl[0, 0, leaf], wl[1, 0, leaf]))


def shadow_5(pos, q5, got4, w, b, r, wl, top, own, top_out, path, rw):
    put(own, lift(rows(q5), w, pos, 5))
    c4 = couple(rows(got4), b, pos, 4).astype(BF)
    put(top_out, rows(top) + lower(c4, w, pos, 3))
    w3 = bit(pos, 3)
    put(path, lift(jnp.concatenate([w[0, 3, w3], w[1, 3, w3]], axis=0), w, pos, 4))
    product(r, wl, 0, rw)


def shadow_6(pos, q6, got5, w, b, r, wl, top, path, own, top_out, path_out, rw):
    put(own, lift(rows(q6), w, pos, 6))
    c5 = couple(rows(got5), b, pos, 5).astype(BF)
    put(top_out, rows(top) + times_t(c5, path[0], path[1]))
    put(path_out, lift(rows(path), w, pos, 5))
    product(r, wl, 1, rw)


def shadow_7(pos, got6, w, b, top, path, top_out, path_out):
    c6 = couple(rows(got6), b, pos, 6).astype(BF)
    put(top_out, rows(top) + times_t(c6, path[0], path[1]))
    longer = lift(rows(path), w, pos, 6).astype(BF)
    put(path_out, couple_path(longer, b, pos))


def couple_path(path, b, pos):
    return lax.cond(
        bit(pos, 7) == 0,
        lambda: times(path, b[0, 7], b[1, 7]),
        lambda: times_t(path, b[0, 7], b[1, 7]),
    )


def top_kernel(pos, got, top, path, c_own, c_oth, w, own, send):
    h = (rows(top) + times_t(rows(got), path[0], path[1])).astype(BF)
    put(own, rows(c_own) + lower(h, w, pos, 2))
    put(send, rows(c_oth) + lower(h, w, pos, 2, 1))


def shadow_8(pos, mine, keep1, got1, b, w0, rw0, rw1, c1, c1_oth, g0, g1):
    put(c1, couple(rows(got1), b, pos, 1))
    put(c1_oth, couple(rows(keep1), b, pos, 1, 1))
    put(g0, lift(rows(rw0), w0, pos, 0))
    put(g1, lift(rows(rw1), w0, pos, 0))


def down_kernel(pos, mine, got, c_own, c_oth, w, own, send):
    h = join(mine, got, side(pos, 2))
    put(own, rows(c_own) + lower(h, w, pos, 1))
    put(send, rows(c_oth) + lower(h, w, pos, 1, 1))


def finish(pos, order, mine, got, base, gs, part, out):
    hw = widen(join(mine, got, side(pos, 1)))
    n = base.shape[3]
    for leaf, g in enumerate(gs):
        size = g.shape[1]
        at = pl.ds(pl.multiple_of((order[0, 0] ^ leaf) * size, size), size)
        add = dot(jnp.concatenate([g[0], g[1]], axis=1), hw, NT)
        for c in range(2):
            out[leaf, c] = (base[part, c, at] + add[:, c * n : (c + 1) * n]).astype(BF)
        yield leaf, at


def own_kernel(pos, order, mine, got, base, g0, g1, out):
    for _ in finish(pos, order, mine, got, base, (g0, g1), 0, out):
        pass


def last_kernel(pos, order, mine, got, base, g0, g1, done, out, buf, sems):
    size = g0.shape[1]
    n = base.shape[3]
    copies = []

    def store(src, part, leaf, at):
        lanes = half_lanes(side(pos, 0) ^ part, n)
        copies.append(
            pltpu.make_async_copy(src.at[leaf], out.at[:, at, lanes], sems.at[part, leaf])
        )
        copies[-1].start()

    for leaf in range(2):
        at = pl.ds(pl.multiple_of((order[0, 0] ^ leaf) * size, size), size)
        store(done, 0, leaf, at)
    for leaf, at in finish(pos, order, mine, got, base, (g0, g1), 1, buf):
        store(buf, 1, leaf, at)
    for copy in copies:
        copy.wait()


VMEM = pl.BlockSpec(memory_space=pltpu.VMEM)
SMEM = pl.BlockSpec(memory_space=pltpu.SMEM)
HBM = pl.BlockSpec(memory_space=pltpu.HBM)
GRANT = 20 * 2**20


def call(name, kernel, ins, outs, *args, scratch=(), flops=0, out_spec=VMEM):
    specs = {"s": SMEM, "v": VMEM, "h": HBM}
    moved = sum(a.size * a.dtype.itemsize for a in args)
    return pl.pallas_call(
        kernel,
        out_shape=[jax.ShapeDtypeStruct(shape, dtype) for shape, dtype in outs],
        in_specs=[specs[kind] for kind in ins],
        out_specs=[out_spec] * len(outs),
        scratch_shapes=list(scratch),
        compiler_params=pltpu.CompilerParams(vmem_limit_bytes=GRANT),
        cost_estimate=pl.CostEstimate(flops=flops, bytes_accessed=moved, transcendentals=0),
        name=name,
    )(*args)


def shards(rhs, diag, row_basis, col_basis, wl, bl, cross_w, cross_b, order):
    n = rhs.shape[2]
    rank = col_basis.shape[3]
    size = col_basis.shape[2]
    axes = ("leaf", "top")
    devices = lax.axis_size("leaf") * lax.axis_size("top")
    pos = lax.axis_index(axes).astype(jnp.int32).reshape(1)
    w = cross_w[:, 0]
    b = cross_b[:, 0]

    def swap(value, flip):
        return lax.ppermute(value, axes, [(i, i ^ flip) for i in range(devices)])

    def block(columns, dtype=BF):
        return ((2, columns, rank), dtype)

    mac = 8 * rank * rank
    half, quarter, eighth = n // 2, n // 4, n // 8
    qleaf_shape = ((2, n, rank), BF)
    hbm = [pltpu.with_memory_space_constraint(a, pltpu.HBM) for a in (order, rhs, col_basis, wl, w)]
    q_other, send, x, u, wl, w0 = call(
        "send_half", send_kernel, "shhhhh",
        [qleaf_shape, block(half), (rhs.shape, BF), (col_basis.shape, BF), (wl.shape, BF),
         ((2, 1, 2, rank, rank), BF)],
        pos, *hbm,
        scratch=(pltpu.SMEM(order.shape, jnp.int32), pltpu.SemaphoreType.DMA((6,))),
        flops=mac * n * 3,
    )
    send, w, b, diag, row_basis = lax.optimization_barrier((send, w, b, diag, row_basis))
    got0 = swap(send, 1)
    q_mine, keep0, own = call(
        "keep_half", keep_kernel, "ssvvvv", [qleaf_shape, block(half), block(half, F32)],
        pos, order, x, u, wl, w0, flops=mac * n * 3,
    )
    got0_other = swap(keep0, 1)
    keep1, send = call(
        "climb_0", climb_kernel(0), "svvv", [block(quarter), block(quarter)],
        pos, got0, own, w0, flops=mac * half,
    )
    got1 = swap(send, 3)
    own, part_0 = call(
        "shadow_1", shadow_1, "ssvvvv", [block(quarter, F32), ((2, size, n), F32)],
        pos, order, keep1, w, x, diag, flops=mac * n * 5,
    )
    keep2, send = call(
        "climb_1", climb_kernel(1), "svvv", [block(eighth), block(eighth)],
        pos, got1, own, w, flops=mac * quarter,
    )
    got2 = swap(send, 5)
    own, part_1 = call(
        "shadow_2", shadow_2, "ssvvvv", [block(eighth, F32), ((2, size, n), F32)],
        pos, order, keep2, w, x, diag, flops=mac * n * 5,
    )
    (q3,) = call("climb_2", climb_kernel(2), "svvv", [block(eighth)], pos, got2, own, w, flops=mac * eighth)
    got3 = swap(q3, 13)
    own, cleaf, c2, c2_oth = call(
        "shadow_3", shadow_3, "s" + "v" * 11,
        [block(eighth, F32), ((2, 2, n, rank), BF), block(eighth, F32), block(eighth, F32)],
        pos, q3, w, b, bl, wl, q_mine, q_other, got0, got0_other, keep2, got2, flops=mac * n * 6,
    )
    (q4,) = call("climb_3", climb_kernel(3), "svvv", [block(eighth)], pos, got3, own, w, flops=mac * eighth)
    got4 = swap(q4, 17)
    own, top, base = call(
        "shadow_4", shadow_4, "ss" + "v" * 8,
        [block(eighth, F32), block(eighth, F32), ((2, 2, 2 * size, half), F32)],
        pos, order, q4, got3, w, b, row_basis, cleaf, part_0, part_1, flops=mac * n * 4,
    )
    (q5,) = call("climb_4", climb_kernel(4), "svvv", [block(eighth)], pos, got4, own, w, flops=mac * eighth)
    got5 = swap(q5, 49)
    own, top, path, rw0 = call(
        "shadow_5", shadow_5, "s" + "v" * 7,
        [block(eighth, F32), block(eighth, F32), block(rank), block(size)],
        pos, q5, got4, w, b, row_basis, wl, top, flops=mac * n * 3,
    )
    (q6,) = call("climb_5", climb_kernel(5), "svvv", [block(eighth)], pos, got5, own, w, flops=mac * eighth)
    got6 = swap(q6, 65)
    own, top, path, rw1 = call(
        "shadow_6", shadow_6, "s" + "v" * 8,
        [block(eighth, F32), block(eighth, F32), block(rank), block(size)],
        pos, q6, got5, w, b, row_basis, wl, top, path, flops=mac * n * 3,
    )
    (q7,) = call("climb_6", climb_kernel(6), "svvv", [block(eighth)], pos, got6, own, w, flops=mac * eighth)
    got7 = swap(q7, 193)
    top, path = call(
        "shadow_7", shadow_7, "s" + "v" * 5, [block(eighth, F32), block(rank)],
        pos, got6, w, b, top, path, flops=mac * n * 2,
    )
    mine, send = call(
        "top", top_kernel, "s" + "v" * 6, [block(eighth), block(eighth)],
        pos, got7, top, path, c2, c2_oth, w, flops=mac * eighth * 3,
    )
    got = swap(send, 5)
    c1, c1_oth, g0, g1 = call(
        "shadow_8", shadow_8, "s" + "v" * 7,
        [block(quarter, F32), block(quarter, F32), block(size), block(size)],
        pos, mine, keep1, got1, b, w0, rw0, rw1, flops=mac * n * 5,
    )
    mine, send = call(
        "down", down_kernel, "s" + "v" * 5, [block(quarter), block(quarter)],
        pos, mine, got, c1, c1_oth, w, flops=mac * quarter * 2,
    )
    got = swap(send, 3)
    mine_other = swap(mine, 1)
    got, mine_other = lax.optimization_barrier((got, mine_other))
    got_other = swap(got, 1)
    piece = (2, 2, size, half)
    (done,) = call(
        "own_columns", own_kernel, "ss" + "v" * 5, [(piece, BF)],
        pos, order, mine, got, base, g0, g1, flops=mac * n * 2,
    )
    (out,) = call(
        "other_columns", last_kernel, "ss" + "v" * 6, [(rhs.shape, BF)],
        pos, order, mine_other, got_other, base, g0, g1, done,
        scratch=(pltpu.VMEM(piece, BF), pltpu.SemaphoreType.DMA((2, 2))),
        flops=mac * n * 2, out_spec=HBM,
    )
    return out


def solution(mesh):
    return jax.shard_map(
        shards,
        mesh=mesh,
        in_specs=(
            P(None, ("leaf", "top"), None),
            P(None, ("leaf", "top"), None, None),
            P(None, ("leaf", "top"), None, None),
            P(None, ("leaf", "top"), None, None),
            P(None, ("leaf", "top"), None, None, None),
            P(None, ("leaf", "top"), None, None),
            P(None, ("leaf", "top"), None, None, None, None),
            P(None, ("leaf", "top"), None, None, None),
            P(("leaf", "top"), None),
        ),
        out_specs=P(None, ("leaf", "top"), None),
        check_vma=False,
    )
```

```python
import jax
import jax.numpy as jnp
from jax import lax
from jax.experimental import pallas as pl
from jax.experimental.pallas import tpu as pltpu
from jax.sharding import PartitionSpec as P

BF = jnp.bfloat16
F32 = jnp.float32
NN = (((1,), (0,)), ((), ()))
NT = (((1,), (1,)), ((), ()))


def dot(a, b, dims=NN):
    return lax.dot_general(a, b, dims, preferred_element_type=F32)


def widen(a):
    half = a.shape[0] // 2
    re, im = a[:half], a[half:]
    return jnp.concatenate(
        [jnp.concatenate([re, -im], axis=1), jnp.concatenate([im, re], axis=1)], axis=0
    )


def times(a, w_re, w_im):
    return dot(widen(a), jnp.concatenate([w_re, w_im], axis=0))


def times_t(a, w_re, w_im):
    return dot(widen(a), jnp.concatenate([w_re, w_im], axis=1), NT)


def rows(ref):
    return jnp.concatenate([ref[0], ref[1]], axis=0)


def put(ref, value):
    half = value.shape[0] // 2
    ref[0] = value[:half].astype(ref.dtype)
    ref[1] = value[half:].astype(ref.dtype)


def bit(pos, level):
    return (pos[0] >> level) & 1


def lift(q, w, pos, level, flip=0):
    child = bit(pos, level) ^ flip
    return times(q, w[0, level, child], w[1, level, child])


def lower(h, w, pos, level, flip=0):
    child = bit(pos, level) ^ flip
    return times_t(h, w[0, level, child], w[1, level, child])


def couple(q, b, pos, level, flip=0):
    return lax.cond(
        (bit(pos, level) ^ flip) == 0,
        lambda: times_t(q, b[0, level], b[1, level]),
        lambda: times(q, b[0, level], b[1, level]),
    )


def split(value, side, keep, send):
    half = value.shape[0] // 2
    part = half // 2
    for c in range(2):
        low = value[c * half : c * half + part]
        high = value[c * half + part : (c + 1) * half]
        keep[c] = jnp.where(side == 0, low, high)
        send[c] = jnp.where(side == 0, high, low)


def join(own, got, side):
    parts = []
    for c in range(2):
        parts.append(jnp.where(side == 0, own[c], got[c]))
        parts.append(jnp.where(side == 0, got[c], own[c]))
    return jnp.concatenate(parts, axis=0)


def side(pos, level):
    if level == 0:
        return (pos[0] ^ (pos[0] >> 1) ^ (pos[0] >> 2) ^ (pos[0] >> 4) ^ (pos[0] >> 6)) & 1
    if level == 1:
        return bit(pos, 1)
    return bit(pos, 2) ^ bit(pos, 3)


def half_lanes(half, n):
    return pl.ds(pl.multiple_of(half * n, n), n)


class Levels:
    def __init__(self, ref, start):
        self.ref, self.start = ref, start

    def __getitem__(self, key):
        c, level, child = key
        return self.ref[c, level - self.start, child]


def parent(qleaf, wl):
    q = times(qleaf[0], wl[0, 0, 0], wl[1, 0, 0]) + times(qleaf[1], wl[0, 0, 1], wl[1, 0, 1])
    return q.astype(BF)


def send_kernel(pos, order, x, u, wl, w, qleaf, send, xt, x_v, u_v, wl_v, w0, order_s, sems):
    size = u.shape[2]
    half = x.shape[2] // 2

    def x_copy(block):
        at = pl.ds(block * size, size)
        return pltpu.make_async_copy(x.at[:, at], x_v.at[:, at], sems.at[block])

    def u_copy(leaf):
        return pltpu.make_async_copy(u.at[:, leaf], u_v.at[:, leaf], sems.at[2 + leaf])

    order_copy = pltpu.make_async_copy(order, order_s, sems.at[4])
    wl_copy = pltpu.make_async_copy(wl, wl_v, sems.at[5])
    w_copy = pltpu.make_async_copy(w.at[:, 0], w0.at[:, 0], sems.at[6])
    order_copy.start()
    for i in range(2):
        x_copy(i).start()
        u_copy(i).start()
    wl_copy.start()
    w_copy.start()
    order_copy.wait()
    first = order_s[0, 0]

    def transposed(block, which):
        at = pl.ds(block * size, size)
        lanes = half_lanes(which, half)
        return jnp.concatenate([x_v[0, at, lanes].T, x_v[1, at, lanes].T], axis=0)

    keep = side(pos, 0)
    for block in range(2):
        x_copy(block).wait()
        xt[block] = transposed(block, keep)
        xs = transposed(block, 1 - keep)
        if block == 0:
            u_copy(0).wait()
            u_copy(1).wait()
        leaf = first ^ block
        qleaf[leaf] = times(xs, u_v[0, leaf], u_v[1, leaf]).astype(BF)
    wl_copy.wait()
    put(send, parent(qleaf, wl_v))
    w_copy.wait()


def keep_kernel(pos, order, xt, u, wl, w0, w, qleaf, keep, own, w_low, sem):
    copy = pltpu.make_async_copy(w.at[:, pl.ds(1, 3)], w_low, sem)
    copy.start()
    for block in range(2):
        leaf = order[0, 0] ^ block
        qleaf[leaf] = times(xt[block], u[0, leaf], u[1, leaf]).astype(BF)
    q = parent(qleaf, wl)
    put(keep, q)
    put(own, lift(q, w0, pos, 0))
    copy.wait()


def climb_kernel(level, start):
    def kernel(pos, got, own, w, *outs):
        q = (rows(own) + lift(rows(got), Levels(w, start), pos, level, 1)).astype(BF)
        if len(outs) == 2:
            split(q, side(pos, level + 1), *outs)
        else:
            put(outs[0], q)

    return kernel


def direct(order, block, x, d, out):
    size = d.shape[2]
    leaf = order[0, 0] ^ block
    at = pl.ds(block * size, size)
    xs = jnp.concatenate([x[0, at], x[1, at]], axis=0)
    re, im = d[0, leaf], d[1, leaf]
    out[0] = dot(jnp.concatenate([re, -im], axis=1), xs)
    out[1] = dot(jnp.concatenate([im, re], axis=1), xs)


def shadow_1(pos, order, keep, w, w_all, x, d, own, part, w_high, sem):
    copy = pltpu.make_async_copy(w_all.at[:, pl.ds(4, 4)], w_high, sem)
    copy.start()
    put(own, lift(rows(keep), Levels(w, 1), pos, 1))
    direct(order, 0, x, d, part)
    copy.wait()


def leaf_coupled(pos, q, got, b, bl, wl, cleaf):
    c0 = couple(rows(got), b, pos, 0).astype(BF)
    left = times_t(q[1], bl[0, 0], bl[1, 0])
    right = times(q[0], bl[0, 0], bl[1, 0])
    cleaf[0] = (left + times_t(c0, wl[0, 0, 0], wl[1, 0, 0])).astype(BF)
    cleaf[1] = (right + times_t(c0, wl[0, 0, 1], wl[1, 0, 1])).astype(BF)


def shadow_2(pos, order, keep, w, x, d, own, part):
    put(own, lift(rows(keep), Levels(w, 1), pos, 2))
    direct(order, 1, x, d, part)


def shadow_3(pos, q3, w, b, bl, wl, q_mine, got0, own, cleaf):
    put(own, lift(rows(q3), Levels(w, 1), pos, 3))
    leaf_coupled(pos, q_mine, got0, b, bl, wl, cleaf)


def set_base(pos, order, part, r, cleaf, parts, base):
    n = base.shape[2]
    size = r.shape[2]
    first = order[0, 0]
    lanes = half_lanes(side(pos, 0) ^ part, n)
    for block, direct_part in enumerate(parts):
        leaf = first ^ block
        add = dot(jnp.concatenate([r[0, leaf], r[1, leaf]], axis=1), widen(cleaf[leaf]), NT)
        for c in range(2):
            base[c, pl.ds(block * size, size)] = (
                direct_part[c, :, lanes] + add[:, c * n : (c + 1) * n]
            )


def shadow_4(pos, order, q4, got3, w, b, r, cleaf, part_0, part_1, own, top, base):
    put(own, lift(rows(q4), Levels(w, 4), pos, 4))
    put(top, couple(rows(got3), b, pos, 3))
    set_base(pos, order, 0, r, cleaf, (part_0, part_1), base)


def product(r, wl, leaf, out):
    put(out, times(jnp.concatenate([r[0, leaf], r[1, leaf]], axis=0), wl[0, 0, leaf], wl[1, 0, leaf]))


def shadow_5(pos, q5, got4, w_low, w_high, b, r, wl, top, own, top_out, path, rw):
    low, high = Levels(w_low, 1), Levels(w_high, 4)
    put(own, lift(rows(q5), high, pos, 5))
    c4 = couple(rows(got4), b, pos, 4).astype(BF)
    put(top_out, rows(top) + lower(c4, low, pos, 3))
    w3 = bit(pos, 3)
    put(path, lift(jnp.concatenate([low[0, 3, w3], low[1, 3, w3]], axis=0), high, pos, 4))
    product(r, wl, 0, rw)


def shadow_6(pos, q6, got5, w, b, r, wl, top, path, own, top_out, path_out, rw):
    high = Levels(w, 4)
    put(own, lift(rows(q6), high, pos, 6))
    c5 = couple(rows(got5), b, pos, 5).astype(BF)
    put(top_out, rows(top) + times_t(c5, path[0], path[1]))
    put(path_out, lift(rows(path), high, pos, 5))
    product(r, wl, 1, rw)


def shadow_7(pos, got6, w, b, top, path, keep2, got2, top_out, path_out, c2, c2_oth):
    c6 = couple(rows(got6), b, pos, 6).astype(BF)
    put(top_out, rows(top) + times_t(c6, path[0], path[1]))
    longer = lift(rows(path), Levels(w, 4), pos, 6).astype(BF)
    put(path_out, couple_path(longer, b, pos))
    put(c2, couple(rows(got2), b, pos, 2))
    put(c2_oth, couple(rows(keep2), b, pos, 2, 1))


def couple_path(path, b, pos):
    return lax.cond(
        bit(pos, 7) == 0,
        lambda: times(path, b[0, 7], b[1, 7]),
        lambda: times_t(path, b[0, 7], b[1, 7]),
    )


def top_kernel(pos, got, top, path, c_own, c_oth, w, own, send):
    h = (rows(top) + times_t(rows(got), path[0], path[1])).astype(BF)
    low = Levels(w, 1)
    put(own, rows(c_own) + lower(h, low, pos, 2))
    put(send, rows(c_oth) + lower(h, low, pos, 2, 1))


def shadow_8(pos, mine, keep1, got1, b, w0, rw0, rw1, c1, c1_oth, g0, g1):
    put(c1, couple(rows(got1), b, pos, 1))
    put(c1_oth, couple(rows(keep1), b, pos, 1, 1))
    put(g0, lift(rows(rw0), w0, pos, 0))
    put(g1, lift(rows(rw1), w0, pos, 0))


def down_kernel(pos, mine, got, c_own, c_oth, w, own, send):
    h = join(mine, got, side(pos, 2))
    low = Levels(w, 1)
    put(own, rows(c_own) + lower(h, low, pos, 1))
    put(send, rows(c_oth) + lower(h, low, pos, 1, 1))


def shadow_9(pos, order, mine, q_other, got0_other, b, bl, wl, r, part_0, part_1, base, cleaf):
    leaf_coupled(pos, q_other, got0_other, b, bl, wl, cleaf)
    set_base(pos, order, 1, r, cleaf, (part_0, part_1), base)


def finish(pos, order, mine, got, base, gs, out, tile):
    hw = widen(join(mine, got, side(pos, 1)))
    n = base.shape[2]
    for leaf, g in enumerate(gs):
        size = g.shape[1]
        for step in range(size // tile):
            here = pl.ds(step * tile, tile)
            start = (order[0, 0] ^ leaf) * size + step * tile
            at = pl.ds(pl.multiple_of(start, tile), tile)
            add = dot(jnp.concatenate([g[0, here], g[1, here]], axis=1), hw, NT)
            for c in range(2):
                out[leaf, c, here] = (base[c, at] + add[:, c * n : (c + 1) * n]).astype(BF)
            yield leaf, here, at


def own_kernel(pos, order, mine, got, base, g0, g1, out):
    for _ in finish(pos, order, mine, got, base, (g0, g1), out, g0.shape[1]):
        pass


def last_kernel(pos, order, mine, got, base, g0, g1, done, out, buf, sems):
    size = g0.shape[1]
    n = base.shape[2]
    copies = []

    def store(src, part, at):
        lanes = half_lanes(side(pos, 0) ^ part, n)
        sem = sems.at[len(copies)]
        copies.append(pltpu.make_async_copy(src, out.at[:, at, lanes], sem))
        copies[-1].start()

    for leaf in range(2):
        at = pl.ds(pl.multiple_of((order[0, 0] ^ leaf) * size, size), size)
        store(done.at[leaf], 0, at)
    for leaf, here, at in finish(pos, order, mine, got, base, (g0, g1), buf, size // 2):
        store(buf.at[leaf, :, here], 1, at)
    for copy in copies:
        copy.wait()


VMEM = pl.BlockSpec(memory_space=pltpu.VMEM)
SMEM = pl.BlockSpec(memory_space=pltpu.SMEM)
HBM = pl.BlockSpec(memory_space=pltpu.HBM)
GRANT = 20 * 2**20


def call(name, kernel, ins, outs, *args, scratch=(), flops=0, out_spec=VMEM):
    specs = {"s": SMEM, "v": VMEM, "h": HBM}
    moved = sum(a.size * a.dtype.itemsize for a in args)
    return pl.pallas_call(
        kernel,
        out_shape=[jax.ShapeDtypeStruct(shape, dtype) for shape, dtype in outs],
        in_specs=[specs[kind] for kind in ins],
        out_specs=[out_spec] * len(outs),
        scratch_shapes=list(scratch),
        compiler_params=pltpu.CompilerParams(vmem_limit_bytes=GRANT),
        cost_estimate=pl.CostEstimate(flops=flops, bytes_accessed=moved, transcendentals=0),
        name=name,
    )(*args)


def shards(rhs, diag, row_basis, col_basis, wl, bl, cross_w, cross_b, order):
    n = rhs.shape[2]
    rank = col_basis.shape[3]
    size = col_basis.shape[2]
    axes = ("leaf", "top")
    devices = lax.axis_size("leaf") * lax.axis_size("top")
    pos = lax.axis_index(axes).astype(jnp.int32).reshape(1)
    b = cross_b[:, 0]

    def swap(value, flip):
        return lax.ppermute(value, axes, [(i, i ^ flip) for i in range(devices)])

    def block(columns, dtype=BF):
        return ((2, columns, rank), dtype)

    mac = 8 * rank * rank
    half, quarter, eighth = n // 2, n // 4, n // 8
    qleaf_shape = ((2, n, rank), BF)
    hbm = [pltpu.with_memory_space_constraint(a, pltpu.HBM) for a in (order, rhs, col_basis, wl, cross_w[:, 0])]
    w_hbm = hbm[-1]
    q_other, send, xt, x, u, wl, w0 = call(
        "send_half", send_kernel, "shhhhh",
        [qleaf_shape, block(half), ((2, n, size), BF), (rhs.shape, BF), (col_basis.shape, BF),
         (wl.shape, BF), ((2, 1, 2, rank, rank), BF)],
        pos, *hbm,
        scratch=(pltpu.SMEM(order.shape, jnp.int32), pltpu.SemaphoreType.DMA((7,))),
        flops=mac * n * 3,
    )
    got0 = swap(send, 1)
    q_mine, keep0, own, w_low = call(
        "keep_half", keep_kernel, "ssvvvvh",
        [qleaf_shape, block(half), block(half, F32), ((2, 3, 2, rank, rank), BF)],
        pos, order, xt, u, wl, w0, w_hbm,
        scratch=(pltpu.SemaphoreType.DMA,), flops=mac * n * 3,
    )
    got0_other = swap(keep0, 1)
    keep1, send = call(
        "climb_0", climb_kernel(0, 0), "svvv", [block(quarter), block(quarter)],
        pos, got0, own, w0, flops=mac * half,
    )
    got1 = swap(send, 3)
    own, part_0, w_high = call(
        "shadow_1", shadow_1, "ssvvhvv",
        [block(quarter, F32), ((2, size, n), F32), ((2, 4, 2, rank, rank), BF)],
        pos, order, keep1, w_low, w_hbm, x, diag,
        scratch=(pltpu.SemaphoreType.DMA,), flops=mac * n * 5,
    )
    keep2, send = call(
        "climb_1", climb_kernel(1, 1), "svvv", [block(eighth), block(eighth)],
        pos, got1, own, w_low, flops=mac * quarter,
    )
    got2 = swap(send, 5)
    own, part_1 = call(
        "shadow_2", shadow_2, "ssvvvv", [block(eighth, F32), ((2, size, n), F32)],
        pos, order, keep2, w_low, x, diag, flops=mac * n * 5,
    )

    def climb(level, start, got, own, w):
        return call(
            "climb_%d" % level, climb_kernel(level, start), "svvv", [block(eighth)],
            pos, got, own, w, flops=mac * eighth,
        )[0]

    cleaf_shape = ((2, n, rank), BF)
    base_shape = ((2, 2 * size, half), F32)
    q3 = climb(2, 1, got2, own, w_low)
    got3 = swap(q3, 13)
    own, cleaf = call(
        "shadow_3", shadow_3, "s" + "v" * 7, [block(eighth, F32), cleaf_shape],
        pos, q3, w_low, b, bl, wl, q_mine, got0, flops=mac * n * 4,
    )
    q4 = climb(3, 1, got3, own, w_low)
    got4 = swap(q4, 17)
    own, top, base = call(
        "shadow_4", shadow_4, "ss" + "v" * 8,
        [block(eighth, F32), block(eighth, F32), base_shape],
        pos, order, q4, got3, w_high, b, row_basis, cleaf, part_0, part_1, flops=mac * n * 2,
    )
    q5 = climb(4, 4, got4, own, w_high)
    got5 = swap(q5, 49)
    own, top, path, rw0 = call(
        "shadow_5", shadow_5, "s" + "v" * 8,
        [block(eighth, F32), block(eighth, F32), block(rank), block(size)],
        pos, q5, got4, w_low, w_high, b, row_basis, wl, top, flops=mac * n * 3,
    )
    q6 = climb(5, 4, got5, own, w_high)
    got6 = swap(q6, 65)
    own, top, path, rw1 = call(
        "shadow_6", shadow_6, "s" + "v" * 8,
        [block(eighth, F32), block(eighth, F32), block(rank), block(size)],
        pos, q6, got5, w_high, b, row_basis, wl, top, path, flops=mac * n * 3,
    )
    q7 = climb(6, 4, got6, own, w_high)
    got7 = swap(q7, 193)
    top, path, c2, c2_oth = call(
        "shadow_7", shadow_7, "s" + "v" * 7,
        [block(eighth, F32), block(rank), block(eighth, F32), block(eighth, F32)],
        pos, got6, w_high, b, top, path, keep2, got2, flops=mac * n * 2,
    )
    mine, send = call(
        "top", top_kernel, "s" + "v" * 6, [block(eighth), block(eighth)],
        pos, got7, top, path, c2, c2_oth, w_low, flops=mac * eighth * 3,
    )
    got = swap(send, 5)
    c1, c1_oth, g0, g1 = call(
        "shadow_8", shadow_8, "s" + "v" * 7,
        [block(quarter, F32), block(quarter, F32), block(size), block(size)],
        pos, mine, keep1, got1, b, w0, rw0, rw1, flops=mac * n * 5,
    )
    mine, send = call(
        "down", down_kernel, "s" + "v" * 5, [block(quarter), block(quarter)],
        pos, mine, got, c1, c1_oth, w_low, flops=mac * quarter * 2,
    )
    got = swap(send, 3)
    mine_other = swap(mine, 1)
    (base_other,) = call(
        "shadow_9", shadow_9, "ss" + "v" * 9, [base_shape],
        pos, order, mine, q_other, got0_other, b, bl, wl, row_basis, part_0, part_1,
        scratch=(pltpu.VMEM(*cleaf_shape),), flops=mac * n * 4,
    )
    got, mine_other, base_other = lax.optimization_barrier((got, mine_other, base_other))
    got_other = swap(got, 1)
    piece = (2, 2, size, half)
    (done,) = call(
        "own_columns", own_kernel, "ss" + "v" * 5, [(piece, BF)],
        pos, order, mine, got, base, g0, g1, flops=mac * n * 2,
    )
    (out,) = call(
        "other_columns", last_kernel, "ss" + "v" * 6, [(rhs.shape, BF)],
        pos, order, mine_other, got_other, base_other, g0, g1, done,
        scratch=(pltpu.VMEM(piece, BF), pltpu.SemaphoreType.DMA((6,))),
        flops=mac * n * 2, out_spec=HBM,
    )
    return out


def solution(mesh):
    return jax.shard_map(
        shards,
        mesh=mesh,
        in_specs=(
            P(None, ("leaf", "top"), None),
            P(None, ("leaf", "top"), None, None),
            P(None, ("leaf", "top"), None, None),
            P(None, ("leaf", "top"), None, None),
            P(None, ("leaf", "top"), None, None, None),
            P(None, ("leaf", "top"), None, None),
            P(None, ("leaf", "top"), None, None, None, None),
            P(None, ("leaf", "top"), None, None, None),
            P(("leaf", "top"), None),
        ),
        out_specs=P(None, ("leaf", "top"), None),
        check_vma=False,
    )
```

```python
import jax
import jax.numpy as jnp
from jax import lax
from jax.experimental import pallas as pl
from jax.experimental.pallas import tpu as pltpu
from jax.sharding import PartitionSpec as P

BF = jnp.bfloat16
F32 = jnp.float32
NN = (((1,), (0,)), ((), ()))
NT = (((1,), (1,)), ((), ()))


def dot(a, b, dims=NN):
    return lax.dot_general(a, b, dims, preferred_element_type=F32)


def widen(a):
    half = a.shape[0] // 2
    re, im = a[:half], a[half:]
    return jnp.concatenate(
        [jnp.concatenate([re, -im], axis=1), jnp.concatenate([im, re], axis=1)], axis=0
    )


def times(a, w_re, w_im):
    return dot(widen(a), jnp.concatenate([w_re, w_im], axis=0))


def times_t(a, w_re, w_im):
    return dot(widen(a), jnp.concatenate([w_re, w_im], axis=1), NT)


def rows(ref):
    return jnp.concatenate([ref[0], ref[1]], axis=0)


def put(ref, value):
    half = value.shape[0] // 2
    ref[0] = value[:half].astype(ref.dtype)
    ref[1] = value[half:].astype(ref.dtype)


def bit(pos, level):
    return (pos[0] >> level) & 1


def lift(q, w, pos, level, flip=0):
    child = bit(pos, level) ^ flip
    return times(q, w[0, level, child], w[1, level, child])


def lower(h, w, pos, level, flip=0):
    child = bit(pos, level) ^ flip
    return times_t(h, w[0, level, child], w[1, level, child])


def couple(q, b, pos, level, flip=0):
    return lax.cond(
        (bit(pos, level) ^ flip) == 0,
        lambda: times_t(q, b[0, level], b[1, level]),
        lambda: times(q, b[0, level], b[1, level]),
    )


def split(value, side, keep, send):
    half = value.shape[0] // 2
    part = half // 2
    for c in range(2):
        low = value[c * half : c * half + part]
        high = value[c * half + part : (c + 1) * half]
        keep[c] = jnp.where(side == 0, low, high)
        send[c] = jnp.where(side == 0, high, low)


def join(own, got, side):
    parts = []
    for c in range(2):
        parts.append(jnp.where(side == 0, own[c], got[c]))
        parts.append(jnp.where(side == 0, got[c], own[c]))
    return jnp.concatenate(parts, axis=0)


def side(pos, level):
    if level == 0:
        return (pos[0] ^ (pos[0] >> 1) ^ (pos[0] >> 2) ^ (pos[0] >> 4) ^ (pos[0] >> 6)) & 1
    if level == 1:
        return bit(pos, 1)
    return bit(pos, 2) ^ bit(pos, 3)


def half_lanes(half, n):
    return pl.ds(pl.multiple_of(half * n, n), n)


def parent(qleaf, wl):
    q = times(qleaf[0], wl[0, 0, 0], wl[1, 0, 0]) + times(qleaf[1], wl[0, 0, 1], wl[1, 0, 1])
    return q.astype(BF)


def send_kernel(pos, order, x, u, wl, w, qleaf, send, xt, x_v, u_v, wl_v, w0, order_s, xs, sems):
    size = u.shape[2]
    half = x.shape[2] // 2

    def x_copy(block):
        at = pl.ds(block * size, size)
        return pltpu.make_async_copy(x.at[:, at], x_v.at[:, at], sems.at[block])

    order_copy = pltpu.make_async_copy(order, order_s, sems.at[2])
    u_copy = pltpu.make_async_copy(u, u_v, sems.at[3])
    wl_copy = pltpu.make_async_copy(wl, wl_v, sems.at[4])
    w_copy = pltpu.make_async_copy(w.at[:, 0], w0.at[:, 0], sems.at[5])
    x_copy(0).start()
    x_copy(1).start()
    order_copy.start()
    u_copy.start()
    wl_copy.start()
    w_copy.start()
    keep = side(pos, 0)
    for block in range(2):
        x_copy(block).wait()
        at = pl.ds(block * size, size)
        for out, which in ((xs, 1 - keep), (xt, keep)):
            lanes = half_lanes(which, half)
            out[block, :half] = x_v[0, at, lanes].T
            out[block, half:] = x_v[1, at, lanes].T
    order_copy.wait()
    u_copy.wait()
    for block in range(2):
        leaf = order_s[0, 0] ^ block
        qleaf[leaf] = times(xs[block], u_v[0, leaf], u_v[1, leaf]).astype(BF)
    wl_copy.wait()
    put(send, parent(qleaf, wl_v))
    w_copy.wait()


def keep_kernel(pos, order, xt, u, wl, w0, qleaf, keep, own):
    for block in range(2):
        leaf = order[0, 0] ^ block
        qleaf[leaf] = times(xt[block], u[0, leaf], u[1, leaf]).astype(BF)
    q = parent(qleaf, wl)
    put(keep, q)
    put(own, lift(q, w0, pos, 0))


def climb_kernel(level):
    def kernel(pos, got, own, w, *outs):
        q = (rows(own) + lift(rows(got), w, pos, level, 1)).astype(BF)
        if len(outs) == 2:
            split(q, side(pos, level + 1), *outs)
        else:
            put(outs[0], q)

    return kernel


def direct(order, block, x, d, out):
    size = d.shape[2]
    leaf = order[0, 0] ^ block
    at = pl.ds(block * size, size)
    xs = jnp.concatenate([x[0, at], x[1, at]], axis=0)
    re, im = d[0, leaf], d[1, leaf]
    out[0] = dot(jnp.concatenate([re, -im], axis=1), xs)
    out[1] = dot(jnp.concatenate([im, re], axis=1), xs)


def shadow_1(pos, order, keep, w, x, d, own, part):
    put(own, lift(rows(keep), w, pos, 1))
    direct(order, 0, x, d, part)


def leaf_coupled(pos, q, got, b, bl, wl, cleaf):
    c0 = couple(rows(got), b, pos, 0).astype(BF)
    left = times_t(q[1], bl[0, 0], bl[1, 0])
    right = times(q[0], bl[0, 0], bl[1, 0])
    cleaf[0] = (left + times_t(c0, wl[0, 0, 0], wl[1, 0, 0])).astype(BF)
    cleaf[1] = (right + times_t(c0, wl[0, 0, 1], wl[1, 0, 1])).astype(BF)


def shadow_2(pos, order, keep, w, x, d, b, bl, wl, q_mine, got0, own, part, cleaf):
    put(own, lift(rows(keep), w, pos, 2))
    direct(order, 1, x, d, part)
    leaf_coupled(pos, q_mine, got0, b, bl, wl, cleaf)


def shadow_3(pos, q3, w, b, bl, wl, q_other, got0_other, own, cleaf):
    put(own, lift(rows(q3), w, pos, 3))
    leaf_coupled(pos, q_other, got0_other, b, bl, wl, cleaf)


def set_base(pos, order, part, r, cleaf, parts, base):
    n = base.shape[2]
    size = r.shape[2]
    first = order[0, 0]
    lanes = half_lanes(side(pos, 0) ^ part, n)
    for block, direct_part in enumerate(parts):
        leaf = first ^ block
        add = dot(jnp.concatenate([r[0, leaf], r[1, leaf]], axis=1), widen(cleaf[leaf]), NT)
        for c in range(2):
            base[c, pl.ds(block * size, size)] = (
                direct_part[c, :, lanes] + add[:, c * n : (c + 1) * n]
            )


def shadow_4(pos, order, q4, got3, w, b, r, cleaf, part_0, part_1, own, top, base):
    put(own, lift(rows(q4), w, pos, 4))
    put(top, couple(rows(got3), b, pos, 3))
    set_base(pos, order, 0, r, cleaf, (part_0, part_1), base)


def product(r, wl, leaf, out):
    put(out, times(jnp.concatenate([r[0, leaf], r[1, leaf]], axis=0), wl[0, 0, leaf], wl[1, 0, leaf]))


def shadow_5(pos, q5, got4, w, b, r, wl, top, own, top_out, path, rw):
    put(own, lift(rows(q5), w, pos, 5))
    c4 = couple(rows(got4), b, pos, 4).astype(BF)
    put(top_out, rows(top) + lower(c4, w, pos, 3))
    w3 = bit(pos, 3)
    put(path, lift(jnp.concatenate([w[0, 3, w3], w[1, 3, w3]], axis=0), w, pos, 4))
    product(r, wl, 0, rw)


def shadow_6(pos, q6, got5, w, b, r, wl, top, path, own, top_out, path_out, rw):
    put(own, lift(rows(q6), w, pos, 6))
    c5 = couple(rows(got5), b, pos, 5).astype(BF)
    put(top_out, rows(top) + times_t(c5, path[0], path[1]))
    put(path_out, lift(rows(path), w, pos, 5))
    product(r, wl, 1, rw)


def shadow_7(pos, got6, w, b, top, path, keep2, got2, top_out, path_out, c2, c2_oth):
    c6 = couple(rows(got6), b, pos, 6).astype(BF)
    put(top_out, rows(top) + times_t(c6, path[0], path[1]))
    longer = lift(rows(path), w, pos, 6).astype(BF)
    put(path_out, couple_path(longer, b, pos))
    put(c2, couple(rows(got2), b, pos, 2))
    put(c2_oth, couple(rows(keep2), b, pos, 2, 1))


def couple_path(path, b, pos):
    return lax.cond(
        bit(pos, 7) == 0,
        lambda: times(path, b[0, 7], b[1, 7]),
        lambda: times_t(path, b[0, 7], b[1, 7]),
    )


def top_kernel(pos, got, top, path, c_own, c_oth, w, own, send):
    h = (rows(top) + times_t(rows(got), path[0], path[1])).astype(BF)
    put(own, rows(c_own) + lower(h, w, pos, 2))
    put(send, rows(c_oth) + lower(h, w, pos, 2, 1))


def shadow_8(pos, mine, keep1, got1, b, w0, rw0, rw1, c1, c1_oth, g0, g1):
    put(c1, couple(rows(got1), b, pos, 1))
    put(c1_oth, couple(rows(keep1), b, pos, 1, 1))
    put(g0, lift(rows(rw0), w0, pos, 0))
    put(g1, lift(rows(rw1), w0, pos, 0))


def down_kernel(pos, mine, got, c_own, c_oth, w, own, send):
    h = join(mine, got, side(pos, 2))
    put(own, rows(c_own) + lower(h, w, pos, 1))
    put(send, rows(c_oth) + lower(h, w, pos, 1, 1))


def shadow_9(pos, order, mine, r, cleaf, part_0, part_1, base):
    set_base(pos, order, 1, r, cleaf, (part_0, part_1), base)


def finish(pos, order, mine, got, base, gs, out, tile):
    hw = widen(join(mine, got, side(pos, 1)))
    n = base.shape[2]
    for leaf, g in enumerate(gs):
        size = g.shape[1]
        for step in range(size // tile):
            here = pl.ds(step * tile, tile)
            start = (order[0, 0] ^ leaf) * size + step * tile
            at = pl.ds(pl.multiple_of(start, tile), tile)
            add = dot(jnp.concatenate([g[0, here], g[1, here]], axis=1), hw, NT)
            for c in range(2):
                out[leaf, c, here] = (base[c, at] + add[:, c * n : (c + 1) * n]).astype(BF)
            yield leaf, here, at


def own_kernel(pos, order, mine, got, base, g0, g1, out):
    for _ in finish(pos, order, mine, got, base, (g0, g1), out, g0.shape[1]):
        pass


def last_kernel(pos, order, mine, got, base, g0, g1, done, out, buf, sems):
    size = g0.shape[1]
    n = base.shape[2]
    copies = []

    def store(src, part, at):
        lanes = half_lanes(side(pos, 0) ^ part, n)
        sem = sems.at[len(copies)]
        copies.append(pltpu.make_async_copy(src, out.at[:, at, lanes], sem))
        copies[-1].start()

    for leaf in range(2):
        at = pl.ds(pl.multiple_of((order[0, 0] ^ leaf) * size, size), size)
        store(done.at[leaf], 0, at)
    for leaf, here, at in finish(pos, order, mine, got, base, (g0, g1), buf, size):
        store(buf.at[leaf, :, here], 1, at)
    for copy in copies:
        copy.wait()


VMEM = pl.BlockSpec(memory_space=pltpu.VMEM)
SMEM = pl.BlockSpec(memory_space=pltpu.SMEM)
HBM = pl.BlockSpec(memory_space=pltpu.HBM)
GRANT = 20 * 2**20


def call(name, kernel, ins, outs, *args, scratch=(), flops=0, out_spec=VMEM):
    specs = {"s": SMEM, "v": VMEM, "h": HBM}
    moved = sum(a.size * a.dtype.itemsize for a in args)
    return pl.pallas_call(
        kernel,
        out_shape=[jax.ShapeDtypeStruct(shape, dtype) for shape, dtype in outs],
        in_specs=[specs[kind] for kind in ins],
        out_specs=[out_spec] * len(outs),
        scratch_shapes=list(scratch),
        compiler_params=pltpu.CompilerParams(vmem_limit_bytes=GRANT),
        cost_estimate=pl.CostEstimate(flops=flops, bytes_accessed=moved, transcendentals=0),
        name=name,
    )(*args)


def shards(rhs, diag, row_basis, col_basis, wl, bl, cross_w, cross_b, order):
    n = rhs.shape[2]
    rank = col_basis.shape[3]
    size = col_basis.shape[2]
    axes = ("leaf", "top")
    devices = lax.axis_size("leaf") * lax.axis_size("top")
    pos = lax.axis_index(axes).astype(jnp.int32).reshape(1)
    w = cross_w[:, 0]
    b = cross_b[:, 0]

    def swap(value, flip):
        return lax.ppermute(value, axes, [(i, i ^ flip) for i in range(devices)])

    def block(columns, dtype=BF):
        return ((2, columns, rank), dtype)

    mac = 8 * rank * rank
    half, quarter, eighth = n // 2, n // 4, n // 8
    qleaf_shape = ((2, n, rank), BF)
    hbm = [pltpu.with_memory_space_constraint(a, pltpu.HBM) for a in (order, rhs, col_basis, wl, w)]
    q_other, send, xt, x, u, wl, w0 = call(
        "send_half", send_kernel, "shhhhh",
        [qleaf_shape, block(half), ((2, n, size), BF), (rhs.shape, BF), (col_basis.shape, BF),
         (wl.shape, BF), ((2, 1, 2, rank, rank), BF)],
        pos, *hbm,
        scratch=(
            pltpu.SMEM(order.shape, jnp.int32),
            pltpu.VMEM((2, n, size), BF),
            pltpu.SemaphoreType.DMA((6,)),
        ),
        flops=mac * n * 3,
    )
    got0 = swap(send, 1)
    q_mine, keep0, own = call(
        "keep_half", keep_kernel, "ssvvvv", [qleaf_shape, block(half), block(half, F32)],
        pos, order, xt, u, wl, w0, flops=mac * n * 3,
    )
    got0_other = swap(keep0, 1)
    keep1, send = call(
        "climb_0", climb_kernel(0), "svvv", [block(quarter), block(quarter)],
        pos, got0, own, w0, flops=mac * half,
    )
    got1 = swap(send, 3)
    own, part_0 = call(
        "shadow_1", shadow_1, "ssvvvv", [block(quarter, F32), ((2, size, n), F32)],
        pos, order, keep1, w, x, diag, flops=mac * n * 5,
    )
    keep2, send = call(
        "climb_1", climb_kernel(1), "svvv", [block(eighth), block(eighth)],
        pos, got1, own, w, flops=mac * quarter,
    )
    got2 = swap(send, 5)
    cleaf_shape = ((2, n, rank), BF)
    own, part_1, cleaf = call(
        "shadow_2", shadow_2, "ss" + "v" * 9,
        [block(eighth, F32), ((2, size, n), F32), cleaf_shape],
        pos, order, keep2, w, x, diag, b, bl, wl, q_mine, got0, flops=mac * n * 8,
    )

    def climb(level, got, own):
        return call(
            "climb_%d" % level, climb_kernel(level), "svvv", [block(eighth)],
            pos, got, own, w, flops=mac * eighth,
        )[0]

    base_shape = ((2, 2 * size, half), F32)
    q3 = climb(2, got2, own)
    got3 = swap(q3, 13)
    own, cleaf_other = call(
        "shadow_3", shadow_3, "s" + "v" * 7, [block(eighth, F32), cleaf_shape],
        pos, q3, w, b, bl, wl, q_other, got0_other, flops=mac * n * 4,
    )
    q4 = climb(3, got3, own)
    got4 = swap(q4, 17)
    own, top, base = call(
        "shadow_4", shadow_4, "ss" + "v" * 8,
        [block(eighth, F32), block(eighth, F32), base_shape],
        pos, order, q4, got3, w, b, row_basis, cleaf, part_0, part_1, flops=mac * n * 2,
    )
    q5 = climb(4, got4, own)
    got5 = swap(q5, 49)
    own, top, path, rw0 = call(
        "shadow_5", shadow_5, "s" + "v" * 7,
        [block(eighth, F32), block(eighth, F32), block(rank), block(size)],
        pos, q5, got4, w, b, row_basis, wl, top, flops=mac * n * 3,
    )
    q6 = climb(5, got5, own)
    got6 = swap(q6, 65)
    own, top, path, rw1 = call(
        "shadow_6", shadow_6, "s" + "v" * 8,
        [block(eighth, F32), block(eighth, F32), block(rank), block(size)],
        pos, q6, got5, w, b, row_basis, wl, top, path, flops=mac * n * 3,
    )
    q7 = climb(6, got6, own)
    got7 = swap(q7, 193)
    top, path, c2, c2_oth = call(
        "shadow_7", shadow_7, "s" + "v" * 7,
        [block(eighth, F32), block(rank), block(eighth, F32), block(eighth, F32)],
        pos, got6, w, b, top, path, keep2, got2, flops=mac * n * 2,
    )
    mine, send = call(
        "top", top_kernel, "s" + "v" * 6, [block(eighth), block(eighth)],
        pos, got7, top, path, c2, c2_oth, w, flops=mac * eighth * 3,
    )
    got = swap(send, 5)
    c1, c1_oth, g0, g1 = call(
        "shadow_8", shadow_8, "s" + "v" * 7,
        [block(quarter, F32), block(quarter, F32), block(size), block(size)],
        pos, mine, keep1, got1, b, w0, rw0, rw1, flops=mac * n * 5,
    )
    mine, send = call(
        "down", down_kernel, "s" + "v" * 5, [block(quarter), block(quarter)],
        pos, mine, got, c1, c1_oth, w, flops=mac * quarter * 2,
    )
    got = swap(send, 3)
    mine_other = swap(mine, 1)
    (base_other,) = call(
        "shadow_9", shadow_9, "ss" + "v" * 5, [base_shape],
        pos, order, mine, row_basis, cleaf_other, part_0, part_1, flops=mac * n * 2,
    )
    got, mine_other, base_other = lax.optimization_barrier((got, mine_other, base_other))
    got_other = swap(got, 1)
    piece = (2, 2, size, half)
    (done,) = call(
        "own_columns", own_kernel, "ss" + "v" * 5, [(piece, BF)],
        pos, order, mine, got, base, g0, g1, flops=mac * n * 2,
    )
    (out,) = call(
        "other_columns", last_kernel, "ss" + "v" * 6, [(rhs.shape, BF)],
        pos, order, mine_other, got_other, base_other, g0, g1, done,
        scratch=(pltpu.VMEM(piece, BF), pltpu.SemaphoreType.DMA((6,))),
        flops=mac * n * 2, out_spec=HBM,
    )
    return out


def solution(mesh):
    return jax.shard_map(
        shards,
        mesh=mesh,
        in_specs=(
            P(None, ("leaf", "top"), None),
            P(None, ("leaf", "top"), None, None),
            P(None, ("leaf", "top"), None, None),
            P(None, ("leaf", "top"), None, None),
            P(None, ("leaf", "top"), None, None, None),
            P(None, ("leaf", "top"), None, None),
            P(None, ("leaf", "top"), None, None, None, None),
            P(None, ("leaf", "top"), None, None, None),
            P(("leaf", "top"), None),
        ),
        out_specs=P(None, ("leaf", "top"), None),
        check_vma=False,
    )
```

```python
import jax
import jax.numpy as jnp
from jax import lax
from jax.experimental import pallas as pl
from jax.experimental.pallas import tpu as pltpu
from jax.sharding import PartitionSpec as P

BF = jnp.bfloat16
F32 = jnp.float32
NN = (((1,), (0,)), ((), ()))
NT = (((1,), (1,)), ((), ()))


def dot(a, b, dims=NN):
    return lax.dot_general(a, b, dims, preferred_element_type=F32)


def widen(a):
    half = a.shape[0] // 2
    re, im = a[:half], a[half:]
    return jnp.concatenate(
        [jnp.concatenate([re, -im], axis=1), jnp.concatenate([im, re], axis=1)], axis=0
    )


def times(a, w_re, w_im):
    return dot(widen(a), jnp.concatenate([w_re, w_im], axis=0))


def times_t(a, w_re, w_im):
    return dot(widen(a), jnp.concatenate([w_re, w_im], axis=1), NT)


def rows(ref):
    return jnp.concatenate([ref[0], ref[1]], axis=0)


def put(ref, value):
    half = value.shape[0] // 2
    ref[0] = value[:half].astype(ref.dtype)
    ref[1] = value[half:].astype(ref.dtype)


def bit(pos, level):
    return (pos[0] >> level) & 1


def lift(q, w, pos, level, flip=0):
    child = bit(pos, level) ^ flip
    return times(q, w[0, level, child], w[1, level, child])


def lower(h, w, pos, level, flip=0):
    child = bit(pos, level) ^ flip
    return times_t(h, w[0, level, child], w[1, level, child])


def couple(q, b, pos, level, flip=0):
    return lax.cond(
        (bit(pos, level) ^ flip) == 0,
        lambda: times_t(q, b[0, level], b[1, level]),
        lambda: times(q, b[0, level], b[1, level]),
    )


def split(value, side, keep, send):
    half = value.shape[0] // 2
    part = half // 2
    for c in range(2):
        low = value[c * half : c * half + part]
        high = value[c * half + part : (c + 1) * half]
        keep[c] = jnp.where(side == 0, low, high)
        send[c] = jnp.where(side == 0, high, low)


def join(own, got, side):
    parts = []
    for c in range(2):
        parts.append(jnp.where(side == 0, own[c], got[c]))
        parts.append(jnp.where(side == 0, got[c], own[c]))
    return jnp.concatenate(parts, axis=0)


def side(pos, level):
    if level == 0:
        return (pos[0] ^ (pos[0] >> 1) ^ (pos[0] >> 2) ^ (pos[0] >> 4) ^ (pos[0] >> 6)) & 1
    if level == 1:
        return bit(pos, 1)
    return bit(pos, 2) ^ bit(pos, 3)


def half_lanes(half, n):
    return pl.ds(pl.multiple_of(half * n, n), n)


def parent(qleaf, wl):
    q = times(qleaf[0], wl[0, 0, 0], wl[1, 0, 0]) + times(qleaf[1], wl[0, 0, 1], wl[1, 0, 1])
    return q.astype(BF)


def send_kernel(pos, order, x, u, wl, w, qleaf, send, xt, x_v, u_v, wl_v, w0, order_s, sems):
    size = u.shape[2]
    part = x.shape[2] // 4

    def x_copy(block):
        at = pl.ds(block * size, size)
        return pltpu.make_async_copy(x.at[:, at], x_v.at[:, at], sems.at[block])

    order_copy = pltpu.make_async_copy(order, order_s, sems.at[2])
    u_copy = pltpu.make_async_copy(u, u_v, sems.at[3])
    wl_copy = pltpu.make_async_copy(wl, wl_v, sems.at[4])
    w_copy = pltpu.make_async_copy(w.at[:, 0], w0.at[:, 0], sems.at[5])
    x_copy(0).start()
    x_copy(1).start()
    order_copy.start()
    u_copy.start()
    wl_copy.start()
    w_copy.start()
    for block in range(2):
        x_copy(block).wait()
        at = pl.ds(block * size, size)
        for c in range(2):
            turned = x_v[c, at].T
            for s1 in range(2):
                for s0 in range(2):
                    here = (2 * s1 + s0) * part
                    to = (2 * c + s1) * part
                    xt[s0, block, to : to + part] = turned[here : here + part]
    order_copy.wait()
    u_copy.wait()
    share = 1 - side(pos, 0)
    for block in range(2):
        leaf = order_s[0, 0] ^ block
        qleaf[leaf] = times(xt[share, block], u_v[0, leaf], u_v[1, leaf]).astype(BF)
    wl_copy.wait()
    put(send, parent(qleaf, wl_v))
    w_copy.wait()


def keep_kernel(pos, order, xt, u, wl, w0, qleaf, keep, own):
    share = side(pos, 0)
    for block in range(2):
        leaf = order[0, 0] ^ block
        qleaf[leaf] = times(xt[share, block], u[0, leaf], u[1, leaf]).astype(BF)
    q = parent(qleaf, wl)
    put(keep, q)
    put(own, lift(q, w0, pos, 0))


def climb_kernel(level):
    def kernel(pos, got, own, w, *outs):
        q = (rows(own) + lift(rows(got), w, pos, level, 1)).astype(BF)
        if len(outs) == 2:
            split(q, side(pos, level + 1), *outs)
        else:
            put(outs[0], q)

    return kernel


def direct(order, block, x, d, out):
    size = d.shape[2]
    leaf = order[0, 0] ^ block
    at = pl.ds(block * size, size)
    xs = jnp.concatenate([x[0, at], x[1, at]], axis=0)
    re, im = d[0, leaf], d[1, leaf]
    out[0] = dot(jnp.concatenate([re, -im], axis=1), xs)
    out[1] = dot(jnp.concatenate([im, re], axis=1), xs)


def stack(w, level, child):
    return jnp.concatenate([w[0, level, child], w[1, level, child]], axis=0)


def shadow_1(pos, order, keep, w, w0, wl, x, d, own, part, paths):
    put(own, lift(rows(keep), w, pos, 1))
    two = lift(stack(w0, 0, bit(pos, 0)), w, pos, 1).astype(BF)
    half = two.shape[0] // 2
    for leaf in range(2):
        put(paths.at[leaf], times(stack(wl, 0, leaf), two[:half], two[half:]))
    direct(order, 0, x, d, part)


def product(r, paths, leaf, out):
    put(out, times(rows(r.at[:, leaf]), paths[leaf, 0], paths[leaf, 1]))


def shadow_2(pos, order, keep, w, x, d, r, paths, own, part, g):
    put(own, lift(rows(keep), w, pos, 2))
    direct(order, 1, x, d, part)
    product(r, paths, 0, g)


def shadow_3(pos, q3, w, b, r, paths, keep2, got2, own, c2, c2_oth, g):
    put(own, lift(rows(q3), w, pos, 3))
    put(c2, couple(rows(got2), b, pos, 2))
    put(c2_oth, couple(rows(keep2), b, pos, 2, 1))
    product(r, paths, 1, g)


def leaf_coupled(pos, q, got0, got1, got1_far, b, bl, w0, wl, cleaf):
    c1 = couple(join(got1, got1_far, bit(pos, 1)), b, pos, 1).astype(BF)
    c0 = (couple(rows(got0), b, pos, 0) + lower(c1, w0, pos, 0)).astype(BF)
    left = times_t(q[1], bl[0, 0], bl[1, 0])
    right = times(q[0], bl[0, 0], bl[1, 0])
    put(cleaf.at[0], left + times_t(c0, wl[0, 0, 0], wl[1, 0, 0]))
    put(cleaf.at[1], right + times_t(c0, wl[0, 0, 1], wl[1, 0, 1]))


def shares(pos, mine, other):
    a = side(pos, 0)
    half = mine.shape[0] // 2
    low = jnp.where(a == 0, mine, other)
    high = jnp.where(a == 0, other, mine)
    return jnp.concatenate([low[:half], high[:half], low[half:], high[half:]], axis=0)


def set_base(pos, order, tile, r, cleaf, cleaf_other, parts, base):
    n = base.shape[2]
    size = r.shape[2]
    part = n // 2
    at = pl.ds(pl.multiple_of(tile * part, part), part)
    lanes = half_lanes(tile, n)
    for block, direct_part in enumerate(parts):
        leaf = order[0, 0] ^ block
        h = [jnp.concatenate([c[leaf, 0, at], c[leaf, 1, at]], axis=0) for c in (cleaf, cleaf_other)]
        basis = jnp.concatenate([r[0, leaf], r[1, leaf]], axis=1)
        add = dot(basis, widen(shares(pos, *h)), NT)
        for c in range(2):
            base[c, pl.ds(block * size, size)] = (
                direct_part[c, :, lanes] + add[:, c * n : (c + 1) * n]
            )


def shadow_4(pos, q4, got3, w, b, own, top):
    put(own, lift(rows(q4), w, pos, 4))
    put(top, couple(rows(got3), b, pos, 3))


def shadow_5(pos, q5, got4, w, b, top, own, top_out, path_5, path_6):
    put(own, lift(rows(q5), w, pos, 5))
    c4 = couple(rows(got4), b, pos, 4).astype(BF)
    put(top_out, rows(top) + lower(c4, w, pos, 3))
    path = lift(stack(w, 3, bit(pos, 3)), w, pos, 4).astype(BF)
    put(path_5, path)
    put(path_6, lift(path, w, pos, 5))


def shadow_6(pos, q6, got5, w, b, top, path, q, got0, got1, got1_far, bl, w0, wl, own, top_out, cleaf):
    put(own, lift(rows(q6), w, pos, 6))
    c5 = couple(rows(got5), b, pos, 5).astype(BF)
    put(top_out, rows(top) + times_t(c5, path[0], path[1]))
    leaf_coupled(pos, q, got0, got1, got1_far, b, bl, w0, wl, cleaf)


def shadow_7(pos, got6, w, b, top, path, q, got0, got1, got1_far, bl, w0, wl, top_out, path_out, cleaf):
    c6 = couple(rows(got6), b, pos, 6).astype(BF)
    put(top_out, rows(top) + times_t(c6, path[0], path[1]))
    longer = lift(rows(path), w, pos, 6).astype(BF)
    put(path_out, couple_path(longer, b, pos))
    leaf_coupled(pos, q, got0, got1, got1_far, b, bl, w0, wl, cleaf)


def couple_path(path, b, pos):
    return lax.cond(
        bit(pos, 7) == 0,
        lambda: times(path, b[0, 7], b[1, 7]),
        lambda: times_t(path, b[0, 7], b[1, 7]),
    )


def top_kernel(pos, got, top, path, c_oth, w, send, h_out):
    h = (rows(top) + times_t(rows(got), path[0], path[1])).astype(BF)
    put(h_out, h)
    put(send, rows(c_oth) + lower(h, w, pos, 2, 1))


def own_kernel(pos, h, send, c_own, w, own):
    put(own, rows(c_own) + lower(rows(h), w, pos, 2))


def shadow_8(pos, order, send, r, cleaf, cleaf_other, part_0, part_1, base):
    set_base(pos, order, bit(pos, 1), r, cleaf, cleaf_other, (part_0, part_1), base)


def shadow_9(pos, order, got, far, far_other, r, cleaf, cleaf_other, part_0, part_1, base):
    set_base(pos, order, 1 - bit(pos, 1), r, cleaf, cleaf_other, (part_0, part_1), base)


def finish(pos, order, h_mine, h_other, base, gs, out):
    f = side(pos, 2)
    hw = widen(shares(pos, join(*h_mine, f), join(*h_other, f)))
    n = base.shape[2]
    for leaf, g in enumerate(gs):
        size = g.shape[1]
        at = pl.ds(pl.multiple_of((order[0, 0] ^ leaf) * size, size), size)
        add = dot(jnp.concatenate([g[0], g[1]], axis=1), hw, NT)
        for c in range(2):
            out[leaf, c] = (base[c, at] + add[:, c * n : (c + 1) * n]).astype(BF)
        yield leaf, at


def near_kernel(pos, order, mine, got, mine_other, got_other, base, g0, g1, out):
    for _ in finish(pos, order, (mine, got), (mine_other, got_other), base, (g0, g1), out):
        pass


def last_kernel(pos, order, mine, got, mine_other, got_other, base, g0, g1, done, out, buf, sems):
    size = g0.shape[1]
    n = base.shape[2]
    near = bit(pos, 1)
    copies = []

    def store(src, tile, leaf, at):
        sem = sems.at[len(copies)]
        copies.append(pltpu.make_async_copy(src.at[leaf], out.at[:, at, half_lanes(tile, n)], sem))
        copies[-1].start()

    for leaf in range(2):
        at = pl.ds(pl.multiple_of((order[0, 0] ^ leaf) * size, size), size)
        store(done, near, leaf, at)
    for leaf, at in finish(pos, order, (mine, got), (mine_other, got_other), base, (g0, g1), buf):
        store(buf, 1 - near, leaf, at)
    for copy in copies:
        copy.wait()


VMEM = pl.BlockSpec(memory_space=pltpu.VMEM)
SMEM = pl.BlockSpec(memory_space=pltpu.SMEM)
HBM = pl.BlockSpec(memory_space=pltpu.HBM)
GRANT = 20 * 2**20


def call(name, kernel, ins, outs, *args, scratch=(), flops=0, out_spec=VMEM):
    specs = {"s": SMEM, "v": VMEM, "h": HBM}
    moved = sum(a.size * a.dtype.itemsize for a in args)
    return pl.pallas_call(
        kernel,
        out_shape=[jax.ShapeDtypeStruct(shape, dtype) for shape, dtype in outs],
        in_specs=[specs[kind] for kind in ins],
        out_specs=[out_spec] * len(outs),
        scratch_shapes=list(scratch),
        compiler_params=pltpu.CompilerParams(vmem_limit_bytes=GRANT),
        cost_estimate=pl.CostEstimate(flops=flops, bytes_accessed=moved, transcendentals=0),
        name=name,
    )(*args)


def shards(rhs, diag, row_basis, col_basis, wl, bl, cross_w, cross_b, order):
    n = rhs.shape[2]
    rank = col_basis.shape[3]
    size = col_basis.shape[2]
    axes = ("leaf", "top")
    devices = lax.axis_size("leaf") * lax.axis_size("top")
    pos = lax.axis_index(axes).astype(jnp.int32).reshape(1)
    w = cross_w[:, 0]
    b = cross_b[:, 0]

    def swap(value, flip):
        return lax.ppermute(value, axes, [(i, i ^ flip) for i in range(devices)])

    def block(columns, dtype=BF):
        return ((2, columns, rank), dtype)

    mac = 8 * rank * rank
    half, quarter, eighth = n // 2, n // 4, n // 8
    qleaf_shape = ((2, n, rank), BF)
    hbm = [pltpu.with_memory_space_constraint(a, pltpu.HBM) for a in (order, rhs, col_basis, wl, w)]
    q_other, send, xt, x, u, wl, w0 = call(
        "send_half", send_kernel, "shhhhh",
        [qleaf_shape, block(half), ((2, 2, n, size), BF), (rhs.shape, BF), (col_basis.shape, BF),
         (wl.shape, BF), ((2, 1, 2, rank, rank), BF)],
        pos, *hbm,
        scratch=(pltpu.SMEM(order.shape, jnp.int32), pltpu.SemaphoreType.DMA((6,))),
        flops=mac * n * 3,
    )
    got0 = swap(send, 1)
    q_mine, keep0, own = call(
        "keep_half", keep_kernel, "ssvvvv", [qleaf_shape, block(half), block(half, F32)],
        pos, order, xt, u, wl, w0, flops=mac * n * 3,
    )
    got0_other = swap(keep0, 1)
    keep1, send = call(
        "climb_0", climb_kernel(0), "svvv", [block(quarter), block(quarter)],
        pos, got0, own, w0, flops=mac * half,
    )
    got1 = swap(send, 3)
    own, part_0, paths = call(
        "shadow_1", shadow_1, "ss" + "v" * 6,
        [block(quarter, F32), ((2, size, n), F32), ((2, 2, rank, rank), BF)],
        pos, order, keep1, w, w0, wl, x, diag, flops=mac * n * 8,
    )
    keep2, send = call(
        "climb_1", climb_kernel(1), "svvv", [block(eighth), block(eighth)],
        pos, got1, own, w, flops=mac * quarter,
    )
    got2 = swap(send, 5)
    own, part_1, g0 = call(
        "shadow_2", shadow_2, "ss" + "v" * 6,
        [block(eighth, F32), ((2, size, n), F32), block(size)],
        pos, order, keep2, w, x, diag, row_basis, paths, flops=mac * n * 7,
    )

    def climb(level, got, own):
        return call(
            "climb_%d" % level, climb_kernel(level), "svvv", [block(eighth)],
            pos, got, own, w, flops=mac * eighth,
        )[0]

    top_shape = block(eighth, F32)
    cleaf_shape = ((2, 2, half, rank), BF)
    base_shape = ((2, 2 * size, half), F32)
    q3 = climb(2, got2, own)
    got3 = swap(q3, 13)
    own, c2, c2_oth, g1 = call(
        "shadow_3", shadow_3, "s" + "v" * 7, [top_shape, top_shape, top_shape, block(size)],
        pos, q3, w, b, row_basis, paths, keep2, got2, flops=mac * n * 3,
    )
    q4 = climb(3, got3, own)
    q4, keep1 = lax.optimization_barrier((q4, keep1))
    got4 = swap(q4, 17)
    own, top = call(
        "shadow_4", shadow_4, "s" + "v" * 4, [top_shape, top_shape],
        pos, q4, got3, w, b, flops=mac * half,
    )
    got1_far, got1_far_other = swap(keep1, 3), swap(keep1, 2)
    got1_other = swap(got1, 1)
    q5 = climb(4, got4, own)
    got5 = swap(q5, 49)
    own, top, path_5, path_6 = call(
        "shadow_5", shadow_5, "s" + "v" * 5, [top_shape, top_shape, block(rank), block(rank)],
        pos, q5, got4, w, b, top, flops=mac * n * 2,
    )
    q6 = climb(5, got5, own)
    got6 = swap(q6, 65)
    own, top, cleaf = call(
        "shadow_6", shadow_6, "s" + "v" * 13, [top_shape, top_shape, cleaf_shape],
        pos, q6, got5, w, b, top, path_5, q_mine, got0, got1, got1_far, bl, w0, wl,
        flops=mac * n * 3,
    )
    q7 = climb(6, got6, own)
    got7 = swap(q7, 193)
    top, path, cleaf_other = call(
        "shadow_7", shadow_7, "s" + "v" * 12, [top_shape, block(rank), cleaf_shape],
        pos, got6, w, b, top, path_6, q_other, got0_other, got1_other, got1_far_other, bl, w0, wl,
        flops=mac * n * 4,
    )
    send, h = call(
        "top", top_kernel, "s" + "v" * 5, [block(eighth), block(eighth)],
        pos, got7, top, path, c2_oth, w, flops=mac * eighth * 2,
    )
    got = swap(send, 5)
    (mine,) = call(
        "own_h", own_kernel, "s" + "v" * 4, [block(eighth)],
        pos, h, send, c2, w, flops=mac * eighth,
    )
    far, far_other, mine_other = swap(mine, 3), swap(mine, 2), swap(mine, 1)
    (base_near,) = call(
        "shadow_8", shadow_8, "ss" + "v" * 6, [base_shape],
        pos, order, send, row_basis, cleaf, cleaf_other, part_0, part_1, flops=mac * n * 2,
    )
    got, base_near = lax.optimization_barrier((got, base_near))
    far_got, far_got_other = swap(got, 3), swap(got, 2)
    (base_far,) = call(
        "shadow_9", shadow_9, "ss" + "v" * 8, [base_shape],
        pos, order, got, far, far_other, row_basis, cleaf, cleaf_other, part_0, part_1, flops=mac * n * 2,
    )
    got_other = swap(got, 1)
    piece = (2, 2, size, half)
    (done,) = call(
        "near_columns", near_kernel, "ss" + "v" * 7, [(piece, BF)],
        pos, order, mine, got, mine_other, got_other, base_near, g0, g1, flops=mac * n * 2,
    )
    (out,) = call(
        "far_columns", last_kernel, "ss" + "v" * 8, [(rhs.shape, BF)],
        pos, order, far, far_got, far_other, far_got_other, base_far, g0, g1, done,
        scratch=(pltpu.VMEM(piece, BF), pltpu.SemaphoreType.DMA((4,))),
        flops=mac * n * 2, out_spec=HBM,
    )
    return out


def solution(mesh):
    return jax.shard_map(
        shards,
        mesh=mesh,
        in_specs=(
            P(None, ("leaf", "top"), None),
            P(None, ("leaf", "top"), None, None),
            P(None, ("leaf", "top"), None, None),
            P(None, ("leaf", "top"), None, None),
            P(None, ("leaf", "top"), None, None, None),
            P(None, ("leaf", "top"), None, None),
            P(None, ("leaf", "top"), None, None, None, None),
            P(None, ("leaf", "top"), None, None, None),
            P(("leaf", "top"), None),
        ),
        out_specs=P(None, ("leaf", "top"), None),
        check_vma=False,
    )
```

```python
import jax
import jax.numpy as jnp
from jax import lax
from jax.experimental import pallas as pl
from jax.experimental.pallas import tpu as pltpu
from jax.sharding import PartitionSpec as P

BF = jnp.bfloat16
F32 = jnp.float32
NN = (((1,), (0,)), ((), ()))
NT = (((1,), (1,)), ((), ()))


def dot(a, b, dims=NN):
    return lax.dot_general(a, b, dims, preferred_element_type=F32)


def widen(a):
    half = a.shape[0] // 2
    re, im = a[:half], a[half:]
    return jnp.concatenate(
        [jnp.concatenate([re, -im], axis=1), jnp.concatenate([im, re], axis=1)], axis=0
    )


def times(a, w_re, w_im):
    return dot(widen(a), jnp.concatenate([w_re, w_im], axis=0))


def times_t(a, w_re, w_im):
    return dot(widen(a), jnp.concatenate([w_re, w_im], axis=1), NT)


def rows(ref):
    return jnp.concatenate([ref[0], ref[1]], axis=0)


def put(ref, value):
    half = value.shape[0] // 2
    ref[0] = value[:half].astype(ref.dtype)
    ref[1] = value[half:].astype(ref.dtype)


def bit(pos, level):
    return (pos[0] >> level) & 1


def lift(q, w, pos, level, flip=0):
    child = bit(pos, level) ^ flip
    return times(q, w[0, level, child], w[1, level, child])


def lower(h, w, pos, level, flip=0):
    child = bit(pos, level) ^ flip
    return times_t(h, w[0, level, child], w[1, level, child])


def couple(q, b, pos, level, flip=0):
    return lax.cond(
        (bit(pos, level) ^ flip) == 0,
        lambda: times_t(q, b[0, level], b[1, level]),
        lambda: times(q, b[0, level], b[1, level]),
    )


def split(value, side, keep, send):
    half = value.shape[0] // 2
    part = half // 2
    for c in range(2):
        low = value[c * half : c * half + part]
        high = value[c * half + part : (c + 1) * half]
        keep[c] = jnp.where(side == 0, low, high)
        send[c] = jnp.where(side == 0, high, low)


def join(own, got, side):
    parts = []
    for c in range(2):
        parts.append(jnp.where(side == 0, own[c], got[c]))
        parts.append(jnp.where(side == 0, got[c], own[c]))
    return jnp.concatenate(parts, axis=0)


def side(pos, level):
    if level == 0:
        return (pos[0] ^ (pos[0] >> 1) ^ (pos[0] >> 2) ^ (pos[0] >> 4) ^ (pos[0] >> 6)) & 1
    if level == 1:
        return bit(pos, 1)
    return bit(pos, 2) ^ bit(pos, 3)


def half_lanes(half, n):
    return pl.ds(pl.multiple_of(half * n, n), n)


def parent(qleaf, wl):
    q = times(qleaf[0], wl[0, 0, 0], wl[1, 0, 0]) + times(qleaf[1], wl[0, 0, 1], wl[1, 0, 1])
    return q.astype(BF)


def send_kernel(pos, order, x, u, wl, w, qleaf, send, xt, x_v, u_v, wl_v, w0, order_s, sems):
    size = u.shape[2]
    part = x.shape[2] // 4

    def x_copy(block):
        at = pl.ds(block * size, size)
        return pltpu.make_async_copy(x.at[:, at], x_v.at[:, at], sems.at[block])

    order_copy = pltpu.make_async_copy(order, order_s, sems.at[2])
    u_copy = pltpu.make_async_copy(u, u_v, sems.at[3])
    wl_copy = pltpu.make_async_copy(wl, wl_v, sems.at[4])
    w_copy = pltpu.make_async_copy(w.at[:, 0], w0.at[:, 0], sems.at[5])
    x_copy(0).start()
    x_copy(1).start()
    order_copy.start()
    u_copy.start()
    wl_copy.start()
    w_copy.start()
    for block in range(2):
        x_copy(block).wait()
        at = pl.ds(block * size, size)
        for c in range(2):
            turned = x_v[c, at].T
            for s1 in range(2):
                for s0 in range(2):
                    here = (2 * s1 + s0) * part
                    to = (2 * c + s1) * part
                    xt[s0, block, to : to + part] = turned[here : here + part]
    order_copy.wait()
    u_copy.wait()
    share = 1 - side(pos, 0)
    for block in range(2):
        leaf = order_s[0, 0] ^ block
        qleaf[leaf] = times(xt[share, block], u_v[0, leaf], u_v[1, leaf]).astype(BF)
    wl_copy.wait()
    put(send, parent(qleaf, wl_v))
    w_copy.wait()


def keep_kernel(pos, order, xt, u, wl, w0, qleaf, keep, own):
    share = side(pos, 0)
    for block in range(2):
        leaf = order[0, 0] ^ block
        qleaf[leaf] = times(xt[share, block], u[0, leaf], u[1, leaf]).astype(BF)
    q = parent(qleaf, wl)
    put(keep, q)
    put(own, lift(q, w0, pos, 0))


def climb_kernel(level):
    def kernel(pos, got, own, w, *outs):
        q = (rows(own) + lift(rows(got), w, pos, level, 1)).astype(BF)
        if len(outs) == 2:
            split(q, side(pos, level + 1), *outs)
        else:
            put(outs[0], q)

    return kernel


def direct(order, block, x, d, out):
    size = d.shape[2]
    leaf = order[0, 0] ^ block
    at = pl.ds(block * size, size)
    xs = jnp.concatenate([x[0, at], x[1, at]], axis=0)
    re, im = d[0, leaf], d[1, leaf]
    out[0] = dot(jnp.concatenate([re, -im], axis=1), xs)
    out[1] = dot(jnp.concatenate([im, re], axis=1), xs)


def stack(w, level, child):
    return jnp.concatenate([w[0, level, child], w[1, level, child]], axis=0)


def shadow_1(pos, order, keep, w, w0, wl, x, d, own, part, paths):
    put(own, lift(rows(keep), w, pos, 1))
    for leaf in range(2):
        put(paths.at[leaf], lift(stack(wl, 0, leaf), w0, pos, 0))
    direct(order, 0, x, d, part)


def product(r, paths, leaf, out):
    put(out, times(rows(r.at[:, leaf]), paths[leaf, 0], paths[leaf, 1]))


def leaf_coupled(pos, q, got, b, bl, wl, cleaf):
    c0 = couple(rows(got), b, pos, 0).astype(BF)
    left = times_t(q[1], bl[0, 0], bl[1, 0])
    right = times(q[0], bl[0, 0], bl[1, 0])
    put(cleaf.at[0], left + times_t(c0, wl[0, 0, 0], wl[1, 0, 0]))
    put(cleaf.at[1], right + times_t(c0, wl[0, 0, 1], wl[1, 0, 1]))


def shadow_2(pos, order, keep, w, x, d, r, paths, b, bl, wl, q, got0, own, part, g, cleaf):
    put(own, lift(rows(keep), w, pos, 2))
    direct(order, 1, x, d, part)
    product(r, paths, 0, g)
    leaf_coupled(pos, q, got0, b, bl, wl, cleaf)


def shadow_3(pos, q3, w, r, paths, b, bl, wl, q, got0, own, g, cleaf):
    put(own, lift(rows(q3), w, pos, 3))
    product(r, paths, 1, g)
    leaf_coupled(pos, q, got0, b, bl, wl, cleaf)


def shares(pos, mine, other):
    a = side(pos, 0)
    half = mine.shape[0] // 2
    low = jnp.where(a == 0, mine, other)
    high = jnp.where(a == 0, other, mine)
    return jnp.concatenate([low[:half], high[:half], low[half:], high[half:]], axis=0)


def set_base(pos, order, tile, r, cleaf, cleaf_other, parts, base):
    n = base.shape[2]
    size = r.shape[2]
    part = n // 2
    at = pl.ds(pl.multiple_of(tile * part, part), part)
    lanes = half_lanes(tile, n)
    for block, direct_part in enumerate(parts):
        leaf = order[0, 0] ^ block
        h = [jnp.concatenate([c[leaf, 0, at], c[leaf, 1, at]], axis=0) for c in (cleaf, cleaf_other)]
        basis = jnp.concatenate([r[0, leaf], r[1, leaf]], axis=1)
        add = dot(basis, widen(shares(pos, *h)), NT)
        for c in range(2):
            base[c, pl.ds(block * size, size)] = (
                direct_part[c, :, lanes] + add[:, c * n : (c + 1) * n]
            )


def shadow_4(pos, order, q4, got3, w, b, r, cleaf, cleaf_other, part_0, part_1, own, top, base):
    put(own, lift(rows(q4), w, pos, 4))
    put(top, couple(rows(got3), b, pos, 3))
    set_base(pos, order, bit(pos, 1), r, cleaf, cleaf_other, (part_0, part_1), base)


def shadow_5(
    pos, order, q5, got4, w, b, top, r, cleaf, cleaf_other, part_0, part_1, own, top_out, path, base
):
    put(own, lift(rows(q5), w, pos, 5))
    c4 = couple(rows(got4), b, pos, 4).astype(BF)
    put(top_out, rows(top) + lower(c4, w, pos, 3))
    put(path, lift(stack(w, 3, bit(pos, 3)), w, pos, 4))
    set_base(pos, order, 1 - bit(pos, 1), r, cleaf, cleaf_other, (part_0, part_1), base)


def shadow_6(
    pos, q6, got5, w, b, top, path, keep2, got2, keep1, got1,
    own, top_out, path_out, c2, c2_oth, c1, c1_oth,
):
    put(own, lift(rows(q6), w, pos, 6))
    c5 = couple(rows(got5), b, pos, 5).astype(BF)
    put(top_out, rows(top) + times_t(c5, path[0], path[1]))
    put(path_out, lift(rows(path), w, pos, 5))
    put(c2, couple(rows(got2), b, pos, 2))
    put(c2_oth, couple(rows(keep2), b, pos, 2, 1))
    put(c1, couple(rows(got1), b, pos, 1))
    put(c1_oth, couple(rows(keep1), b, pos, 1, 1))


def shadow_7(pos, got6, w, b, top, path, top_out, path_out):
    c6 = couple(rows(got6), b, pos, 6).astype(BF)
    put(top_out, rows(top) + times_t(c6, path[0], path[1]))
    longer = lift(rows(path), w, pos, 6).astype(BF)
    put(path_out, couple_path(longer, b, pos))


def couple_path(path, b, pos):
    return lax.cond(
        bit(pos, 7) == 0,
        lambda: times(path, b[0, 7], b[1, 7]),
        lambda: times_t(path, b[0, 7], b[1, 7]),
    )


def top_kernel(pos, got, top, path, c_own, c_oth, w, own, send):
    h = (rows(top) + times_t(rows(got), path[0], path[1])).astype(BF)
    put(send, rows(c_oth) + lower(h, w, pos, 2, 1))
    put(own, rows(c_own) + lower(h, w, pos, 2))


def piece_kernel(other):
    def kernel(pos, h, c_own, c_oth, w, own, send):
        n = h.shape[1]
        at = pl.ds(pl.multiple_of((side(pos, 2) ^ other) * n, n), n)
        values = rows(h)
        const = jnp.concatenate([c_oth[0, at], c_oth[1, at]], axis=0)
        put(send, const + lower(values, w, pos, 1, 1))
        const = jnp.concatenate([c_own[0, at], c_own[1, at]], axis=0)
        put(own, const + lower(values, w, pos, 1))

    return kernel


def finish(pos, order, h_mine, h_other, base, gs, out):
    f = side(pos, 2)
    hw = widen(shares(pos, join(*h_mine, f), join(*h_other, f)))
    n = base.shape[2]
    for leaf, g in enumerate(gs):
        size = g.shape[1]
        at = pl.ds(pl.multiple_of((order[0, 0] ^ leaf) * size, size), size)
        add = dot(jnp.concatenate([g[0], g[1]], axis=1), hw, NT)
        for c in range(2):
            out[leaf, c] = (base[c, at] + add[:, c * n : (c + 1) * n]).astype(BF)
        yield leaf, at


def write(pos, order, tile, h_mine, h_other, base, gs, out, buf, sems):
    lanes = half_lanes(tile, base.shape[2])
    copies = []
    for leaf, at in finish(pos, order, h_mine, h_other, base, gs, buf):
        copies.append(pltpu.make_async_copy(buf.at[leaf], out.at[:, at, lanes], sems.at[leaf]))
        copies[-1].start()
    for copy in copies:
        copy.wait()


def near_kernel(pos, order, mine, got, mine_other, got_other, base, g0, g1, far, far_other, out, buf, sems):
    tile = bit(pos, 1)
    write(pos, order, tile, (mine, got), (mine_other, got_other), base, (g0, g1), out, buf, sems)


def far_kernel(pos, order, mine, got, mine_other, got_other, base, g0, g1, done, out, buf, sems):
    tile = 1 - bit(pos, 1)
    write(pos, order, tile, (mine, got), (mine_other, got_other), base, (g0, g1), out, buf, sems)


VMEM = pl.BlockSpec(memory_space=pltpu.VMEM)
SMEM = pl.BlockSpec(memory_space=pltpu.SMEM)
HBM = pl.BlockSpec(memory_space=pltpu.HBM)
GRANT = 20 * 2**20


def call(name, kernel, ins, outs, *args, scratch=(), flops=0, out_spec=VMEM, aliases=None):
    specs = {"s": SMEM, "v": VMEM, "h": HBM}
    moved = sum(a.size * a.dtype.itemsize for a in args)
    return pl.pallas_call(
        kernel,
        out_shape=[jax.ShapeDtypeStruct(shape, dtype) for shape, dtype in outs],
        in_specs=[specs[kind] for kind in ins],
        out_specs=[out_spec] * len(outs),
        scratch_shapes=list(scratch),
        input_output_aliases=aliases or {},
        compiler_params=pltpu.CompilerParams(vmem_limit_bytes=GRANT),
        cost_estimate=pl.CostEstimate(flops=flops, bytes_accessed=moved, transcendentals=0),
        name=name,
    )(*args)


def shards(rhs, diag, row_basis, col_basis, wl, bl, cross_w, cross_b, order):
    n = rhs.shape[2]
    rank = col_basis.shape[3]
    size = col_basis.shape[2]
    axes = ("leaf", "top")
    devices = lax.axis_size("leaf") * lax.axis_size("top")
    pos = lax.axis_index(axes).astype(jnp.int32).reshape(1)
    w = cross_w[:, 0]
    b = cross_b[:, 0]

    def swap(value, flip):
        return lax.ppermute(value, axes, [(i, i ^ flip) for i in range(devices)])

    def block(columns, dtype=BF):
        return ((2, columns, rank), dtype)

    mac = 8 * rank * rank
    half, quarter, eighth = n // 2, n // 4, n // 8
    qleaf_shape = ((2, n, rank), BF)
    hbm = [pltpu.with_memory_space_constraint(a, pltpu.HBM) for a in (order, rhs, col_basis, wl, w)]
    q_other, send, xt, x, u, wl, w0 = call(
        "send_half", send_kernel, "shhhhh",
        [qleaf_shape, block(half), ((2, 2, n, size), BF), (rhs.shape, BF), (col_basis.shape, BF),
         (wl.shape, BF), ((2, 1, 2, rank, rank), BF)],
        pos, *hbm,
        scratch=(pltpu.SMEM(order.shape, jnp.int32), pltpu.SemaphoreType.DMA((6,))),
        flops=mac * n * 3,
    )
    got0 = swap(send, 1)
    q_mine, keep0, own = call(
        "keep_half", keep_kernel, "ssvvvv", [qleaf_shape, block(half), block(half, F32)],
        pos, order, xt, u, wl, w0, flops=mac * n * 3,
    )
    got0_other = swap(keep0, 1)
    keep1, send = call(
        "climb_0", climb_kernel(0), "svvv", [block(quarter), block(quarter)],
        pos, got0, own, w0, flops=mac * half,
    )
    got1 = swap(send, 3)
    own, part_0, paths = call(
        "shadow_1", shadow_1, "ss" + "v" * 6,
        [block(quarter, F32), ((2, size, n), F32), ((2, 2, rank, rank), BF)],
        pos, order, keep1, w, w0, wl, x, diag, flops=mac * n * 8,
    )
    keep2, send = call(
        "climb_1", climb_kernel(1), "svvv", [block(eighth), block(eighth)],
        pos, got1, own, w, flops=mac * quarter,
    )
    got2 = swap(send, 5)
    cleaf_shape = ((2, 2, half, rank), BF)
    own, part_1, g0, cleaf = call(
        "shadow_2", shadow_2, "ss" + "v" * 11,
        [block(eighth, F32), ((2, size, n), F32), block(size), cleaf_shape],
        pos, order, keep2, w, x, diag, row_basis, paths, b, bl, wl, q_mine, got0,
        flops=mac * n * 9,
    )

    def climb(level, got, own):
        return call(
            "climb_%d" % level, climb_kernel(level), "svvv", [block(eighth)],
            pos, got, own, w, flops=mac * eighth,
        )[0]

    top_shape = block(eighth, F32)
    base_shape = ((2, 2 * size, half), F32)
    q3 = climb(2, got2, own)
    got3 = swap(q3, 13)
    own, g1, cleaf_other = call(
        "shadow_3", shadow_3, "s" + "v" * 9, [top_shape, block(size), cleaf_shape],
        pos, q3, w, row_basis, paths, b, bl, wl, q_other, got0_other, flops=mac * n * 5,
    )
    q4 = climb(3, got3, own)
    got4 = swap(q4, 17)
    own, top, base_near = call(
        "shadow_4", shadow_4, "ss" + "v" * 9, [top_shape, top_shape, base_shape],
        pos, order, q4, got3, w, b, row_basis, cleaf, cleaf_other, part_0, part_1,
        flops=mac * n * 2,
    )
    q5 = climb(4, got4, own)
    got5 = swap(q5, 49)
    own, top, path, base_far = call(
        "shadow_5", shadow_5, "ss" + "v" * 10, [top_shape, top_shape, block(rank), base_shape],
        pos, order, q5, got4, w, b, top, row_basis, cleaf, cleaf_other, part_0, part_1,
        flops=mac * n * 3,
    )
    q6 = climb(5, got5, own)
    got6 = swap(q6, 65)
    own, top, path, c2, c2_oth, c1, c1_oth = call(
        "shadow_6", shadow_6, "s" + "v" * 10,
        [top_shape, top_shape, block(rank), top_shape, top_shape, block(quarter, F32), block(quarter, F32)],
        pos, q6, got5, w, b, top, path, keep2, got2, keep1, got1, flops=mac * n * 2,
    )
    q7 = climb(6, got6, own)
    got7 = swap(q7, 193)
    top, path = call(
        "shadow_7", shadow_7, "s" + "v" * 5, [top_shape, block(rank)],
        pos, got6, w, b, top, path, flops=mac * n * 2,
    )
    mine, send = call(
        "top", top_kernel, "s" + "v" * 6, [block(eighth), block(eighth)],
        pos, got7, top, path, c2, c2_oth, w, flops=mac * eighth * 3,
    )
    got = swap(send, 5)

    def piece(name, other, h):
        own, send = call(
            name, piece_kernel(other), "s" + "v" * 4, [block(eighth), block(eighth)],
            pos, h, c1, c1_oth, w, flops=mac * eighth * 2,
        )
        return own, swap(send, 3), swap(send, 2), swap(own, 1)

    near_a, far_a, far_a_other, near_a_other = piece("first_piece", 0, mine)
    near_b, far_b, far_b_other, near_b_other = piece("second_piece", 1, got)
    scratch = (pltpu.VMEM((2, 2, size, half), BF), pltpu.SemaphoreType.DMA((2,)))
    (done,) = call(
        "near_columns", near_kernel, "ss" + "v" * 9, [(rhs.shape, BF)],
        pos, order, near_a, near_b, near_a_other, near_b_other, base_near, g0, g1, far_a, far_a_other,
        scratch=scratch, flops=mac * n * 2, out_spec=HBM,
    )
    (out,) = call(
        "far_columns", far_kernel, "ss" + "v" * 7 + "h", [(rhs.shape, BF)],
        pos, order, far_a, far_b, far_a_other, far_b_other, base_far, g0, g1, done,
        scratch=scratch, flops=mac * n * 2, out_spec=HBM, aliases={9: 0},
    )
    return out


def solution(mesh):
    return jax.shard_map(
        shards,
        mesh=mesh,
        in_specs=(
            P(None, ("leaf", "top"), None),
            P(None, ("leaf", "top"), None, None),
            P(None, ("leaf", "top"), None, None),
            P(None, ("leaf", "top"), None, None),
            P(None, ("leaf", "top"), None, None, None),
            P(None, ("leaf", "top"), None, None),
            P(None, ("leaf", "top"), None, None, None, None),
            P(None, ("leaf", "top"), None, None, None),
            P(("leaf", "top"), None),
        ),
        out_specs=P(None, ("leaf", "top"), None),
        check_vma=False,
    )
```

```python
import jax
import jax.numpy as jnp
from jax import lax
from jax.experimental import pallas as pl
from jax.experimental.pallas import tpu as pltpu
from jax.sharding import PartitionSpec as P

BF = jnp.bfloat16
F32 = jnp.float32
NN = (((1,), (0,)), ((), ()))
NT = (((1,), (1,)), ((), ()))


def dot(a, b, dims=NN):
    return lax.dot_general(a, b, dims, preferred_element_type=F32)


def widen(a):
    half = a.shape[0] // 2
    re, im = a[:half], a[half:]
    return jnp.concatenate(
        [jnp.concatenate([re, -im], axis=1), jnp.concatenate([im, re], axis=1)], axis=0
    )


def times(a, w_re, w_im):
    return dot(widen(a), jnp.concatenate([w_re, w_im], axis=0))


def times_t(a, w_re, w_im):
    return dot(widen(a), jnp.concatenate([w_re, w_im], axis=1), NT)


def rows(ref):
    return jnp.concatenate([ref[0], ref[1]], axis=0)


def put(ref, value):
    half = value.shape[0] // 2
    ref[0] = value[:half].astype(ref.dtype)
    ref[1] = value[half:].astype(ref.dtype)


def bit(pos, level):
    return (pos[0] >> level) & 1


def lift(q, w, pos, level, flip=0):
    child = bit(pos, level) ^ flip
    return times(q, w[0, level, child], w[1, level, child])


def lower(h, w, pos, level, flip=0):
    child = bit(pos, level) ^ flip
    return times_t(h, w[0, level, child], w[1, level, child])


def couple(q, b, pos, level, flip=0):
    return lax.cond(
        (bit(pos, level) ^ flip) == 0,
        lambda: times_t(q, b[0, level], b[1, level]),
        lambda: times(q, b[0, level], b[1, level]),
    )


def split(value, side, keep, send):
    half = value.shape[0] // 2
    part = half // 2
    for c in range(2):
        low = value[c * half : c * half + part]
        high = value[c * half + part : (c + 1) * half]
        keep[c] = jnp.where(side == 0, low, high)
        send[c] = jnp.where(side == 0, high, low)


def join(own, got, side):
    parts = []
    for c in range(2):
        parts.append(jnp.where(side == 0, own[c], got[c]))
        parts.append(jnp.where(side == 0, got[c], own[c]))
    return jnp.concatenate(parts, axis=0)


def side(pos, level):
    if level == 0:
        return (pos[0] ^ (pos[0] >> 1) ^ (pos[0] >> 2) ^ (pos[0] >> 4) ^ (pos[0] >> 6)) & 1
    if level == 1:
        return bit(pos, 1)
    return bit(pos, 2) ^ bit(pos, 3)


def half_lanes(half, n):
    return pl.ds(pl.multiple_of(half * n, n), n)


def parent(qleaf, wl):
    q = times(qleaf[0], wl[0, 0, 0], wl[1, 0, 0]) + times(qleaf[1], wl[0, 0, 1], wl[1, 0, 1])
    return q.astype(BF)


def send_kernel(pos, order, x, u, wl, w, qleaf, send, xt, x_v, u_v, wl_v, w0, order_s, xs, sems):
    size = u.shape[2]
    half = x.shape[2] // 2

    def x_copy(block):
        at = pl.ds(block * size, size)
        return pltpu.make_async_copy(x.at[:, at], x_v.at[:, at], sems.at[block])

    def u_copy(leaf):
        return pltpu.make_async_copy(u.at[:, leaf], u_v.at[:, leaf], sems.at[2 + leaf])

    order_copy = pltpu.make_async_copy(order, order_s, sems.at[4])
    wl_copy = pltpu.make_async_copy(wl, wl_v, sems.at[5])
    w_copy = pltpu.make_async_copy(w.at[:, 0], w0.at[:, 0], sems.at[6])
    x_copy(0).start()
    x_copy(1).start()
    order_copy.start()
    u_copy(0).start()
    u_copy(1).start()
    wl_copy.start()
    w_copy.start()
    keep = side(pos, 0)
    for block in range(2):
        x_copy(block).wait()
        at = pl.ds(block * size, size)
        for out, which in ((xs, 1 - keep), (xt, keep)):
            lanes = half_lanes(which, half)
            out[block, :half] = x_v[0, at, lanes].T
            out[block, half:] = x_v[1, at, lanes].T
    order_copy.wait()
    for leaf in range(2):
        u_copy(leaf).wait()
        block = order_s[0, leaf]
        qleaf[leaf] = times(xs[block], u_v[0, leaf], u_v[1, leaf]).astype(BF)
    wl_copy.wait()
    put(send, parent(qleaf, wl_v))
    w_copy.wait()


def keep_kernel(pos, order, xt, u, wl, qleaf, keep):
    for leaf in range(2):
        block = order[0, leaf]
        qleaf[leaf] = times(xt[block], u[0, leaf], u[1, leaf]).astype(BF)
    put(keep, parent(qleaf, wl))


def first_climb(pos, got, q, w, keep, send):
    c = bit(pos, 0)
    pair = jnp.concatenate([widen(rows(q)), widen(rows(got))], axis=1)
    mats = jnp.concatenate([w[0, 0, c], w[1, 0, c], w[0, 0, 1 - c], w[1, 0, 1 - c]], axis=0)
    split(dot(pair, mats).astype(BF), side(pos, 1), keep, send)


def climb_kernel(level):
    def kernel(pos, got, own, w, out):
        put(out, rows(own) + lift(rows(got), w, pos, level, 1))

    return kernel


def direct(order, block, x, d, out):
    size = d.shape[2]
    leaf = order[0, 0] ^ block
    at = pl.ds(block * size, size)
    xs = jnp.concatenate([x[0, at], x[1, at]], axis=0)
    re, im = d[0, leaf], d[1, leaf]
    out[0] = dot(jnp.concatenate([re, -im], axis=1), xs)
    out[1] = dot(jnp.concatenate([im, re], axis=1), xs)


def stack(w, level, child):
    return jnp.concatenate([w[0, level, child], w[1, level, child]], axis=0)


def shadow_1(pos, order, keep, w, w0, wl, x, d, own, part, paths):
    put(own, lift(rows(keep), w, pos, 1))
    for leaf in range(2):
        put(paths.at[leaf], lift(stack(wl, 0, leaf), w0, pos, 0))
    direct(order, 0, x, d, part)


def leaf_coupled(pos, q, got, b, bl, wl, cleaf):
    c0 = couple(rows(got), b, pos, 0).astype(BF)
    left = times_t(q[1], bl[0, 0], bl[1, 0])
    right = times(q[0], bl[0, 0], bl[1, 0])
    cleaf[0] = (left + times_t(c0, wl[0, 0, 0], wl[1, 0, 0])).astype(BF)
    cleaf[1] = (right + times_t(c0, wl[0, 0, 1], wl[1, 0, 1])).astype(BF)


def shadow_2(pos, order, keep, w, x, d, b, bl, wl, q_mine, got0, own, part, cleaf):
    put(own, lift(rows(keep), w, pos, 2))
    direct(order, 1, x, d, part)
    leaf_coupled(pos, q_mine, got0, b, bl, wl, cleaf)


def shadow_3(pos, q3, w, b, bl, wl, q_other, got0_other, own, cleaf):
    put(own, lift(rows(q3), w, pos, 3))
    leaf_coupled(pos, q_other, got0_other, b, bl, wl, cleaf)


def set_base(pos, order, part, r, cleaf, parts, base):
    n = base.shape[2]
    size = r.shape[2]
    first = order[0, 0]
    lanes = half_lanes(side(pos, 0) ^ part, n)
    for block, direct_part in enumerate(parts):
        leaf = first ^ block
        add = dot(jnp.concatenate([r[0, leaf], r[1, leaf]], axis=1), widen(cleaf[leaf]), NT)
        for c in range(2):
            base[c, pl.ds(block * size, size)] = (
                direct_part[c, :, lanes] + add[:, c * n : (c + 1) * n]
            )


def shadow_4(pos, order, q4, got3, w, b, r, cleaf, part_0, part_1, own, top, base):
    put(own, lift(rows(q4), w, pos, 4))
    put(top, couple(rows(got3), b, pos, 3))
    set_base(pos, order, 0, r, cleaf, (part_0, part_1), base)


def product(r, paths, leaf, out):
    put(out, times(rows(r.at[:, leaf]), paths[leaf, 0], paths[leaf, 1]))


def shadow_5(pos, q5, got4, w, b, r, paths, top, keep1, got1, own, top_out, path, g, c1, c1_oth):
    put(own, lift(rows(q5), w, pos, 5))
    c4 = couple(rows(got4), b, pos, 4).astype(BF)
    put(top_out, rows(top) + lower(c4, w, pos, 3))
    put(path, lift(stack(w, 3, bit(pos, 3)), w, pos, 4))
    product(r, paths, 0, g)
    put(c1, couple(rows(got1), b, pos, 1))
    put(c1_oth, couple(rows(keep1), b, pos, 1, 1))


def shadow_6(pos, q6, got5, w, b, r, paths, top, path, own, top_out, path_6, path_7, g):
    put(own, lift(rows(q6), w, pos, 6))
    c5 = couple(rows(got5), b, pos, 5).astype(BF)
    put(top_out, rows(top) + times_t(c5, path[0], path[1]))
    longer = lift(rows(path), w, pos, 5).astype(BF)
    put(path_6, longer)
    put(path_7, lift(longer, w, pos, 6))
    product(r, paths, 1, g)


def shadow_7(pos, got6, w, b, top, path_6, path_7, got2, const, path_out):
    c6 = couple(rows(got6), b, pos, 6).astype(BF)
    h = (rows(top) + times_t(c6, path_6[0], path_6[1])).astype(BF)
    put(const, couple(rows(got2), b, pos, 2) + lower(h, w, pos, 2))
    path = couple_path(rows(path_7), b, pos).astype(BF)
    half = path.shape[0] // 2
    put(path_out, times(stack(w, 2, bit(pos, 2)), path[:half], path[half:]))


def couple_path(path, b, pos):
    return lax.cond(
        bit(pos, 7) == 0,
        lambda: times(path, b[0, 7], b[1, 7]),
        lambda: times_t(path, b[0, 7], b[1, 7]),
    )


def top_kernel(pos, got, const, path, c_own, c_oth, w, own, send):
    h = (rows(const) + times_t(rows(got), path[0], path[1])).astype(BF)
    put(send, rows(c_oth) + lower(h, w, pos, 1, 1))
    put(own, rows(c_own) + lower(h, w, pos, 1))


def shadow_9(pos, order, mine, r, cleaf, part_0, part_1, base):
    set_base(pos, order, 1, r, cleaf, (part_0, part_1), base)


def finish(pos, order, mine, got, base, gs, out, tile):
    hw = widen(join(mine, got, side(pos, 1)))
    n = base.shape[2]
    for leaf, g in enumerate(gs):
        size = g.shape[1]
        for step in range(size // tile):
            here = pl.ds(step * tile, tile)
            start = (order[0, 0] ^ leaf) * size + step * tile
            at = pl.ds(pl.multiple_of(start, tile), tile)
            add = dot(jnp.concatenate([g[0, here], g[1, here]], axis=1), hw, NT)
            for c in range(2):
                out[leaf, c, here] = (base[c, at] + add[:, c * n : (c + 1) * n]).astype(BF)
            yield leaf, here, at


def own_kernel(pos, order, mine, got, base, g0, g1, out):
    for _ in finish(pos, order, mine, got, base, (g0, g1), out, g0.shape[1]):
        pass


def last_kernel(pos, order, mine, got, base, g0, g1, done, out, buf, sems):
    size = g0.shape[1]
    n = base.shape[2]
    copies = []

    def store(src, part, at):
        lanes = half_lanes(side(pos, 0) ^ part, n)
        sem = sems.at[len(copies)]
        copies.append(pltpu.make_async_copy(src, out.at[:, at, lanes], sem))
        copies[-1].start()

    for leaf in range(2):
        at = pl.ds(pl.multiple_of((order[0, 0] ^ leaf) * size, size), size)
        store(done.at[leaf], 0, at)
    for leaf, here, at in finish(pos, order, mine, got, base, (g0, g1), buf, size):
        store(buf.at[leaf, :, here], 1, at)
    for copy in copies:
        copy.wait()


VMEM = pl.BlockSpec(memory_space=pltpu.VMEM)
SMEM = pl.BlockSpec(memory_space=pltpu.SMEM)
HBM = pl.BlockSpec(memory_space=pltpu.HBM)
GRANT = 20 * 2**20


def call(name, kernel, ins, outs, *args, scratch=(), flops=0, out_spec=VMEM):
    specs = {"s": SMEM, "v": VMEM, "h": HBM}
    moved = sum(a.size * a.dtype.itemsize for a in args)
    return pl.pallas_call(
        kernel,
        out_shape=[jax.ShapeDtypeStruct(shape, dtype) for shape, dtype in outs],
        in_specs=[specs[kind] for kind in ins],
        out_specs=[out_spec] * len(outs),
        scratch_shapes=list(scratch),
        compiler_params=pltpu.CompilerParams(vmem_limit_bytes=GRANT),
        cost_estimate=pl.CostEstimate(flops=flops, bytes_accessed=moved, transcendentals=0),
        name=name,
    )(*args)


def shards(rhs, diag, row_basis, col_basis, wl, bl, cross_w, cross_b, order):
    n = rhs.shape[2]
    rank = col_basis.shape[3]
    size = col_basis.shape[2]
    axes = ("leaf", "top")
    devices = lax.axis_size("leaf") * lax.axis_size("top")
    pos = lax.axis_index(axes).astype(jnp.int32).reshape(1)
    w = cross_w[:, 0]
    b = cross_b[:, 0]

    def swap(value, flip):
        return lax.ppermute(value, axes, [(i, i ^ flip) for i in range(devices)])

    def block(columns, dtype=BF):
        return ((2, columns, rank), dtype)

    mac = 8 * rank * rank
    half, quarter = n // 2, n // 4
    qleaf_shape = ((2, n, rank), BF)
    hbm = [pltpu.with_memory_space_constraint(a, pltpu.HBM) for a in (order, rhs, col_basis, wl, w)]
    q_other, send, xt, x, u, wl, w0 = call(
        "send_half", send_kernel, "shhhhh",
        [qleaf_shape, block(half), ((2, n, size), BF), (rhs.shape, BF), (col_basis.shape, BF),
         (wl.shape, BF), ((2, 1, 2, rank, rank), BF)],
        pos, *hbm,
        scratch=(
            pltpu.SMEM(order.shape, jnp.int32),
            pltpu.VMEM((2, n, size), BF),
            pltpu.SemaphoreType.DMA((7,)),
        ),
        flops=mac * n * 3,
    )
    got0 = swap(send, 1)
    q_mine, keep0 = call(
        "keep_half", keep_kernel, "ssvvv", [qleaf_shape, block(half)],
        pos, order, xt, u, wl, flops=mac * n * 3,
    )
    keep1, send = call(
        "climb_0", first_climb, "svvv", [block(quarter), block(quarter)],
        pos, got0, keep0, w0, flops=mac * n,
    )
    got1 = swap(send, 3)
    keep0, keep1 = lax.optimization_barrier((keep0, keep1))
    got0_other = swap(keep0, 1)
    own, part_0, paths = call(
        "shadow_1", shadow_1, "ss" + "v" * 6,
        [block(quarter, F32), ((2, size, n), F32), ((2, 2, rank, rank), BF)],
        pos, order, keep1, w, w0, wl, x, diag, flops=mac * n * 7,
    )

    def climb(level, got, own):
        return call(
            "climb_%d" % level, climb_kernel(level), "svvv", [block(quarter)],
            pos, got, own, w, flops=mac * quarter,
        )[0]

    q2 = climb(1, got1, own)
    got2 = swap(q2, 5)
    cleaf_shape = ((2, n, rank), BF)
    top_shape = block(quarter, F32)
    own, part_1, cleaf = call(
        "shadow_2", shadow_2, "ss" + "v" * 9, [top_shape, ((2, size, n), F32), cleaf_shape],
        pos, order, q2, w, x, diag, b, bl, wl, q_mine, got0, flops=mac * n * 8,
    )
    base_shape = ((2, 2 * size, half), F32)
    q3 = climb(2, got2, own)
    got3 = swap(q3, 13)
    own, cleaf_other = call(
        "shadow_3", shadow_3, "s" + "v" * 7, [top_shape, cleaf_shape],
        pos, q3, w, b, bl, wl, q_other, got0_other, flops=mac * n * 4,
    )
    q4 = climb(3, got3, own)
    got4 = swap(q4, 17)
    own, top, base = call(
        "shadow_4", shadow_4, "ss" + "v" * 8,
        [top_shape, top_shape, base_shape],
        pos, order, q4, got3, w, b, row_basis, cleaf, part_0, part_1, flops=mac * n * 2,
    )
    q5 = climb(4, got4, own)
    got5 = swap(q5, 49)
    own, top, path, g0, c1, c1_oth = call(
        "shadow_5", shadow_5, "s" + "v" * 9,
        [top_shape, top_shape, block(rank), block(size), top_shape, top_shape],
        pos, q5, got4, w, b, row_basis, paths, top, keep1, got1, flops=mac * n * 3,
    )
    q6 = climb(5, got5, own)
    got6 = swap(q6, 65)
    own, top, path_6, path_7, g1 = call(
        "shadow_6", shadow_6, "s" + "v" * 8,
        [top_shape, top_shape, block(rank), block(rank), block(size)],
        pos, q6, got5, w, b, row_basis, paths, top, path, flops=mac * n * 3,
    )
    q7 = climb(6, got6, own)
    got7 = swap(q7, 193)
    const, path = call(
        "shadow_7", shadow_7, "s" + "v" * 7, [top_shape, block(rank)],
        pos, got6, w, b, top, path_6, path_7, got2, flops=mac * n * 2,
    )
    mine, send = call(
        "top", top_kernel, "s" + "v" * 6, [block(quarter), block(quarter)],
        pos, got7, const, path, c1, c1_oth, w, flops=mac * quarter * 3,
    )
    got = swap(send, 3)
    (base_other,) = call(
        "shadow_9", shadow_9, "ss" + "v" * 5, [base_shape],
        pos, order, mine, row_basis, cleaf_other, part_0, part_1, flops=mac * n * 2,
    )
    late, base_other = lax.optimization_barrier((mine, base_other))
    mine_other = swap(late, 1)
    got_other = swap(got, 1)
    piece = (2, 2, size, half)
    (done,) = call(
        "own_columns", own_kernel, "ss" + "v" * 5, [(piece, BF)],
        pos, order, mine, got, base, g0, g1, flops=mac * n * 2,
    )
    (out,) = call(
        "other_columns", last_kernel, "ss" + "v" * 6, [(rhs.shape, BF)],
        pos, order, mine_other, got_other, base_other, g0, g1, done,
        scratch=(pltpu.VMEM(piece, BF), pltpu.SemaphoreType.DMA((6,))),
        flops=mac * n * 2, out_spec=HBM,
    )
    return out


def solution(mesh):
    return jax.shard_map(
        shards,
        mesh=mesh,
        in_specs=(
            P(None, ("leaf", "top"), None),
            P(None, ("leaf", "top"), None, None),
            P(None, ("leaf", "top"), None, None),
            P(None, ("leaf", "top"), None, None),
            P(None, ("leaf", "top"), None, None, None),
            P(None, ("leaf", "top"), None, None),
            P(None, ("leaf", "top"), None, None, None, None),
            P(None, ("leaf", "top"), None, None, None),
            P(("leaf", "top"), None),
        ),
        out_specs=P(None, ("leaf", "top"), None),
        check_vma=False,
    )
```

```python
import jax
import jax.numpy as jnp
from jax import lax
from jax.experimental import pallas as pl
from jax.experimental.pallas import tpu as pltpu
from jax.sharding import PartitionSpec as P

BF = jnp.bfloat16
F32 = jnp.float32
NN = (((1,), (0,)), ((), ()))
NT = (((1,), (1,)), ((), ()))


def dot(a, b, dims=NN):
    return lax.dot_general(a, b, dims, preferred_element_type=F32)


def widen(a):
    half = a.shape[0] // 2
    re, im = a[:half], a[half:]
    return jnp.concatenate(
        [jnp.concatenate([re, -im], axis=1), jnp.concatenate([im, re], axis=1)], axis=0
    )


def times(a, w_re, w_im):
    return dot(widen(a), jnp.concatenate([w_re, w_im], axis=0))


def times_t(a, w_re, w_im):
    return dot(widen(a), jnp.concatenate([w_re, w_im], axis=1), NT)


def rows(ref):
    return jnp.concatenate([ref[0], ref[1]], axis=0)


def put(ref, value):
    half = value.shape[0] // 2
    ref[0] = value[:half].astype(ref.dtype)
    ref[1] = value[half:].astype(ref.dtype)


def bit(pos, level):
    return (pos[0] >> level) & 1


def lift(q, w, pos, level, flip=0):
    child = bit(pos, level) ^ flip
    return times(q, w[0, level, child], w[1, level, child])


def lower(h, w, pos, level, flip=0):
    child = bit(pos, level) ^ flip
    return times_t(h, w[0, level, child], w[1, level, child])


def couple(q, b, pos, level, flip=0):
    return lax.cond(
        (bit(pos, level) ^ flip) == 0,
        lambda: times_t(q, b[0, level], b[1, level]),
        lambda: times(q, b[0, level], b[1, level]),
    )


def split(value, side, keep, send):
    half = value.shape[0] // 2
    part = half // 2
    for c in range(2):
        low = value[c * half : c * half + part]
        high = value[c * half + part : (c + 1) * half]
        keep[c] = jnp.where(side == 0, low, high)
        send[c] = jnp.where(side == 0, high, low)


def join(own, got, side):
    parts = []
    for c in range(2):
        parts.append(jnp.where(side == 0, own[c], got[c]))
        parts.append(jnp.where(side == 0, got[c], own[c]))
    return jnp.concatenate(parts, axis=0)


def side(pos, level):
    if level == 0:
        return (pos[0] ^ (pos[0] >> 1) ^ (pos[0] >> 2) ^ (pos[0] >> 4) ^ (pos[0] >> 6)) & 1
    if level == 1:
        return bit(pos, 1)
    return bit(pos, 2) ^ bit(pos, 3)


def half_lanes(half, n):
    return pl.ds(pl.multiple_of(half * n, n), n)


def parent(qleaf, wl):
    pair = jnp.concatenate([widen(qleaf[0]), widen(qleaf[1])], axis=1)
    mats = jnp.concatenate([wl[0, 0, 0], wl[1, 0, 0], wl[0, 0, 1], wl[1, 0, 1]], axis=0)
    return dot(pair, mats).astype(BF)


def send_kernel(pos, order, x, u, wl, w, qleaf, send, xt, x_v, u_v, wl_v, w0, order_s, xs, sems):
    size = u.shape[2]
    half = x.shape[2] // 2

    def x_copy(block):
        at = pl.ds(block * size, size)
        return pltpu.make_async_copy(x.at[:, at], x_v.at[:, at], sems.at[block])

    def u_copy(leaf):
        return pltpu.make_async_copy(u.at[:, leaf], u_v.at[:, leaf], sems.at[2 + leaf])

    order_copy = pltpu.make_async_copy(order, order_s, sems.at[4])
    wl_copy = pltpu.make_async_copy(wl, wl_v, sems.at[5])
    w_copy = pltpu.make_async_copy(w.at[:, 0], w0.at[:, 0], sems.at[6])
    x_copy(0).start()
    x_copy(1).start()
    order_copy.start()
    u_copy(0).start()
    u_copy(1).start()
    wl_copy.start()
    w_copy.start()
    keep = side(pos, 0)
    for block in range(2):
        x_copy(block).wait()
        at = pl.ds(block * size, size)
        for out, which in ((xs, 1 - keep), (xt, keep)):
            lanes = half_lanes(which, half)
            out[block, :half] = x_v[0, at, lanes].T
            out[block, half:] = x_v[1, at, lanes].T
    order_copy.wait()
    for leaf in range(2):
        u_copy(leaf).wait()
        block = order_s[0, leaf]
        qleaf[leaf] = times(xs[block], u_v[0, leaf], u_v[1, leaf]).astype(BF)
    wl_copy.wait()
    put(send, parent(qleaf, wl_v))
    w_copy.wait()


def keep_kernel(pos, order, xt, u, wl, qleaf, keep):
    for leaf in range(2):
        block = order[0, leaf]
        qleaf[leaf] = times(xt[block], u[0, leaf], u[1, leaf]).astype(BF)
    put(keep, parent(qleaf, wl))


def first_climb(pos, got, q, w, keep, send):
    c = bit(pos, 0)
    pair = jnp.concatenate([widen(rows(q)), widen(rows(got))], axis=1)
    mats = jnp.concatenate([w[0, 0, c], w[1, 0, c], w[0, 0, 1 - c], w[1, 0, 1 - c]], axis=0)
    split(dot(pair, mats).astype(BF), side(pos, 1), keep, send)


def climb_kernel(level):
    def kernel(pos, got, own, w, *outs):
        q = (rows(own) + lift(rows(got), w, pos, level, 1)).astype(BF)
        if len(outs) == 2:
            split(q, side(pos, level + 1), *outs)
        else:
            put(outs[0], q)

    return kernel


def direct(order, block, x, d, out):
    size = d.shape[2]
    leaf = order[0, 0] ^ block
    at = pl.ds(block * size, size)
    xs = jnp.concatenate([x[0, at], x[1, at]], axis=0)
    re, im = d[0, leaf], d[1, leaf]
    out[0] = dot(jnp.concatenate([re, -im], axis=1), xs)
    out[1] = dot(jnp.concatenate([im, re], axis=1), xs)


def stack(w, level, child):
    return jnp.concatenate([w[0, level, child], w[1, level, child]], axis=0)


def shadow_1(pos, order, keep, w, w0, wl, x, d, own, part, paths):
    put(own, lift(rows(keep), w, pos, 1))
    for leaf in range(2):
        put(paths.at[leaf], lift(stack(wl, 0, leaf), w0, pos, 0))
    direct(order, 0, x, d, part)


def leaf_coupled(pos, q, got, b, bl, wl, cleaf):
    c0 = couple(rows(got), b, pos, 0).astype(BF)
    left = times_t(q[1], bl[0, 0], bl[1, 0])
    right = times(q[0], bl[0, 0], bl[1, 0])
    cleaf[0] = (left + times_t(c0, wl[0, 0, 0], wl[1, 0, 0])).astype(BF)
    cleaf[1] = (right + times_t(c0, wl[0, 0, 1], wl[1, 0, 1])).astype(BF)


def shadow_2(pos, order, keep, w, x, d, b, bl, wl, q_mine, got0, own, part, cleaf):
    put(own, lift(rows(keep), w, pos, 2))
    direct(order, 1, x, d, part)
    leaf_coupled(pos, q_mine, got0, b, bl, wl, cleaf)


def shadow_3(pos, q3, w, b, bl, wl, q_other, got0_other, own, cleaf):
    put(own, lift(rows(q3), w, pos, 3))
    leaf_coupled(pos, q_other, got0_other, b, bl, wl, cleaf)


def set_base(pos, order, part, r, cleaf, parts, base):
    n = base.shape[2]
    size = r.shape[2]
    first = order[0, 0]
    lanes = half_lanes(side(pos, 0) ^ part, n)
    for block, direct_part in enumerate(parts):
        leaf = first ^ block
        add = dot(jnp.concatenate([r[0, leaf], r[1, leaf]], axis=1), widen(cleaf[leaf]), NT)
        for c in range(2):
            base[c, pl.ds(block * size, size)] = (
                direct_part[c, :, lanes] + add[:, c * n : (c + 1) * n]
            )


def shadow_4(pos, order, q4, got3, w, b, r, cleaf, part_0, part_1, own, top, base):
    put(own, lift(rows(q4), w, pos, 4))
    put(top, couple(rows(got3), b, pos, 3))
    set_base(pos, order, 0, r, cleaf, (part_0, part_1), base)


def product(r, paths, leaf, out):
    put(out, times(rows(r.at[:, leaf]), paths[leaf, 0], paths[leaf, 1]))


def shadow_5(pos, q5, got4, w, b, r, paths, top, own, top_out, path, g):
    put(own, lift(rows(q5), w, pos, 5))
    c4 = couple(rows(got4), b, pos, 4).astype(BF)
    put(top_out, rows(top) + lower(c4, w, pos, 3))
    put(path, lift(stack(w, 3, bit(pos, 3)), w, pos, 4))
    product(r, paths, 0, g)


def shadow_6(pos, q6, got5, w, b, r, paths, top, path, own, top_out, path_6, path_8, g):
    put(own, lift(rows(q6), w, pos, 6))
    c5 = couple(rows(got5), b, pos, 5).astype(BF)
    put(top_out, rows(top) + times_t(c5, path[0], path[1]))
    longer = lift(rows(path), w, pos, 5).astype(BF)
    put(path_6, longer)
    put(path_8, couple_path(lift(longer, w, pos, 6).astype(BF), b, pos))
    product(r, paths, 1, g)


def shadow_7(pos, got6, w, b, top, path_6, path_8, keep2, got2, const, const_oth, path, path_oth):
    c6 = couple(rows(got6), b, pos, 6).astype(BF)
    h = (rows(top) + times_t(c6, path_6[0], path_6[1])).astype(BF)
    put(const, couple(rows(got2), b, pos, 2) + lower(h, w, pos, 2))
    put(const_oth, couple(rows(keep2), b, pos, 2, 1) + lower(h, w, pos, 2, 1))
    for flip, out in enumerate((path, path_oth)):
        put(out, times(stack(w, 2, bit(pos, 2) ^ flip), path_8[0], path_8[1]))


def couple_path(path, b, pos):
    return lax.cond(
        bit(pos, 7) == 0,
        lambda: times(path, b[0, 7], b[1, 7]),
        lambda: times_t(path, b[0, 7], b[1, 7]),
    )


def top_kernel(pos, got, const, const_oth, path, path_oth, own, send):
    q = widen(rows(got))
    put(send, rows(const_oth) + dot(q, jnp.concatenate([path_oth[0], path_oth[1]], axis=1), NT))
    put(own, rows(const) + dot(q, jnp.concatenate([path[0], path[1]], axis=1), NT))


def shadow_8(pos, mine, keep1, got1, b, c1, c1_oth):
    put(c1, couple(rows(got1), b, pos, 1))
    put(c1_oth, couple(rows(keep1), b, pos, 1, 1))


def down_kernel(pos, mine, got, c_own, c_oth, w, own, send):
    h = join(mine, got, side(pos, 2))
    put(send, rows(c_oth) + lower(h, w, pos, 1, 1))
    put(own, rows(c_own) + lower(h, w, pos, 1))


def shadow_9(pos, order, mine, r, cleaf, part_0, part_1, base):
    set_base(pos, order, 1, r, cleaf, (part_0, part_1), base)


def finish(pos, order, mine, got, base, gs, out, tile):
    hw = widen(join(mine, got, side(pos, 1)))
    n = base.shape[2]
    for leaf, g in enumerate(gs):
        size = g.shape[1]
        for step in range(size // tile):
            here = pl.ds(step * tile, tile)
            start = (order[0, 0] ^ leaf) * size + step * tile
            at = pl.ds(pl.multiple_of(start, tile), tile)
            add = dot(jnp.concatenate([g[0, here], g[1, here]], axis=1), hw, NT)
            for c in range(2):
                out[leaf, c, here] = (base[c, at] + add[:, c * n : (c + 1) * n]).astype(BF)
            yield leaf, here, at


def own_kernel(pos, order, mine, got, base, g0, g1, out):
    for _ in finish(pos, order, mine, got, base, (g0, g1), out, g0.shape[1]):
        pass


def last_kernel(pos, order, mine, got, base, g0, g1, done, out, buf, sems):
    size = g0.shape[1]
    n = base.shape[2]
    copies = []

    def store(src, part, at):
        lanes = half_lanes(side(pos, 0) ^ part, n)
        sem = sems.at[len(copies)]
        copies.append(pltpu.make_async_copy(src, out.at[:, at, lanes], sem))
        copies[-1].start()

    for leaf in range(2):
        at = pl.ds(pl.multiple_of((order[0, 0] ^ leaf) * size, size), size)
        store(done.at[leaf], 0, at)
    for leaf, here, at in finish(pos, order, mine, got, base, (g0, g1), buf, size):
        store(buf.at[leaf, :, here], 1, at)
    for copy in copies:
        copy.wait()


VMEM = pl.BlockSpec(memory_space=pltpu.VMEM)
SMEM = pl.BlockSpec(memory_space=pltpu.SMEM)
HBM = pl.BlockSpec(memory_space=pltpu.HBM)
GRANT = 20 * 2**20


def call(name, kernel, ins, outs, *args, scratch=(), flops=0, out_spec=VMEM):
    specs = {"s": SMEM, "v": VMEM, "h": HBM}
    moved = sum(a.size * a.dtype.itemsize for a in args)
    return pl.pallas_call(
        kernel,
        out_shape=[jax.ShapeDtypeStruct(shape, dtype) for shape, dtype in outs],
        in_specs=[specs[kind] for kind in ins],
        out_specs=[out_spec] * len(outs),
        scratch_shapes=list(scratch),
        compiler_params=pltpu.CompilerParams(vmem_limit_bytes=GRANT),
        cost_estimate=pl.CostEstimate(flops=flops, bytes_accessed=moved, transcendentals=0),
        name=name,
    )(*args)


def shards(rhs, diag, row_basis, col_basis, wl, bl, cross_w, cross_b, order):
    n = rhs.shape[2]
    rank = col_basis.shape[3]
    size = col_basis.shape[2]
    axes = ("leaf", "top")
    devices = lax.axis_size("leaf") * lax.axis_size("top")
    pos = lax.axis_index(axes).astype(jnp.int32).reshape(1)
    w = cross_w[:, 0]
    b = cross_b[:, 0]

    def swap(value, flip):
        return lax.ppermute(value, axes, [(i, i ^ flip) for i in range(devices)])

    def block(columns, dtype=BF):
        return ((2, columns, rank), dtype)

    mac = 8 * rank * rank
    half, quarter, eighth = n // 2, n // 4, n // 8
    qleaf_shape = ((2, n, rank), BF)
    hbm = [pltpu.with_memory_space_constraint(a, pltpu.HBM) for a in (order, rhs, col_basis, wl, w)]
    q_other, send, xt, x, u, wl, w0 = call(
        "send_half", send_kernel, "shhhhh",
        [qleaf_shape, block(half), ((2, n, size), BF), (rhs.shape, BF), (col_basis.shape, BF),
         (wl.shape, BF), ((2, 1, 2, rank, rank), BF)],
        pos, *hbm,
        scratch=(
            pltpu.SMEM(order.shape, jnp.int32),
            pltpu.VMEM((2, n, size), BF),
            pltpu.SemaphoreType.DMA((7,)),
        ),
        flops=mac * n * 3,
    )
    got0 = swap(send, 1)
    q_mine, keep0 = call(
        "keep_half", keep_kernel, "ssvvv", [qleaf_shape, block(half)],
        pos, order, xt, u, wl, flops=mac * n * 3,
    )
    keep1, send = call(
        "climb_0", first_climb, "svvv", [block(quarter), block(quarter)],
        pos, got0, keep0, w0, flops=mac * n,
    )
    got1 = swap(send, 3)
    keep0, keep1 = lax.optimization_barrier((keep0, keep1))
    got0_other = swap(keep0, 1)
    own, part_0, paths = call(
        "shadow_1", shadow_1, "ss" + "v" * 6,
        [block(quarter, F32), ((2, size, n), F32), ((2, 2, rank, rank), BF)],
        pos, order, keep1, w, w0, wl, x, diag, flops=mac * n * 7,
    )

    def climb(level, got, own):
        return call(
            "climb_%d" % level, climb_kernel(level), "svvv", [block(eighth)],
            pos, got, own, w, flops=mac * eighth,
        )[0]

    keep2, send = call(
        "climb_1", climb_kernel(1), "svvv", [block(eighth), block(eighth)],
        pos, got1, own, w, flops=mac * quarter,
    )
    got2 = swap(send, 5)
    cleaf_shape = ((2, n, rank), BF)
    top_shape = block(eighth, F32)
    own, part_1, cleaf = call(
        "shadow_2", shadow_2, "ss" + "v" * 9, [top_shape, ((2, size, n), F32), cleaf_shape],
        pos, order, keep2, w, x, diag, b, bl, wl, q_mine, got0, flops=mac * n * 8,
    )
    base_shape = ((2, 2 * size, half), F32)
    q3 = climb(2, got2, own)
    got3 = swap(q3, 13)
    own, cleaf_other = call(
        "shadow_3", shadow_3, "s" + "v" * 7, [top_shape, cleaf_shape],
        pos, q3, w, b, bl, wl, q_other, got0_other, flops=mac * n * 4,
    )
    q4 = climb(3, got3, own)
    got4 = swap(q4, 17)
    own, top, base = call(
        "shadow_4", shadow_4, "ss" + "v" * 8,
        [top_shape, top_shape, base_shape],
        pos, order, q4, got3, w, b, row_basis, cleaf, part_0, part_1, flops=mac * n * 2,
    )
    q5 = climb(4, got4, own)
    got5 = swap(q5, 49)
    own, top, path, g0 = call(
        "shadow_5", shadow_5, "s" + "v" * 7,
        [top_shape, top_shape, block(rank), block(size)],
        pos, q5, got4, w, b, row_basis, paths, top, flops=mac * n * 3,
    )
    q6 = climb(5, got5, own)
    got6 = swap(q6, 65)
    own, top, path_6, path_8, g1 = call(
        "shadow_6", shadow_6, "s" + "v" * 8,
        [top_shape, top_shape, block(rank), block(rank), block(size)],
        pos, q6, got5, w, b, row_basis, paths, top, path, flops=mac * n * 4,
    )
    q7 = climb(6, got6, own)
    got7 = swap(q7, 193)
    const, const_oth, path, path_oth = call(
        "shadow_7", shadow_7, "s" + "v" * 8,
        [top_shape, top_shape, block(rank), block(rank)],
        pos, got6, w, b, top, path_6, path_8, keep2, got2, flops=mac * n * 3,
    )
    mine, send = call(
        "top", top_kernel, "s" + "v" * 5, [block(eighth), block(eighth)],
        pos, got7, const, const_oth, path, path_oth, flops=mac * eighth * 2,
    )
    got = swap(send, 5)
    c1, c1_oth = call(
        "shadow_8", shadow_8, "s" + "v" * 4, [block(quarter, F32), block(quarter, F32)],
        pos, mine, keep1, got1, b, flops=mac * half,
    )
    mine, send = call(
        "down", down_kernel, "s" + "v" * 5, [block(quarter), block(quarter)],
        pos, mine, got, c1, c1_oth, w, flops=mac * quarter * 2,
    )
    got = swap(send, 3)
    (base_other,) = call(
        "shadow_9", shadow_9, "ss" + "v" * 5, [base_shape],
        pos, order, mine, row_basis, cleaf_other, part_0, part_1, flops=mac * n * 2,
    )
    late, base_other = lax.optimization_barrier((mine, base_other))
    mine_other = swap(late, 1)
    got_other = swap(got, 1)
    piece = (2, 2, size, half)
    (done,) = call(
        "own_columns", own_kernel, "ss" + "v" * 5, [(piece, BF)],
        pos, order, mine, got, base, g0, g1, flops=mac * n * 2,
    )
    (out,) = call(
        "other_columns", last_kernel, "ss" + "v" * 6, [(rhs.shape, BF)],
        pos, order, mine_other, got_other, base_other, g0, g1, done,
        scratch=(pltpu.VMEM(piece, BF), pltpu.SemaphoreType.DMA((6,))),
        flops=mac * n * 2, out_spec=HBM,
    )
    return out


def solution(mesh):
    return jax.shard_map(
        shards,
        mesh=mesh,
        in_specs=(
            P(None, ("leaf", "top"), None),
            P(None, ("leaf", "top"), None, None),
            P(None, ("leaf", "top"), None, None),
            P(None, ("leaf", "top"), None, None),
            P(None, ("leaf", "top"), None, None, None),
            P(None, ("leaf", "top"), None, None),
            P(None, ("leaf", "top"), None, None, None, None),
            P(None, ("leaf", "top"), None, None, None),
            P(("leaf", "top"), None),
        ),
        out_specs=P(None, ("leaf", "top"), None),
        check_vma=False,
    )
```

```python
import jax
import jax.numpy as jnp
from jax import lax
from jax.experimental import pallas as pl
from jax.experimental.pallas import tpu as pltpu
from jax.sharding import PartitionSpec as P

BF = jnp.bfloat16
F32 = jnp.float32
NN = (((1,), (0,)), ((), ()))
NT = (((1,), (1,)), ((), ()))


def dot(a, b, dims=NN):
    return lax.dot_general(a, b, dims, preferred_element_type=F32)


def widen(a):
    half = a.shape[0] // 2
    re, im = a[:half], a[half:]
    return jnp.concatenate(
        [jnp.concatenate([re, -im], axis=1), jnp.concatenate([im, re], axis=1)], axis=0
    )


def times(a, w_re, w_im):
    return dot(widen(a), jnp.concatenate([w_re, w_im], axis=0))


def times_t(a, w_re, w_im):
    return dot(widen(a), jnp.concatenate([w_re, w_im], axis=1), NT)


def rows(ref):
    return jnp.concatenate([ref[0], ref[1]], axis=0)


def put(ref, value):
    half = value.shape[0] // 2
    ref[0] = value[:half].astype(ref.dtype)
    ref[1] = value[half:].astype(ref.dtype)


def bit(pos, level):
    return (pos[0] >> level) & 1


def lift(q, w, pos, level, flip=0):
    child = bit(pos, level) ^ flip
    return times(q, w[0, level, child], w[1, level, child])


def lower(h, w, pos, level, flip=0):
    child = bit(pos, level) ^ flip
    return times_t(h, w[0, level, child], w[1, level, child])


def couple(q, b, pos, level, flip=0):
    return lax.cond(
        (bit(pos, level) ^ flip) == 0,
        lambda: times_t(q, b[0, level], b[1, level]),
        lambda: times(q, b[0, level], b[1, level]),
    )


def split(value, side, keep, send):
    half = value.shape[0] // 2
    part = half // 2
    for c in range(2):
        low = value[c * half : c * half + part]
        high = value[c * half + part : (c + 1) * half]
        keep[c] = jnp.where(side == 0, low, high)
        send[c] = jnp.where(side == 0, high, low)


def join(own, got, side):
    parts = []
    for c in range(2):
        parts.append(jnp.where(side == 0, own[c], got[c]))
        parts.append(jnp.where(side == 0, got[c], own[c]))
    return jnp.concatenate(parts, axis=0)


def side(pos, level):
    if level == 0:
        return (pos[0] ^ (pos[0] >> 1) ^ (pos[0] >> 2) ^ (pos[0] >> 4) ^ (pos[0] >> 6)) & 1
    if level == 1:
        return bit(pos, 1)
    return bit(pos, 2) ^ bit(pos, 3)


def half_lanes(half, n):
    return pl.ds(pl.multiple_of(half * n, n), n)


def parent(qleaf, wl):
    pair = jnp.concatenate([widen(qleaf[0]), widen(qleaf[1])], axis=1)
    mats = jnp.concatenate([wl[0, 0, 0], wl[1, 0, 0], wl[0, 0, 1], wl[1, 0, 1]], axis=0)
    return dot(pair, mats).astype(BF)


def send_kernel(pos, order, x, u, wl, w, qleaf, send, xt, x_v, u_v, wl_v, w0, order_s, xs, sems):
    size = u.shape[2]
    half = x.shape[2] // 2

    def x_copy(block):
        at = pl.ds(block * size, size)
        return pltpu.make_async_copy(x.at[:, at], x_v.at[:, at], sems.at[block])

    def u_copy(leaf):
        return pltpu.make_async_copy(u.at[:, leaf], u_v.at[:, leaf], sems.at[2 + leaf])

    order_copy = pltpu.make_async_copy(order, order_s, sems.at[4])
    wl_copy = pltpu.make_async_copy(wl, wl_v, sems.at[5])
    w_copy = pltpu.make_async_copy(w.at[:, 0], w0.at[:, 0], sems.at[6])
    x_copy(0).start()
    x_copy(1).start()
    order_copy.start()
    u_copy(0).start()
    u_copy(1).start()
    wl_copy.start()
    w_copy.start()
    keep = side(pos, 0)
    for block in range(2):
        x_copy(block).wait()
        at = pl.ds(block * size, size)
        for out, which in ((xs, 1 - keep), (xt, keep)):
            lanes = half_lanes(which, half)
            out[block, :half] = x_v[0, at, lanes].T
            out[block, half:] = x_v[1, at, lanes].T
    order_copy.wait()
    for leaf in range(2):
        u_copy(leaf).wait()
        block = order_s[0, leaf]
        qleaf[leaf] = times(xs[block], u_v[0, leaf], u_v[1, leaf]).astype(BF)
    wl_copy.wait()
    put(send, parent(qleaf, wl_v))
    w_copy.wait()


def keep_kernel(pos, order, xt, u, wl, qleaf, keep):
    for leaf in range(2):
        block = order[0, leaf]
        qleaf[leaf] = times(xt[block], u[0, leaf], u[1, leaf]).astype(BF)
    put(keep, parent(qleaf, wl))


def first_climb(pos, got, q, w, keep, send):
    c = bit(pos, 0)
    pair = jnp.concatenate([widen(rows(q)), widen(rows(got))], axis=1)
    mats = jnp.concatenate([w[0, 0, c], w[1, 0, c], w[0, 0, 1 - c], w[1, 0, 1 - c]], axis=0)
    split(dot(pair, mats).astype(BF), side(pos, 1), keep, send)


def climb_kernel(level):
    def kernel(pos, got, own, w, *outs):
        q = (rows(own) + lift(rows(got), w, pos, level, 1)).astype(BF)
        if len(outs) == 2:
            split(q, side(pos, level + 1), *outs)
        else:
            put(outs[0], q)

    return kernel


def direct(order, block, x, d, out):
    size = d.shape[2]
    leaf = order[0, 0] ^ block
    at = pl.ds(block * size, size)
    xs = jnp.concatenate([x[0, at], x[1, at]], axis=0)
    re, im = d[0, leaf], d[1, leaf]
    out[0] = dot(jnp.concatenate([re, -im], axis=1), xs)
    out[1] = dot(jnp.concatenate([im, re], axis=1), xs)


def stack(w, level, child):
    return jnp.concatenate([w[0, level, child], w[1, level, child]], axis=0)


def shadow_1(pos, order, keep, w, w0, wl, x, d, own, part, paths):
    put(own, lift(rows(keep), w, pos, 1))
    for leaf in range(2):
        put(paths.at[leaf], lift(stack(wl, 0, leaf), w0, pos, 0))
    direct(order, 0, x, d, part)


def leaf_coupled(pos, q, got, b, bl, wl, cleaf):
    c0 = couple(rows(got), b, pos, 0).astype(BF)
    left = times_t(q[1], bl[0, 0], bl[1, 0])
    right = times(q[0], bl[0, 0], bl[1, 0])
    cleaf[0] = (left + times_t(c0, wl[0, 0, 0], wl[1, 0, 0])).astype(BF)
    cleaf[1] = (right + times_t(c0, wl[0, 0, 1], wl[1, 0, 1])).astype(BF)


def shadow_2(pos, order, keep, w, x, d, b, bl, wl, q_mine, got0, own, part, cleaf):
    put(own, lift(rows(keep), w, pos, 2))
    direct(order, 1, x, d, part)
    leaf_coupled(pos, q_mine, got0, b, bl, wl, cleaf)


def shadow_3(pos, q3, w, b, bl, wl, q_other, got0_other, own, cleaf):
    put(own, lift(rows(q3), w, pos, 3))
    leaf_coupled(pos, q_other, got0_other, b, bl, wl, cleaf)


def set_base(pos, order, part, r, cleaf, parts, base):
    n = base.shape[2]
    size = r.shape[2]
    first = order[0, 0]
    lanes = half_lanes(side(pos, 0) ^ part, n)
    for block, direct_part in enumerate(parts):
        leaf = first ^ block
        add = dot(jnp.concatenate([r[0, leaf], r[1, leaf]], axis=1), widen(cleaf[leaf]), NT)
        for c in range(2):
            base[c, pl.ds(block * size, size)] = (
                direct_part[c, :, lanes] + add[:, c * n : (c + 1) * n]
            )


def shadow_4(pos, order, q4, got3, w, b, r, cleaf, part_0, part_1, own, top, base):
    put(own, lift(rows(q4), w, pos, 4))
    put(top, couple(rows(got3), b, pos, 3))
    set_base(pos, order, 0, r, cleaf, (part_0, part_1), base)


def product(r, paths, leaf, out):
    put(out, times(rows(r.at[:, leaf]), paths[leaf, 0], paths[leaf, 1]))


def shadow_5(pos, q5, got4, w, b, r, paths, top, own, top_out, path, g):
    put(own, lift(rows(q5), w, pos, 5))
    c4 = couple(rows(got4), b, pos, 4).astype(BF)
    put(top_out, rows(top) + lower(c4, w, pos, 3))
    put(path, lift(stack(w, 3, bit(pos, 3)), w, pos, 4))
    product(r, paths, 0, g)


def shadow_6(pos, q6, got5, w, b, top, path, own, top_out, path_6, path_8):
    put(own, lift(rows(q6), w, pos, 6))
    c5 = couple(rows(got5), b, pos, 5).astype(BF)
    put(top_out, rows(top) + times_t(c5, path[0], path[1]))
    longer = lift(rows(path), w, pos, 5).astype(BF)
    put(path_6, longer)
    put(path_8, couple_path(lift(longer, w, pos, 6).astype(BF), b, pos))


def shadow_7(pos, got6, w, b, top, path_6, path_8, keep2, got2, const, const_oth, path, path_oth):
    c6 = couple(rows(got6), b, pos, 6).astype(BF)
    h = (rows(top) + times_t(c6, path_6[0], path_6[1])).astype(BF)
    put(const, couple(rows(got2), b, pos, 2) + lower(h, w, pos, 2))
    put(const_oth, couple(rows(keep2), b, pos, 2, 1) + lower(h, w, pos, 2, 1))
    for flip, out in enumerate((path, path_oth)):
        put(out, times(stack(w, 2, bit(pos, 2) ^ flip), path_8[0], path_8[1]))


def couple_path(path, b, pos):
    return lax.cond(
        bit(pos, 7) == 0,
        lambda: times(path, b[0, 7], b[1, 7]),
        lambda: times_t(path, b[0, 7], b[1, 7]),
    )


def top_kernel(pos, got, const, const_oth, path, path_oth, own, send):
    q = widen(rows(got))
    put(send, rows(const_oth) + dot(q, jnp.concatenate([path_oth[0], path_oth[1]], axis=1), NT))
    put(own, rows(const) + dot(q, jnp.concatenate([path[0], path[1]], axis=1), NT))


def shadow_8(pos, mine, keep1, got1, b, r, paths, c1, c1_oth, g):
    product(r, paths, 1, g)
    put(c1, couple(rows(got1), b, pos, 1))
    put(c1_oth, couple(rows(keep1), b, pos, 1, 1))


def down_kernel(pos, mine, got, c_own, c_oth, w, own, send):
    h = join(mine, got, side(pos, 2))
    put(send, rows(c_oth) + lower(h, w, pos, 1, 1))
    put(own, rows(c_own) + lower(h, w, pos, 1))


def shadow_9(pos, order, mine, r, cleaf, part_0, part_1, base):
    set_base(pos, order, 1, r, cleaf, (part_0, part_1), base)


def finish(pos, order, mine, got, base, gs, out, tile):
    hw = widen(join(mine, got, side(pos, 1)))
    n = base.shape[2]
    for leaf, g in enumerate(gs):
        size = g.shape[1]
        for step in range(size // tile):
            here = pl.ds(step * tile, tile)
            start = (order[0, 0] ^ leaf) * size + step * tile
            at = pl.ds(pl.multiple_of(start, tile), tile)
            add = dot(jnp.concatenate([g[0, here], g[1, here]], axis=1), hw, NT)
            for c in range(2):
                out[leaf, c, here] = (base[c, at] + add[:, c * n : (c + 1) * n]).astype(BF)
            yield leaf, here, at


def own_kernel(pos, order, mine, got, base, g0, g1, out):
    for _ in finish(pos, order, mine, got, base, (g0, g1), out, g0.shape[1]):
        pass


def last_kernel(pos, order, mine, got, base, g0, g1, done, out, buf, sems):
    size = g0.shape[1]
    n = base.shape[2]
    copies = []

    def store(src, part, at):
        lanes = half_lanes(side(pos, 0) ^ part, n)
        sem = sems.at[len(copies)]
        copies.append(pltpu.make_async_copy(src, out.at[:, at, lanes], sem))
        copies[-1].start()

    for leaf in range(2):
        at = pl.ds(pl.multiple_of((order[0, 0] ^ leaf) * size, size), size)
        store(done.at[leaf], 0, at)
    for leaf, here, at in finish(pos, order, mine, got, base, (g0, g1), buf, size):
        store(buf.at[leaf, :, here], 1, at)
    for copy in copies:
        copy.wait()


VMEM = pl.BlockSpec(memory_space=pltpu.VMEM)
SMEM = pl.BlockSpec(memory_space=pltpu.SMEM)
HBM = pl.BlockSpec(memory_space=pltpu.HBM)
GRANT = 20 * 2**20


def call(name, kernel, ins, outs, *args, scratch=(), flops=0, out_spec=VMEM):
    specs = {"s": SMEM, "v": VMEM, "h": HBM}
    moved = sum(a.size * a.dtype.itemsize for a in args)
    return pl.pallas_call(
        kernel,
        out_shape=[jax.ShapeDtypeStruct(shape, dtype) for shape, dtype in outs],
        in_specs=[specs[kind] for kind in ins],
        out_specs=[out_spec] * len(outs),
        scratch_shapes=list(scratch),
        compiler_params=pltpu.CompilerParams(vmem_limit_bytes=GRANT),
        cost_estimate=pl.CostEstimate(flops=flops, bytes_accessed=moved, transcendentals=0),
        name=name,
    )(*args)


def shards(rhs, diag, row_basis, col_basis, wl, bl, cross_w, cross_b, order):
    n = rhs.shape[2]
    rank = col_basis.shape[3]
    size = col_basis.shape[2]
    axes = ("leaf", "top")
    devices = lax.axis_size("leaf") * lax.axis_size("top")
    pos = lax.axis_index(axes).astype(jnp.int32).reshape(1)
    w = cross_w[:, 0]
    b = cross_b[:, 0]

    def swap(value, flip):
        return lax.ppermute(value, axes, [(i, i ^ flip) for i in range(devices)])

    def block(columns, dtype=BF):
        return ((2, columns, rank), dtype)

    mac = 8 * rank * rank
    half, quarter, eighth = n // 2, n // 4, n // 8
    qleaf_shape = ((2, n, rank), BF)
    hbm = [pltpu.with_memory_space_constraint(a, pltpu.HBM) for a in (order, rhs, col_basis, wl, w)]
    q_other, send, xt, x, u, wl, w0 = call(
        "send_half", send_kernel, "shhhhh",
        [qleaf_shape, block(half), ((2, n, size), BF), (rhs.shape, BF), (col_basis.shape, BF),
         (wl.shape, BF), ((2, 1, 2, rank, rank), BF)],
        pos, *hbm,
        scratch=(
            pltpu.SMEM(order.shape, jnp.int32),
            pltpu.VMEM((2, n, size), BF),
            pltpu.SemaphoreType.DMA((7,)),
        ),
        flops=mac * n * 3,
    )
    got0 = swap(send, 1)
    q_mine, keep0 = call(
        "keep_half", keep_kernel, "ssvvv", [qleaf_shape, block(half)],
        pos, order, xt, u, wl, flops=mac * n * 3,
    )
    keep1, send = call(
        "climb_0", first_climb, "svvv", [block(quarter), block(quarter)],
        pos, got0, keep0, w0, flops=mac * n,
    )
    got1 = swap(send, 3)
    keep0, keep1 = lax.optimization_barrier((keep0, keep1))
    got0_other = swap(keep0, 1)
    own, part_0, paths = call(
        "shadow_1", shadow_1, "ss" + "v" * 6,
        [block(quarter, F32), ((2, size, n), F32), ((2, 2, rank, rank), BF)],
        pos, order, keep1, w, w0, wl, x, diag, flops=mac * n * 7,
    )

    def climb(level, got, own):
        return call(
            "climb_%d" % level, climb_kernel(level), "svvv", [block(eighth)],
            pos, got, own, w, flops=mac * eighth,
        )[0]

    keep2, send = call(
        "climb_1", climb_kernel(1), "svvv", [block(eighth), block(eighth)],
        pos, got1, own, w, flops=mac * quarter,
    )
    got2 = swap(send, 5)
    cleaf_shape = ((2, n, rank), BF)
    top_shape = block(eighth, F32)
    own, part_1, cleaf = call(
        "shadow_2", shadow_2, "ss" + "v" * 9, [top_shape, ((2, size, n), F32), cleaf_shape],
        pos, order, keep2, w, x, diag, b, bl, wl, q_mine, got0, flops=mac * n * 8,
    )
    base_shape = ((2, 2 * size, half), F32)
    q3 = climb(2, got2, own)
    got3 = swap(q3, 13)
    own, cleaf_other = call(
        "shadow_3", shadow_3, "s" + "v" * 7, [top_shape, cleaf_shape],
        pos, q3, w, b, bl, wl, q_other, got0_other, flops=mac * n * 4,
    )
    q4 = climb(3, got3, own)
    got4 = swap(q4, 17)
    own, top, base = call(
        "shadow_4", shadow_4, "ss" + "v" * 8,
        [top_shape, top_shape, base_shape],
        pos, order, q4, got3, w, b, row_basis, cleaf, part_0, part_1, flops=mac * n * 2,
    )
    q5 = climb(4, got4, own)
    got5 = swap(q5, 49)
    own, top, path, g0 = call(
        "shadow_5", shadow_5, "s" + "v" * 7,
        [top_shape, top_shape, block(rank), block(size)],
        pos, q5, got4, w, b, row_basis, paths, top, flops=mac * n * 3,
    )
    q6 = climb(5, got5, own)
    got6 = swap(q6, 65)
    own, top, path_6, path_8 = call(
        "shadow_6", shadow_6, "s" + "v" * 6, [top_shape, top_shape, block(rank), block(rank)],
        pos, q6, got5, w, b, top, path, flops=mac * n * 3,
    )
    q7 = climb(6, got6, own)
    got7 = swap(q7, 193)
    const, const_oth, path, path_oth = call(
        "shadow_7", shadow_7, "s" + "v" * 8,
        [top_shape, top_shape, block(rank), block(rank)],
        pos, got6, w, b, top, path_6, path_8, keep2, got2, flops=mac * n * 3,
    )
    mine, send = call(
        "top", top_kernel, "s" + "v" * 5, [block(eighth), block(eighth)],
        pos, got7, const, const_oth, path, path_oth, flops=mac * eighth * 2,
    )
    got = swap(send, 5)
    c1, c1_oth, g1 = call(
        "shadow_8", shadow_8, "s" + "v" * 6,
        [block(quarter, F32), block(quarter, F32), block(size)],
        pos, mine, keep1, got1, b, row_basis, paths, flops=mac * n * 2,
    )
    mine, send = call(
        "down", down_kernel, "s" + "v" * 5, [block(quarter), block(quarter)],
        pos, mine, got, c1, c1_oth, w, flops=mac * quarter * 2,
    )
    got = swap(send, 3)
    (base_other,) = call(
        "shadow_9", shadow_9, "ss" + "v" * 5, [base_shape],
        pos, order, mine, row_basis, cleaf_other, part_0, part_1, flops=mac * n * 2,
    )
    late, base_other = lax.optimization_barrier((mine, base_other))
    mine_other = swap(late, 1)
    got_other = swap(got, 1)
    piece = (2, 2, size, half)
    (done,) = call(
        "own_columns", own_kernel, "ss" + "v" * 5, [(piece, BF)],
        pos, order, mine, got, base, g0, g1, flops=mac * n * 2,
    )
    (out,) = call(
        "other_columns", last_kernel, "ss" + "v" * 6, [(rhs.shape, BF)],
        pos, order, mine_other, got_other, base_other, g0, g1, done,
        scratch=(pltpu.VMEM(piece, BF), pltpu.SemaphoreType.DMA((6,))),
        flops=mac * n * 2, out_spec=HBM,
    )
    return out


def solution(mesh):
    return jax.shard_map(
        shards,
        mesh=mesh,
        in_specs=(
            P(None, ("leaf", "top"), None),
            P(None, ("leaf", "top"), None, None),
            P(None, ("leaf", "top"), None, None),
            P(None, ("leaf", "top"), None, None),
            P(None, ("leaf", "top"), None, None, None),
            P(None, ("leaf", "top"), None, None),
            P(None, ("leaf", "top"), None, None, None, None),
            P(None, ("leaf", "top"), None, None, None),
            P(("leaf", "top"), None),
        ),
        out_specs=P(None, ("leaf", "top"), None),
        check_vma=False,
    )
```

```python
import jax
import jax.numpy as jnp
from jax import lax
from jax.experimental import pallas as pl
from jax.experimental.pallas import tpu as pltpu
from jax.sharding import PartitionSpec as P

BF = jnp.bfloat16
F32 = jnp.float32
NN = (((1,), (0,)), ((), ()))
NT = (((1,), (1,)), ((), ()))


def dot(a, b, dims=NN):
    return lax.dot_general(a, b, dims, preferred_element_type=F32)


def widen(a):
    half = a.shape[0] // 2
    re, im = a[:half], a[half:]
    return jnp.concatenate(
        [jnp.concatenate([re, -im], axis=1), jnp.concatenate([im, re], axis=1)], axis=0
    )


def times(a, w_re, w_im):
    return dot(widen(a), jnp.concatenate([w_re, w_im], axis=0))


def times_t(a, w_re, w_im):
    return dot(widen(a), jnp.concatenate([w_re, w_im], axis=1), NT)


def rows(ref):
    return jnp.concatenate([ref[0], ref[1]], axis=0)


def put(ref, value):
    half = value.shape[0] // 2
    ref[0] = value[:half].astype(ref.dtype)
    ref[1] = value[half:].astype(ref.dtype)


def bit(pos, level):
    return (pos[0] >> level) & 1


def lift(q, w, pos, level, flip=0):
    child = bit(pos, level) ^ flip
    return times(q, w[0, level, child], w[1, level, child])


def lower(h, w, pos, level, flip=0):
    child = bit(pos, level) ^ flip
    return times_t(h, w[0, level, child], w[1, level, child])


def couple(q, b, pos, level, flip=0):
    return lax.cond(
        (bit(pos, level) ^ flip) == 0,
        lambda: times_t(q, b[0, level], b[1, level]),
        lambda: times(q, b[0, level], b[1, level]),
    )


def split(value, side, keep, send):
    half = value.shape[0] // 2
    part = half // 2
    for c in range(2):
        low = value[c * half : c * half + part]
        high = value[c * half + part : (c + 1) * half]
        keep[c] = jnp.where(side == 0, low, high)
        send[c] = jnp.where(side == 0, high, low)


def join(own, got, side):
    parts = []
    for c in range(2):
        parts.append(jnp.where(side == 0, own[c], got[c]))
        parts.append(jnp.where(side == 0, got[c], own[c]))
    return jnp.concatenate(parts, axis=0)


def side(pos, level):
    if level == 0:
        return (pos[0] ^ (pos[0] >> 1) ^ (pos[0] >> 2) ^ (pos[0] >> 4) ^ (pos[0] >> 6)) & 1
    if level == 1:
        return bit(pos, 1)
    return bit(pos, 2) ^ bit(pos, 3)


def half_lanes(half, n):
    return pl.ds(pl.multiple_of(half * n, n), n)


def parent(qleaf, wl):
    pair = jnp.concatenate([widen(qleaf[0]), widen(qleaf[1])], axis=1)
    mats = jnp.concatenate([wl[0, 0, 0], wl[1, 0, 0], wl[0, 0, 1], wl[1, 0, 1]], axis=0)
    return dot(pair, mats).astype(BF)


def send_kernel(pos, order, x, u, wl, w, qleaf, send, xt, x_v, u_v, wl_v, w0, order_s, xs, sems):
    size = u.shape[2]
    half = x.shape[2] // 2

    def x_copy(block):
        at = pl.ds(block * size, size)
        return pltpu.make_async_copy(x.at[:, at], x_v.at[:, at], sems.at[block])

    def u_copy(leaf):
        return pltpu.make_async_copy(u.at[:, leaf], u_v.at[:, leaf], sems.at[2 + leaf])

    order_copy = pltpu.make_async_copy(order, order_s, sems.at[4])
    wl_copy = pltpu.make_async_copy(wl, wl_v, sems.at[5])
    w_copy = pltpu.make_async_copy(w.at[:, 0], w0.at[:, 0], sems.at[6])
    x_copy(0).start()
    x_copy(1).start()
    order_copy.start()
    u_copy(0).start()
    u_copy(1).start()
    wl_copy.start()
    w_copy.start()
    keep = side(pos, 0)
    for block in range(2):
        x_copy(block).wait()
        at = pl.ds(block * size, size)
        for out, which in ((xs, 1 - keep), (xt, keep)):
            lanes = half_lanes(which, half)
            out[block, :half] = x_v[0, at, lanes].T
            out[block, half:] = x_v[1, at, lanes].T
    order_copy.wait()
    for leaf in range(2):
        u_copy(leaf).wait()
        block = order_s[0, leaf]
        qleaf[leaf] = times(xs[block], u_v[0, leaf], u_v[1, leaf]).astype(BF)
    wl_copy.wait()
    put(send, parent(qleaf, wl_v))
    w_copy.wait()


def keep_kernel(pos, order, xt, u, wl, qleaf, keep):
    for leaf in range(2):
        block = order[0, leaf]
        qleaf[leaf] = times(xt[block], u[0, leaf], u[1, leaf]).astype(BF)
    put(keep, parent(qleaf, wl))


def first_climb(pos, got, q, w, keep, send):
    c = bit(pos, 0)
    pair = jnp.concatenate([widen(rows(q)), widen(rows(got))], axis=1)
    mats = jnp.concatenate([w[0, 0, c], w[1, 0, c], w[0, 0, 1 - c], w[1, 0, 1 - c]], axis=0)
    split(dot(pair, mats).astype(BF), side(pos, 1), keep, send)


def climb_kernel(level):
    def kernel(pos, got, own, w, *outs):
        q = (rows(own) + lift(rows(got), w, pos, level, 1)).astype(BF)
        if len(outs) == 2:
            split(q, side(pos, level + 1), *outs)
        else:
            put(outs[0], q)

    return kernel


def direct(order, block, x, d, out):
    size = d.shape[2]
    leaf = order[0, 0] ^ block
    at = pl.ds(block * size, size)
    xs = jnp.concatenate([x[0, at], x[1, at]], axis=0)
    re, im = d[0, leaf], d[1, leaf]
    out[0] = dot(jnp.concatenate([re, -im], axis=1), xs)
    out[1] = dot(jnp.concatenate([im, re], axis=1), xs)


def stack(w, level, child):
    return jnp.concatenate([w[0, level, child], w[1, level, child]], axis=0)


def shadow_1(pos, order, keep, w, w0, wl, x, d, own, part, paths):
    put(own, lift(rows(keep), w, pos, 1))
    for leaf in range(2):
        put(paths.at[leaf], lift(stack(wl, 0, leaf), w0, pos, 0))
    direct(order, 0, x, d, part)


def leaf_coupled(pos, q, got, b, bl, wl, cleaf):
    c0 = couple(rows(got), b, pos, 0).astype(BF)
    left = times_t(q[1], bl[0, 0], bl[1, 0])
    right = times(q[0], bl[0, 0], bl[1, 0])
    cleaf[0] = (left + times_t(c0, wl[0, 0, 0], wl[1, 0, 0])).astype(BF)
    cleaf[1] = (right + times_t(c0, wl[0, 0, 1], wl[1, 0, 1])).astype(BF)


def shadow_2(pos, order, keep, w, x, d, b, bl, wl, q_mine, got0, own, part, cleaf):
    put(own, lift(rows(keep), w, pos, 2))
    direct(order, 1, x, d, part)
    leaf_coupled(pos, q_mine, got0, b, bl, wl, cleaf)


def shadow_3(pos, q3, w, b, bl, wl, q_other, got0_other, keep2, got2, own, cleaf, c2, c2_oth):
    put(own, lift(rows(q3), w, pos, 3))
    put(c2, couple(rows(got2), b, pos, 2))
    put(c2_oth, couple(rows(keep2), b, pos, 2, 1))
    leaf_coupled(pos, q_other, got0_other, b, bl, wl, cleaf)


def set_base(pos, order, part, r, cleaf, parts, base):
    n = base.shape[2]
    size = r.shape[2]
    first = order[0, 0]
    lanes = half_lanes(side(pos, 0) ^ part, n)
    for block, direct_part in enumerate(parts):
        leaf = first ^ block
        add = dot(jnp.concatenate([r[0, leaf], r[1, leaf]], axis=1), widen(cleaf[leaf]), NT)
        for c in range(2):
            base[c, pl.ds(block * size, size)] = (
                direct_part[c, :, lanes] + add[:, c * n : (c + 1) * n]
            )


def shadow_4(pos, order, q4, got3, w, b, r, cleaf, part_0, part_1, own, top, base):
    put(own, lift(rows(q4), w, pos, 4))
    put(top, couple(rows(got3), b, pos, 3))
    set_base(pos, order, 0, r, cleaf, (part_0, part_1), base)


def product(r, paths, leaf, out):
    put(out, times(rows(r.at[:, leaf]), paths[leaf, 0], paths[leaf, 1]))


def shadow_5(pos, q5, got4, w, b, r, paths, top, own, top_out, path, g):
    put(own, lift(rows(q5), w, pos, 5))
    c4 = couple(rows(got4), b, pos, 4).astype(BF)
    put(top_out, rows(top) + lower(c4, w, pos, 3))
    put(path, lift(stack(w, 3, bit(pos, 3)), w, pos, 4))
    product(r, paths, 0, g)


def shadow_6(pos, q6, got5, w, b, top, path, own, top_out, path_6, path_8):
    put(own, lift(rows(q6), w, pos, 6))
    c5 = couple(rows(got5), b, pos, 5).astype(BF)
    put(top_out, rows(top) + times_t(c5, path[0], path[1]))
    longer = lift(rows(path), w, pos, 5).astype(BF)
    put(path_6, longer)
    put(path_8, couple_path(lift(longer, w, pos, 6).astype(BF), b, pos))


def shadow_7(pos, got6, w, b, top, path_6, path_8, c2, c2_oth, const, const_oth, path, path_oth):
    c6 = couple(rows(got6), b, pos, 6).astype(BF)
    h = (rows(top) + times_t(c6, path_6[0], path_6[1])).astype(BF)
    put(const, rows(c2) + lower(h, w, pos, 2))
    put(const_oth, rows(c2_oth) + lower(h, w, pos, 2, 1))
    for flip, out in enumerate((path, path_oth)):
        put(out, times(stack(w, 2, bit(pos, 2) ^ flip), path_8[0], path_8[1]))


def couple_path(path, b, pos):
    return lax.cond(
        bit(pos, 7) == 0,
        lambda: times(path, b[0, 7], b[1, 7]),
        lambda: times_t(path, b[0, 7], b[1, 7]),
    )


def top_kernel(pos, got, const, const_oth, path, path_oth, own, send):
    q = widen(rows(got))
    put(send, rows(const_oth) + dot(q, jnp.concatenate([path_oth[0], path_oth[1]], axis=1), NT))
    put(own, rows(const) + dot(q, jnp.concatenate([path[0], path[1]], axis=1), NT))


def shadow_8(pos, mine, keep1, got1, b, r, paths, c1, c1_oth, g):
    product(r, paths, 1, g)
    put(c1, couple(rows(got1), b, pos, 1))
    put(c1_oth, couple(rows(keep1), b, pos, 1, 1))


def down_kernel(pos, mine, got, c_own, c_oth, w, own, send):
    h = join(mine, got, side(pos, 2))
    put(send, rows(c_oth) + lower(h, w, pos, 1, 1))
    put(own, rows(c_own) + lower(h, w, pos, 1))


def shadow_9(pos, order, mine, r, cleaf, part_0, part_1, base):
    set_base(pos, order, 1, r, cleaf, (part_0, part_1), base)


def finish(pos, order, mine, got, base, gs, out, tile):
    hw = widen(join(mine, got, side(pos, 1)))
    n = base.shape[2]
    for leaf, g in enumerate(gs):
        size = g.shape[1]
        for step in range(size // tile):
            here = pl.ds(step * tile, tile)
            start = (order[0, 0] ^ leaf) * size + step * tile
            at = pl.ds(pl.multiple_of(start, tile), tile)
            add = dot(jnp.concatenate([g[0, here], g[1, here]], axis=1), hw, NT)
            for c in range(2):
                out[leaf, c, here] = (base[c, at] + add[:, c * n : (c + 1) * n]).astype(BF)
            yield leaf, here, at


def own_kernel(pos, order, mine, got, base, g0, g1, out):
    for _ in finish(pos, order, mine, got, base, (g0, g1), out, g0.shape[1]):
        pass


def last_kernel(pos, order, mine, got, base, g0, g1, done, out, buf, sems):
    size = g0.shape[1]
    n = base.shape[2]
    copies = []

    def store(src, part, at):
        lanes = half_lanes(side(pos, 0) ^ part, n)
        sem = sems.at[len(copies)]
        copies.append(pltpu.make_async_copy(src, out.at[:, at, lanes], sem))
        copies[-1].start()

    for leaf in range(2):
        at = pl.ds(pl.multiple_of((order[0, 0] ^ leaf) * size, size), size)
        store(done.at[leaf], 0, at)
    for leaf, here, at in finish(pos, order, mine, got, base, (g0, g1), buf, size):
        store(buf.at[leaf, :, here], 1, at)
    for copy in copies:
        copy.wait()


VMEM = pl.BlockSpec(memory_space=pltpu.VMEM)
SMEM = pl.BlockSpec(memory_space=pltpu.SMEM)
HBM = pl.BlockSpec(memory_space=pltpu.HBM)
GRANT = 20 * 2**20


def call(name, kernel, ins, outs, *args, scratch=(), flops=0, out_spec=VMEM):
    specs = {"s": SMEM, "v": VMEM, "h": HBM}
    moved = sum(a.size * a.dtype.itemsize for a in args)
    return pl.pallas_call(
        kernel,
        out_shape=[jax.ShapeDtypeStruct(shape, dtype) for shape, dtype in outs],
        in_specs=[specs[kind] for kind in ins],
        out_specs=[out_spec] * len(outs),
        scratch_shapes=list(scratch),
        compiler_params=pltpu.CompilerParams(vmem_limit_bytes=GRANT),
        cost_estimate=pl.CostEstimate(flops=flops, bytes_accessed=moved, transcendentals=0),
        name=name,
    )(*args)


def shards(rhs, diag, row_basis, col_basis, wl, bl, cross_w, cross_b, order):
    n = rhs.shape[2]
    rank = col_basis.shape[3]
    size = col_basis.shape[2]
    axes = ("leaf", "top")
    devices = lax.axis_size("leaf") * lax.axis_size("top")
    pos = lax.axis_index(axes).astype(jnp.int32).reshape(1)
    w = cross_w[:, 0]
    b = cross_b[:, 0]

    def swap(value, flip):
        return lax.ppermute(value, axes, [(i, i ^ flip) for i in range(devices)])

    def block(columns, dtype=BF):
        return ((2, columns, rank), dtype)

    mac = 8 * rank * rank
    half, quarter, eighth = n // 2, n // 4, n // 8
    qleaf_shape = ((2, n, rank), BF)
    hbm = [pltpu.with_memory_space_constraint(a, pltpu.HBM) for a in (order, rhs, col_basis, wl, w)]
    q_other, send, xt, x, u, wl, w0 = call(
        "send_half", send_kernel, "shhhhh",
        [qleaf_shape, block(half), ((2, n, size), BF), (rhs.shape, BF), (col_basis.shape, BF),
         (wl.shape, BF), ((2, 1, 2, rank, rank), BF)],
        pos, *hbm,
        scratch=(
            pltpu.SMEM(order.shape, jnp.int32),
            pltpu.VMEM((2, n, size), BF),
            pltpu.SemaphoreType.DMA((7,)),
        ),
        flops=mac * n * 3,
    )
    got0 = swap(send, 1)
    q_mine, keep0 = call(
        "keep_half", keep_kernel, "ssvvv", [qleaf_shape, block(half)],
        pos, order, xt, u, wl, flops=mac * n * 3,
    )
    keep1, send = call(
        "climb_0", first_climb, "svvv", [block(quarter), block(quarter)],
        pos, got0, keep0, w0, flops=mac * n,
    )
    got1 = swap(send, 3)
    keep0, keep1 = lax.optimization_barrier((keep0, keep1))
    got0_other = swap(keep0, 1)
    own, part_0, paths = call(
        "shadow_1", shadow_1, "ss" + "v" * 6,
        [block(quarter, F32), ((2, size, n), F32), ((2, 2, rank, rank), BF)],
        pos, order, keep1, w, w0, wl, x, diag, flops=mac * n * 7,
    )

    def climb(level, got, own):
        return call(
            "climb_%d" % level, climb_kernel(level), "svvv", [block(eighth)],
            pos, got, own, w, flops=mac * eighth,
        )[0]

    keep2, send = call(
        "climb_1", climb_kernel(1), "svvv", [block(eighth), block(eighth)],
        pos, got1, own, w, flops=mac * quarter,
    )
    got2 = swap(send, 5)
    cleaf_shape = ((2, n, rank), BF)
    top_shape = block(eighth, F32)
    own, part_1, cleaf = call(
        "shadow_2", shadow_2, "ss" + "v" * 9, [top_shape, ((2, size, n), F32), cleaf_shape],
        pos, order, keep2, w, x, diag, b, bl, wl, q_mine, got0, flops=mac * n * 8,
    )
    base_shape = ((2, 2 * size, half), F32)
    q3 = climb(2, got2, own)
    got3 = swap(q3, 13)
    own, cleaf_other, c2, c2_oth = call(
        "shadow_3", shadow_3, "s" + "v" * 9, [top_shape, cleaf_shape, top_shape, top_shape],
        pos, q3, w, b, bl, wl, q_other, got0_other, keep2, got2, flops=mac * n * 4,
    )
    q4 = climb(3, got3, own)
    got4 = swap(q4, 17)
    own, top, base = call(
        "shadow_4", shadow_4, "ss" + "v" * 8,
        [top_shape, top_shape, base_shape],
        pos, order, q4, got3, w, b, row_basis, cleaf, part_0, part_1, flops=mac * n * 2,
    )
    q5 = climb(4, got4, own)
    got5 = swap(q5, 49)
    own, top, path, g0 = call(
        "shadow_5", shadow_5, "s" + "v" * 7,
        [top_shape, top_shape, block(rank), block(size)],
        pos, q5, got4, w, b, row_basis, paths, top, flops=mac * n * 3,
    )
    q6 = climb(5, got5, own)
    got6 = swap(q6, 65)
    own, top, path_6, path_8 = call(
        "shadow_6", shadow_6, "s" + "v" * 6, [top_shape, top_shape, block(rank), block(rank)],
        pos, q6, got5, w, b, top, path, flops=mac * n * 3,
    )
    q7 = climb(6, got6, own)
    got7 = swap(q7, 193)
    const, const_oth, path, path_oth = call(
        "shadow_7", shadow_7, "s" + "v" * 8,
        [top_shape, top_shape, block(rank), block(rank)],
        pos, got6, w, b, top, path_6, path_8, c2, c2_oth, flops=mac * n * 3,
    )
    mine, send = call(
        "top", top_kernel, "s" + "v" * 5, [block(eighth), block(eighth)],
        pos, got7, const, const_oth, path, path_oth, flops=mac * eighth * 2,
    )
    got = swap(send, 5)
    c1, c1_oth, g1 = call(
        "shadow_8", shadow_8, "s" + "v" * 6,
        [block(quarter, F32), block(quarter, F32), block(size)],
        pos, mine, keep1, got1, b, row_basis, paths, flops=mac * n * 2,
    )
    mine, send = call(
        "down", down_kernel, "s" + "v" * 5, [block(quarter), block(quarter)],
        pos, mine, got, c1, c1_oth, w, flops=mac * quarter * 2,
    )
    got = swap(send, 3)
    (base_other,) = call(
        "shadow_9", shadow_9, "ss" + "v" * 5, [base_shape],
        pos, order, mine, row_basis, cleaf_other, part_0, part_1, flops=mac * n * 2,
    )
    late, base_other = lax.optimization_barrier((mine, base_other))
    mine_other = swap(late, 1)
    got_other = swap(got, 1)
    piece = (2, 2, size, half)
    (done,) = call(
        "own_columns", own_kernel, "ss" + "v" * 5, [(piece, BF)],
        pos, order, mine, got, base, g0, g1, flops=mac * n * 2,
    )
    (out,) = call(
        "other_columns", last_kernel, "ss" + "v" * 6, [(rhs.shape, BF)],
        pos, order, mine_other, got_other, base_other, g0, g1, done,
        scratch=(pltpu.VMEM(piece, BF), pltpu.SemaphoreType.DMA((6,))),
        flops=mac * n * 2, out_spec=HBM,
    )
    return out


def solution(mesh):
    return jax.shard_map(
        shards,
        mesh=mesh,
        in_specs=(
            P(None, ("leaf", "top"), None),
            P(None, ("leaf", "top"), None, None),
            P(None, ("leaf", "top"), None, None),
            P(None, ("leaf", "top"), None, None),
            P(None, ("leaf", "top"), None, None, None),
            P(None, ("leaf", "top"), None, None),
            P(None, ("leaf", "top"), None, None, None, None),
            P(None, ("leaf", "top"), None, None, None),
            P(("leaf", "top"), None),
        ),
        out_specs=P(None, ("leaf", "top"), None),
        check_vma=False,
    )
```

```python
import jax
import jax.numpy as jnp
from jax import lax
from jax.experimental import pallas as pl
from jax.experimental.pallas import tpu as pltpu
from jax.sharding import PartitionSpec as P

BF = jnp.bfloat16
F32 = jnp.float32
NN = (((1,), (0,)), ((), ()))
NT = (((1,), (1,)), ((), ()))


def dot(a, b, dims=NN):
    return lax.dot_general(a, b, dims, preferred_element_type=F32)


def widen(a):
    half = a.shape[0] // 2
    re, im = a[:half], a[half:]
    return jnp.concatenate(
        [jnp.concatenate([re, -im], axis=1), jnp.concatenate([im, re], axis=1)], axis=0
    )


def times(a, w_re, w_im):
    return dot(widen(a), jnp.concatenate([w_re, w_im], axis=0))


def times_t(a, w_re, w_im):
    return dot(widen(a), jnp.concatenate([w_re, w_im], axis=1), NT)


def rows(ref):
    return jnp.concatenate([ref[0], ref[1]], axis=0)


def put(ref, value):
    half = value.shape[0] // 2
    ref[0] = value[:half].astype(ref.dtype)
    ref[1] = value[half:].astype(ref.dtype)


def bit(pos, level):
    return (pos[0] >> level) & 1


def lift(q, w, pos, level, flip=0):
    child = bit(pos, level) ^ flip
    return times(q, w[0, level, child], w[1, level, child])


def lower(h, w, pos, level, flip=0):
    child = bit(pos, level) ^ flip
    return times_t(h, w[0, level, child], w[1, level, child])


def couple(q, b, pos, level, flip=0):
    return lax.cond(
        (bit(pos, level) ^ flip) == 0,
        lambda: times_t(q, b[0, level], b[1, level]),
        lambda: times(q, b[0, level], b[1, level]),
    )


def split(value, side, keep, send):
    half = value.shape[0] // 2
    part = half // 2
    for c in range(2):
        low = value[c * half : c * half + part]
        high = value[c * half + part : (c + 1) * half]
        keep[c] = jnp.where(side == 0, low, high)
        send[c] = jnp.where(side == 0, high, low)


def join(own, got, side):
    parts = []
    for c in range(2):
        parts.append(jnp.where(side == 0, own[c], got[c]))
        parts.append(jnp.where(side == 0, got[c], own[c]))
    return jnp.concatenate(parts, axis=0)


def side(pos, level):
    if level == 0:
        return (pos[0] ^ (pos[0] >> 1) ^ (pos[0] >> 2) ^ (pos[0] >> 4) ^ (pos[0] >> 6)) & 1
    if level == 1:
        return bit(pos, 1)
    return bit(pos, 2) ^ bit(pos, 3)


def half_lanes(half, n):
    return pl.ds(pl.multiple_of(half * n, n), n)


def parent(qleaf, wl):
    pair = jnp.concatenate([widen(qleaf[0]), widen(qleaf[1])], axis=1)
    mats = jnp.concatenate([wl[0, 0, 0], wl[1, 0, 0], wl[0, 0, 1], wl[1, 0, 1]], axis=0)
    return dot(pair, mats).astype(BF)


def send_kernel(pos, order, x, u, wl, w, qleaf, send, xt, x_v, u_v, wl_v, w0, order_s, xs, sems):
    size = u.shape[2]
    half = x.shape[2] // 2

    def x_copy(block):
        at = pl.ds(block * size, size)
        return pltpu.make_async_copy(x.at[:, at], x_v.at[:, at], sems.at[block])

    def u_copy(leaf):
        return pltpu.make_async_copy(u.at[:, leaf], u_v.at[:, leaf], sems.at[2 + leaf])

    order_copy = pltpu.make_async_copy(order, order_s, sems.at[4])
    wl_copy = pltpu.make_async_copy(wl, wl_v, sems.at[5])
    w_copy = pltpu.make_async_copy(w.at[:, 0], w0.at[:, 0], sems.at[6])
    x_copy(0).start()
    x_copy(1).start()
    order_copy.start()
    u_copy(0).start()
    u_copy(1).start()
    wl_copy.start()
    w_copy.start()
    keep = side(pos, 0)
    for block in range(2):
        x_copy(block).wait()
        at = pl.ds(block * size, size)
        for out, which in ((xs, 1 - keep), (xt, keep)):
            lanes = half_lanes(which, half)
            out[block, :half] = x_v[0, at, lanes].T
            out[block, half:] = x_v[1, at, lanes].T
    order_copy.wait()
    for leaf in range(2):
        u_copy(leaf).wait()
        block = order_s[0, leaf]
        qleaf[leaf] = times(xs[block], u_v[0, leaf], u_v[1, leaf]).astype(BF)
    wl_copy.wait()
    put(send, parent(qleaf, wl_v))
    w_copy.wait()


def keep_kernel(pos, order, xt, u, wl, qleaf, keep):
    for leaf in range(2):
        block = order[0, leaf]
        qleaf[leaf] = times(xt[block], u[0, leaf], u[1, leaf]).astype(BF)
    put(keep, parent(qleaf, wl))


def first_climb(pos, got, q, w, keep, send):
    c = bit(pos, 0)
    pair = jnp.concatenate([widen(rows(q)), widen(rows(got))], axis=1)
    mats = jnp.concatenate([w[0, 0, c], w[1, 0, c], w[0, 0, 1 - c], w[1, 0, 1 - c]], axis=0)
    split(dot(pair, mats).astype(BF), side(pos, 1), keep, send)


def climb_kernel(level):
    def kernel(pos, got, own, w, *outs):
        q = (rows(own) + lift(rows(got), w, pos, level, 1)).astype(BF)
        if len(outs) == 2:
            split(q, side(pos, level + 1), *outs)
        else:
            put(outs[0], q)

    return kernel


def direct(order, block, x, d, out):
    size = d.shape[2]
    leaf = order[0, 0] ^ block
    at = pl.ds(block * size, size)
    xs = jnp.concatenate([x[0, at], x[1, at]], axis=0)
    re, im = d[0, leaf], d[1, leaf]
    out[0] = dot(jnp.concatenate([re, -im], axis=1), xs)
    out[1] = dot(jnp.concatenate([im, re], axis=1), xs)


def stack(w, level, child):
    return jnp.concatenate([w[0, level, child], w[1, level, child]], axis=0)


def shadow_1(pos, order, keep, w, w0, wl, x, d, own, part, paths):
    put(own, lift(rows(keep), w, pos, 1))
    for leaf in range(2):
        put(paths.at[leaf], lift(stack(wl, 0, leaf), w0, pos, 0))
    direct(order, 0, x, d, part)


def leaf_coupled(pos, q, got, b, bl, wl, cleaf):
    c0 = couple(rows(got), b, pos, 0).astype(BF)
    left = times_t(q[1], bl[0, 0], bl[1, 0])
    right = times(q[0], bl[0, 0], bl[1, 0])
    cleaf[0] = (left + times_t(c0, wl[0, 0, 0], wl[1, 0, 0])).astype(BF)
    cleaf[1] = (right + times_t(c0, wl[0, 0, 1], wl[1, 0, 1])).astype(BF)


def shadow_2(pos, order, keep, w, x, d, b, bl, wl, q_mine, got0, own, part, cleaf):
    put(own, lift(rows(keep), w, pos, 2))
    direct(order, 1, x, d, part)
    leaf_coupled(pos, q_mine, got0, b, bl, wl, cleaf)


def shadow_3(pos, q3, w, b, bl, wl, q_other, got0_other, keep2, got2, own, cleaf, c2, c2_oth):
    put(own, lift(rows(q3), w, pos, 3))
    put(c2, couple(rows(got2), b, pos, 2))
    put(c2_oth, couple(rows(keep2), b, pos, 2, 1))
    leaf_coupled(pos, q_other, got0_other, b, bl, wl, cleaf)


def set_base(pos, order, part, r, cleaf, parts, base):
    n = base.shape[2]
    size = r.shape[2]
    first = order[0, 0]
    lanes = half_lanes(side(pos, 0) ^ part, n)
    for block, direct_part in enumerate(parts):
        leaf = first ^ block
        add = dot(jnp.concatenate([r[0, leaf], r[1, leaf]], axis=1), widen(cleaf[leaf]), NT)
        for c in range(2):
            base[c, pl.ds(block * size, size)] = (
                direct_part[c, :, lanes] + add[:, c * n : (c + 1) * n]
            )


def shadow_4(pos, order, q4, got3, w, b, r, cleaf, part_0, part_1, own, top, base):
    put(own, lift(rows(q4), w, pos, 4))
    put(top, couple(rows(got3), b, pos, 3))
    set_base(pos, order, 0, r, cleaf, (part_0, part_1), base)


def product(r, paths, leaf, out):
    put(out, times(rows(r.at[:, leaf]), paths[leaf, 0], paths[leaf, 1]))


def shadow_5(pos, q5, got4, w, b, r, paths, top, own, top_out, path, g):
    put(own, lift(rows(q5), w, pos, 5))
    c4 = couple(rows(got4), b, pos, 4).astype(BF)
    put(top_out, rows(top) + lower(c4, w, pos, 3))
    put(path, lift(stack(w, 3, bit(pos, 3)), w, pos, 4))
    product(r, paths, 0, g)


def shadow_6(pos, q6, got5, w, b, top, path, own, top_out, path_6, path_8):
    put(own, lift(rows(q6), w, pos, 6))
    c5 = couple(rows(got5), b, pos, 5).astype(BF)
    put(top_out, rows(top) + times_t(c5, path[0], path[1]))
    longer = lift(rows(path), w, pos, 5).astype(BF)
    put(path_6, longer)
    put(path_8, couple_path(lift(longer, w, pos, 6).astype(BF), b, pos))


def shadow_7(pos, got6, w, b, top, path_6, path_8, c2, c2_oth, const, const_oth, path, path_oth):
    c6 = couple(rows(got6), b, pos, 6).astype(BF)
    h = (rows(top) + times_t(c6, path_6[0], path_6[1])).astype(BF)
    put(const, rows(c2) + lower(h, w, pos, 2))
    put(const_oth, rows(c2_oth) + lower(h, w, pos, 2, 1))
    for flip, out in enumerate((path, path_oth)):
        put(out, times(stack(w, 2, bit(pos, 2) ^ flip), path_8[0], path_8[1]))


def couple_path(path, b, pos):
    return lax.cond(
        bit(pos, 7) == 0,
        lambda: times(path, b[0, 7], b[1, 7]),
        lambda: times_t(path, b[0, 7], b[1, 7]),
    )


def top_kernel(pos, got, const, const_oth, path, path_oth, own, send):
    q = widen(rows(got))
    put(send, rows(const_oth) + dot(q, jnp.concatenate([path_oth[0], path_oth[1]], axis=1), NT))
    put(own, rows(const) + dot(q, jnp.concatenate([path[0], path[1]], axis=1), NT))


def shadow_8(pos, mine, keep1, got1, b, r, paths, c1, c1_oth, g):
    product(r, paths, 1, g)
    put(c1, couple(rows(got1), b, pos, 1))
    put(c1_oth, couple(rows(keep1), b, pos, 1, 1))


def down_kernel(pos, mine, got, c_own, c_oth, w, own, send):
    h = join(mine, got, side(pos, 2))
    put(send, rows(c_oth) + lower(h, w, pos, 1, 1))
    put(own, rows(c_own) + lower(h, w, pos, 1))


def shadow_9(pos, order, mine, r, cleaf, part_0, part_1, base):
    set_base(pos, order, 1, r, cleaf, (part_0, part_1), base)


def finish(pos, order, mine, got, base, gs, out, tile):
    hw = widen(join(mine, got, side(pos, 1))).T
    n = base.shape[2]
    for leaf, g in enumerate(gs):
        size = g.shape[1]
        for step in range(size // tile):
            here = pl.ds(step * tile, tile)
            start = (order[0, 0] ^ leaf) * size + step * tile
            at = pl.ds(pl.multiple_of(start, tile), tile)
            add = dot(jnp.concatenate([g[0, here], g[1, here]], axis=1), hw)
            for c in range(2):
                out[leaf, c, here] = (base[c, at] + add[:, c * n : (c + 1) * n]).astype(BF)
            yield leaf, here, at


def own_kernel(pos, order, mine, got, base, g0, g1, out):
    for _ in finish(pos, order, mine, got, base, (g0, g1), out, g0.shape[1]):
        pass


def last_kernel(pos, order, mine, got, base, g0, g1, done, out, buf, sems):
    size = g0.shape[1]
    n = base.shape[2]
    copies = []

    def store(src, part, at):
        lanes = half_lanes(side(pos, 0) ^ part, n)
        sem = sems.at[len(copies)]
        copies.append(pltpu.make_async_copy(src, out.at[:, at, lanes], sem))
        copies[-1].start()

    for leaf in range(2):
        at = pl.ds(pl.multiple_of((order[0, 0] ^ leaf) * size, size), size)
        store(done.at[leaf], 0, at)
    for leaf, here, at in finish(pos, order, mine, got, base, (g0, g1), buf, size):
        store(buf.at[leaf, :, here], 1, at)
    for copy in copies:
        copy.wait()


VMEM = pl.BlockSpec(memory_space=pltpu.VMEM)
SMEM = pl.BlockSpec(memory_space=pltpu.SMEM)
HBM = pl.BlockSpec(memory_space=pltpu.HBM)
GRANT = 20 * 2**20


def call(name, kernel, ins, outs, *args, scratch=(), flops=0, out_spec=VMEM):
    specs = {"s": SMEM, "v": VMEM, "h": HBM}
    moved = sum(a.size * a.dtype.itemsize for a in args)
    return pl.pallas_call(
        kernel,
        out_shape=[jax.ShapeDtypeStruct(shape, dtype) for shape, dtype in outs],
        in_specs=[specs[kind] for kind in ins],
        out_specs=[out_spec] * len(outs),
        scratch_shapes=list(scratch),
        compiler_params=pltpu.CompilerParams(vmem_limit_bytes=GRANT),
        cost_estimate=pl.CostEstimate(flops=flops, bytes_accessed=moved, transcendentals=0),
        name=name,
    )(*args)


def shards(rhs, diag, row_basis, col_basis, wl, bl, cross_w, cross_b, order):
    n = rhs.shape[2]
    rank = col_basis.shape[3]
    size = col_basis.shape[2]
    axes = ("leaf", "top")
    devices = lax.axis_size("leaf") * lax.axis_size("top")
    pos = lax.axis_index(axes).astype(jnp.int32).reshape(1)
    w = cross_w[:, 0]
    b = cross_b[:, 0]

    def swap(value, flip):
        return lax.ppermute(value, axes, [(i, i ^ flip) for i in range(devices)])

    def block(columns, dtype=BF):
        return ((2, columns, rank), dtype)

    mac = 8 * rank * rank
    half, quarter, eighth = n // 2, n // 4, n // 8
    qleaf_shape = ((2, n, rank), BF)
    hbm = [pltpu.with_memory_space_constraint(a, pltpu.HBM) for a in (order, rhs, col_basis, wl, w)]
    q_other, send, xt, x, u, wl, w0 = call(
        "send_half", send_kernel, "shhhhh",
        [qleaf_shape, block(half), ((2, n, size), BF), (rhs.shape, BF), (col_basis.shape, BF),
         (wl.shape, BF), ((2, 1, 2, rank, rank), BF)],
        pos, *hbm,
        scratch=(
            pltpu.SMEM(order.shape, jnp.int32),
            pltpu.VMEM((2, n, size), BF),
            pltpu.SemaphoreType.DMA((7,)),
        ),
        flops=mac * n * 3,
    )
    got0 = swap(send, 1)
    q_mine, keep0 = call(
        "keep_half", keep_kernel, "ssvvv", [qleaf_shape, block(half)],
        pos, order, xt, u, wl, flops=mac * n * 3,
    )
    keep1, send = call(
        "climb_0", first_climb, "svvv", [block(quarter), block(quarter)],
        pos, got0, keep0, w0, flops=mac * n,
    )
    got1 = swap(send, 3)
    keep0, keep1 = lax.optimization_barrier((keep0, keep1))
    got0_other = swap(keep0, 1)
    own, part_0, paths = call(
        "shadow_1", shadow_1, "ss" + "v" * 6,
        [block(quarter, F32), ((2, size, n), F32), ((2, 2, rank, rank), BF)],
        pos, order, keep1, w, w0, wl, x, diag, flops=mac * n * 7,
    )

    def climb(level, got, own):
        return call(
            "climb_%d" % level, climb_kernel(level), "svvv", [block(eighth)],
            pos, got, own, w, flops=mac * eighth,
        )[0]

    keep2, send = call(
        "climb_1", climb_kernel(1), "svvv", [block(eighth), block(eighth)],
        pos, got1, own, w, flops=mac * quarter,
    )
    got2 = swap(send, 5)
    cleaf_shape = ((2, n, rank), BF)
    top_shape = block(eighth, F32)
    own, part_1, cleaf = call(
        "shadow_2", shadow_2, "ss" + "v" * 9, [top_shape, ((2, size, n), F32), cleaf_shape],
        pos, order, keep2, w, x, diag, b, bl, wl, q_mine, got0, flops=mac * n * 8,
    )
    base_shape = ((2, 2 * size, half), F32)
    q3 = climb(2, got2, own)
    got3 = swap(q3, 13)
    own, cleaf_other, c2, c2_oth = call(
        "shadow_3", shadow_3, "s" + "v" * 9, [top_shape, cleaf_shape, top_shape, top_shape],
        pos, q3, w, b, bl, wl, q_other, got0_other, keep2, got2, flops=mac * n * 4,
    )
    q4 = climb(3, got3, own)
    got4 = swap(q4, 17)
    own, top, base = call(
        "shadow_4", shadow_4, "ss" + "v" * 8,
        [top_shape, top_shape, base_shape],
        pos, order, q4, got3, w, b, row_basis, cleaf, part_0, part_1, flops=mac * n * 2,
    )
    q5 = climb(4, got4, own)
    got5 = swap(q5, 49)
    own, top, path, g0 = call(
        "shadow_5", shadow_5, "s" + "v" * 7,
        [top_shape, top_shape, block(rank), block(size)],
        pos, q5, got4, w, b, row_basis, paths, top, flops=mac * n * 3,
    )
    q6 = climb(5, got5, own)
    got6 = swap(q6, 65)
    own, top, path_6, path_8 = call(
        "shadow_6", shadow_6, "s" + "v" * 6, [top_shape, top_shape, block(rank), block(rank)],
        pos, q6, got5, w, b, top, path, flops=mac * n * 3,
    )
    q7 = climb(6, got6, own)
    got7 = swap(q7, 193)
    const, const_oth, path, path_oth = call(
        "shadow_7", shadow_7, "s" + "v" * 8,
        [top_shape, top_shape, block(rank), block(rank)],
        pos, got6, w, b, top, path_6, path_8, c2, c2_oth, flops=mac * n * 3,
    )
    mine, send = call(
        "top", top_kernel, "s" + "v" * 5, [block(eighth), block(eighth)],
        pos, got7, const, const_oth, path, path_oth, flops=mac * eighth * 2,
    )
    got = swap(send, 5)
    c1, c1_oth, g1 = call(
        "shadow_8", shadow_8, "s" + "v" * 6,
        [block(quarter, F32), block(quarter, F32), block(size)],
        pos, mine, keep1, got1, b, row_basis, paths, flops=mac * n * 2,
    )
    mine, send = call(
        "down", down_kernel, "s" + "v" * 5, [block(quarter), block(quarter)],
        pos, mine, got, c1, c1_oth, w, flops=mac * quarter * 2,
    )
    got = swap(send, 3)
    (base_other,) = call(
        "shadow_9", shadow_9, "ss" + "v" * 5, [base_shape],
        pos, order, mine, row_basis, cleaf_other, part_0, part_1, flops=mac * n * 2,
    )
    late, base_other = lax.optimization_barrier((mine, base_other))
    mine_other = swap(late, 1)
    got_other = swap(got, 1)
    piece = (2, 2, size, half)
    (done,) = call(
        "own_columns", own_kernel, "ss" + "v" * 5, [(piece, BF)],
        pos, order, mine, got, base, g0, g1, flops=mac * n * 2,
    )
    (out,) = call(
        "other_columns", last_kernel, "ss" + "v" * 6, [(rhs.shape, BF)],
        pos, order, mine_other, got_other, base_other, g0, g1, done,
        scratch=(pltpu.VMEM(piece, BF), pltpu.SemaphoreType.DMA((6,))),
        flops=mac * n * 2, out_spec=HBM,
    )
    return out


def solution(mesh):
    return jax.shard_map(
        shards,
        mesh=mesh,
        in_specs=(
            P(None, ("leaf", "top"), None),
            P(None, ("leaf", "top"), None, None),
            P(None, ("leaf", "top"), None, None),
            P(None, ("leaf", "top"), None, None),
            P(None, ("leaf", "top"), None, None, None),
            P(None, ("leaf", "top"), None, None),
            P(None, ("leaf", "top"), None, None, None, None),
            P(None, ("leaf", "top"), None, None, None),
            P(("leaf", "top"), None),
        ),
        out_specs=P(None, ("leaf", "top"), None),
        check_vma=False,
    )
```

```python
import jax
import jax.numpy as jnp
from jax import lax
from jax.experimental import pallas as pl
from jax.experimental.pallas import tpu as pltpu
from jax.sharding import PartitionSpec as P

BF = jnp.bfloat16
F32 = jnp.float32
NN = (((1,), (0,)), ((), ()))
NT = (((1,), (1,)), ((), ()))


def dot(a, b, dims=NN):
    return lax.dot_general(a, b, dims, preferred_element_type=F32)


def widen(a):
    half = a.shape[0] // 2
    re, im = a[:half], a[half:]
    return jnp.concatenate(
        [jnp.concatenate([re, -im], axis=1), jnp.concatenate([im, re], axis=1)], axis=0
    )


def times(a, w_re, w_im):
    return dot(widen(a), jnp.concatenate([w_re, w_im], axis=0))


def times_t(a, w_re, w_im):
    return dot(widen(a), jnp.concatenate([w_re, w_im], axis=1), NT)


def rows(ref):
    return jnp.concatenate([ref[0], ref[1]], axis=0)


def put(ref, value):
    half = value.shape[0] // 2
    ref[0] = value[:half].astype(ref.dtype)
    ref[1] = value[half:].astype(ref.dtype)


def bit(pos, level):
    return (pos[0] >> level) & 1


def lift(q, w, pos, level, flip=0):
    child = bit(pos, level) ^ flip
    return times(q, w[0, level, child], w[1, level, child])


def lower(h, w, pos, level, flip=0):
    child = bit(pos, level) ^ flip
    return times_t(h, w[0, level, child], w[1, level, child])


def couple(q, b, pos, level, flip=0):
    return lax.cond(
        (bit(pos, level) ^ flip) == 0,
        lambda: times_t(q, b[0, level], b[1, level]),
        lambda: times(q, b[0, level], b[1, level]),
    )


def split(value, side, keep, send):
    half = value.shape[0] // 2
    part = half // 2
    for c in range(2):
        low = value[c * half : c * half + part]
        high = value[c * half + part : (c + 1) * half]
        keep[c] = jnp.where(side == 0, low, high)
        send[c] = jnp.where(side == 0, high, low)


def join(own, got, side):
    parts = []
    for c in range(2):
        parts.append(jnp.where(side == 0, own[c], got[c]))
        parts.append(jnp.where(side == 0, got[c], own[c]))
    return jnp.concatenate(parts, axis=0)


def side(pos, level):
    if level == 0:
        return (pos[0] ^ (pos[0] >> 1) ^ (pos[0] >> 2) ^ (pos[0] >> 4) ^ (pos[0] >> 6)) & 1
    if level == 1:
        return bit(pos, 1)
    return bit(pos, 2) ^ bit(pos, 3)


def half_lanes(half, n):
    return pl.ds(pl.multiple_of(half * n, n), n)


def parent(qleaf, wl):
    pair = jnp.concatenate([widen(qleaf[0]), widen(qleaf[1])], axis=1)
    mats = jnp.concatenate([wl[0, 0, 0], wl[1, 0, 0], wl[0, 0, 1], wl[1, 0, 1]], axis=0)
    return dot(pair, mats).astype(BF)


def send_kernel(pos, order, x, u, wl, w, qleaf, send, xt, x_v, u_v, wl_v, w0, order_s, xs, sems):
    size = u.shape[2]
    half = x.shape[2] // 2

    def x_copy(block):
        at = pl.ds(block * size, size)
        return pltpu.make_async_copy(x.at[:, at], x_v.at[:, at], sems.at[block])

    def u_copy(leaf):
        return pltpu.make_async_copy(u.at[:, leaf], u_v.at[:, leaf], sems.at[2 + leaf])

    order_copy = pltpu.make_async_copy(order, order_s, sems.at[4])
    wl_copy = pltpu.make_async_copy(wl, wl_v, sems.at[5])
    w_copy = pltpu.make_async_copy(w.at[:, 0], w0.at[:, 0], sems.at[6])
    x_copy(0).start()
    x_copy(1).start()
    order_copy.start()
    u_copy(0).start()
    u_copy(1).start()
    wl_copy.start()
    w_copy.start()
    keep = side(pos, 0)
    for block in range(2):
        x_copy(block).wait()
        at = pl.ds(block * size, size)
        for out, which in ((xs, 1 - keep), (xt, keep)):
            lanes = half_lanes(which, half)
            out[block, :half] = x_v[0, at, lanes].T
            out[block, half:] = x_v[1, at, lanes].T
    order_copy.wait()
    for leaf in range(2):
        u_copy(leaf).wait()
        block = order_s[0, leaf]
        qleaf[leaf] = times(xs[block], u_v[0, leaf], u_v[1, leaf]).astype(BF)
    wl_copy.wait()
    put(send, parent(qleaf, wl_v))
    w_copy.wait()


def keep_kernel(pos, order, xt, u, wl, qleaf, keep):
    for leaf in range(2):
        block = order[0, leaf]
        qleaf[leaf] = times(xt[block], u[0, leaf], u[1, leaf]).astype(BF)
    put(keep, parent(qleaf, wl))


def first_climb(pos, got, q, w, keep, send):
    c = bit(pos, 0)
    pair = jnp.concatenate([widen(rows(q)), widen(rows(got))], axis=1)
    mats = jnp.concatenate([w[0, 0, c], w[1, 0, c], w[0, 0, 1 - c], w[1, 0, 1 - c]], axis=0)
    split(dot(pair, mats).astype(BF), side(pos, 1), keep, send)


def climb_kernel(level):
    def kernel(pos, got, own, w, *outs):
        q = (rows(own) + lift(rows(got), w, pos, level, 1)).astype(BF)
        if len(outs) == 2:
            split(q, side(pos, level + 1), *outs)
        else:
            put(outs[0], q)

    return kernel


def direct(order, block, x, d, out):
    size = d.shape[2]
    leaf = order[0, 0] ^ block
    at = pl.ds(block * size, size)
    xs = jnp.concatenate([x[0, at], x[1, at]], axis=0)
    re, im = d[0, leaf], d[1, leaf]
    out[0] = dot(jnp.concatenate([re, -im], axis=1), xs)
    out[1] = dot(jnp.concatenate([im, re], axis=1), xs)


def stack(w, level, child):
    return jnp.concatenate([w[0, level, child], w[1, level, child]], axis=0)


def shadow_1(pos, order, keep, w, w0, wl, x, d, own, part, paths):
    put(own, lift(rows(keep), w, pos, 1))
    for leaf in range(2):
        put(paths.at[leaf], lift(stack(wl, 0, leaf), w0, pos, 0))
    direct(order, 0, x, d, part)


def leaf_coupled(pos, q, got, b, bl, wl, cleaf):
    c0 = couple(rows(got), b, pos, 0).astype(BF)
    left = times_t(q[1], bl[0, 0], bl[1, 0])
    right = times(q[0], bl[0, 0], bl[1, 0])
    cleaf[0] = (left + times_t(c0, wl[0, 0, 0], wl[1, 0, 0])).astype(BF)
    cleaf[1] = (right + times_t(c0, wl[0, 0, 1], wl[1, 0, 1])).astype(BF)


def shadow_2(pos, order, keep, w, x, d, b, bl, wl, q_mine, got0, own, part, cleaf):
    put(own, lift(rows(keep), w, pos, 2))
    direct(order, 1, x, d, part)
    leaf_coupled(pos, q_mine, got0, b, bl, wl, cleaf)


def shadow_3(pos, q3, w, b, bl, wl, q_other, got0_other, own, cleaf):
    put(own, lift(rows(q3), w, pos, 3))
    leaf_coupled(pos, q_other, got0_other, b, bl, wl, cleaf)


def set_base(pos, order, part, r, cleaf, parts, base):
    n = base.shape[2]
    size = r.shape[2]
    first = order[0, 0]
    lanes = half_lanes(side(pos, 0) ^ part, n)
    for block, direct_part in enumerate(parts):
        leaf = first ^ block
        add = dot(jnp.concatenate([r[0, leaf], r[1, leaf]], axis=1), widen(cleaf[leaf]), NT)
        for c in range(2):
            base[c, pl.ds(block * size, size)] = (
                direct_part[c, :, lanes] + add[:, c * n : (c + 1) * n]
            )


def shadow_4(pos, order, q4, got3, w, b, r, cleaf, part_0, part_1, own, top, base):
    put(own, lift(rows(q4), w, pos, 4))
    put(top, couple(rows(got3), b, pos, 3))
    set_base(pos, order, 0, r, cleaf, (part_0, part_1), base)


def product(r, paths, leaf, out):
    put(out, times(rows(r.at[:, leaf]), paths[leaf, 0], paths[leaf, 1]))


def shadow_5(pos, q5, got4, w, b, r, paths, top, own, top_out, path, g):
    put(own, lift(rows(q5), w, pos, 5))
    c4 = couple(rows(got4), b, pos, 4).astype(BF)
    put(top_out, rows(top) + lower(c4, w, pos, 3))
    put(path, lift(stack(w, 3, bit(pos, 3)), w, pos, 4))
    product(r, paths, 0, g)


def shadow_6(pos, q6, got5, w, b, r, paths, top, path, own, top_out, path_6, path_8, g):
    put(own, lift(rows(q6), w, pos, 6))
    c5 = couple(rows(got5), b, pos, 5).astype(BF)
    put(top_out, rows(top) + times_t(c5, path[0], path[1]))
    longer = lift(rows(path), w, pos, 5).astype(BF)
    put(path_6, longer)
    put(path_8, couple_path(lift(longer, w, pos, 6).astype(BF), b, pos))
    product(r, paths, 1, g)


def shadow_7(pos, got6, w, b, top, path_6, path_8, keep2, got2, const, const_oth, path, path_oth):
    c6 = couple(rows(got6), b, pos, 6).astype(BF)
    h = (rows(top) + times_t(c6, path_6[0], path_6[1])).astype(BF)
    put(const, couple(rows(got2), b, pos, 2) + lower(h, w, pos, 2))
    put(const_oth, couple(rows(keep2), b, pos, 2, 1) + lower(h, w, pos, 2, 1))
    for flip, out in enumerate((path, path_oth)):
        put(out, times(stack(w, 2, bit(pos, 2) ^ flip), path_8[0], path_8[1]))


def couple_path(path, b, pos):
    return lax.cond(
        bit(pos, 7) == 0,
        lambda: times(path, b[0, 7], b[1, 7]),
        lambda: times_t(path, b[0, 7], b[1, 7]),
    )


def top_kernel(pos, got, const, const_oth, path, path_oth, own, send):
    q = widen(rows(got))
    put(send, rows(const_oth) + dot(q, jnp.concatenate([path_oth[0], path_oth[1]], axis=1), NT))
    put(own, rows(const) + dot(q, jnp.concatenate([path[0], path[1]], axis=1), NT))


def shadow_8(pos, mine, keep1, got1, b, c1, c1_oth):
    put(c1, couple(rows(got1), b, pos, 1))
    put(c1_oth, couple(rows(keep1), b, pos, 1, 1))


def down_kernel(pos, mine, got, c_own, c_oth, w, own, send):
    h = join(mine, got, side(pos, 2))
    put(send, rows(c_oth) + lower(h, w, pos, 1, 1))
    put(own, rows(c_own) + lower(h, w, pos, 1))


def shadow_9(pos, order, mine, r, cleaf, part_0, part_1, base):
    set_base(pos, order, 1, r, cleaf, (part_0, part_1), base)


def finish(pos, order, mine, got, base, gs, out, tile):
    hw = widen(join(mine, got, side(pos, 1)))
    n = base.shape[2]
    for leaf, g in enumerate(gs):
        size = g.shape[1]
        for step in range(size // tile):
            here = pl.ds(step * tile, tile)
            start = (order[0, 0] ^ leaf) * size + step * tile
            at = pl.ds(pl.multiple_of(start, tile), tile)
            add = dot(jnp.concatenate([g[0, here], g[1, here]], axis=1), hw, NT)
            for c in range(2):
                out[leaf, c, here] = (base[c, at] + add[:, c * n : (c + 1) * n]).astype(BF)
                yield leaf, c, here, at


def own_kernel(pos, order, mine, got, base, g0, g1, out):
    for _ in finish(pos, order, mine, got, base, (g0, g1), out, g0.shape[1]):
        pass


def last_kernel(pos, order, mine, got, base, g0, g1, done, out, buf, sems):
    size = g0.shape[1]
    n = base.shape[2]
    copies = []

    def store(src, part, c, at):
        lanes = half_lanes(side(pos, 0) ^ part, n)
        sem = sems.at[len(copies)]
        copies.append(pltpu.make_async_copy(src, out.at[c, at, lanes], sem))
        copies[-1].start()

    for leaf in range(2):
        at = pl.ds(pl.multiple_of((order[0, 0] ^ leaf) * size, size), size)
        for c in range(2):
            store(done.at[leaf, c], 0, c, at)
    for leaf, c, here, at in finish(pos, order, mine, got, base, (g0, g1), buf, size):
        store(buf.at[leaf, c, here], 1, c, at)
    for copy in copies:
        copy.wait()


VMEM = pl.BlockSpec(memory_space=pltpu.VMEM)
SMEM = pl.BlockSpec(memory_space=pltpu.SMEM)
HBM = pl.BlockSpec(memory_space=pltpu.HBM)
GRANT = 20 * 2**20


def call(name, kernel, ins, outs, *args, scratch=(), flops=0, out_spec=VMEM):
    specs = {"s": SMEM, "v": VMEM, "h": HBM}
    moved = sum(a.size * a.dtype.itemsize for a in args)
    return pl.pallas_call(
        kernel,
        out_shape=[jax.ShapeDtypeStruct(shape, dtype) for shape, dtype in outs],
        in_specs=[specs[kind] for kind in ins],
        out_specs=[out_spec] * len(outs),
        scratch_shapes=list(scratch),
        compiler_params=pltpu.CompilerParams(vmem_limit_bytes=GRANT),
        cost_estimate=pl.CostEstimate(flops=flops, bytes_accessed=moved, transcendentals=0),
        name=name,
    )(*args)


def shards(rhs, diag, row_basis, col_basis, wl, bl, cross_w, cross_b, order):
    n = rhs.shape[2]
    rank = col_basis.shape[3]
    size = col_basis.shape[2]
    axes = ("leaf", "top")
    devices = lax.axis_size("leaf") * lax.axis_size("top")
    pos = lax.axis_index(axes).astype(jnp.int32).reshape(1)
    w = cross_w[:, 0]
    b = cross_b[:, 0]

    def swap(value, flip):
        return lax.ppermute(value, axes, [(i, i ^ flip) for i in range(devices)])

    def block(columns, dtype=BF):
        return ((2, columns, rank), dtype)

    mac = 8 * rank * rank
    half, quarter, eighth = n // 2, n // 4, n // 8
    qleaf_shape = ((2, n, rank), BF)
    hbm = [pltpu.with_memory_space_constraint(a, pltpu.HBM) for a in (order, rhs, col_basis, wl, w)]
    q_other, send, xt, x, u, wl, w0 = call(
        "send_half", send_kernel, "shhhhh",
        [qleaf_shape, block(half), ((2, n, size), BF), (rhs.shape, BF), (col_basis.shape, BF),
         (wl.shape, BF), ((2, 1, 2, rank, rank), BF)],
        pos, *hbm,
        scratch=(
            pltpu.SMEM(order.shape, jnp.int32),
            pltpu.VMEM((2, n, size), BF),
            pltpu.SemaphoreType.DMA((7,)),
        ),
        flops=mac * n * 3,
    )
    got0 = swap(send, 1)
    q_mine, keep0 = call(
        "keep_half", keep_kernel, "ssvvv", [qleaf_shape, block(half)],
        pos, order, xt, u, wl, flops=mac * n * 3,
    )
    keep1, send = call(
        "climb_0", first_climb, "svvv", [block(quarter), block(quarter)],
        pos, got0, keep0, w0, flops=mac * n,
    )
    got1 = swap(send, 3)
    keep0, keep1 = lax.optimization_barrier((keep0, keep1))
    got0_other = swap(keep0, 1)
    own, part_0, paths = call(
        "shadow_1", shadow_1, "ss" + "v" * 6,
        [block(quarter, F32), ((2, size, n), F32), ((2, 2, rank, rank), BF)],
        pos, order, keep1, w, w0, wl, x, diag, flops=mac * n * 7,
    )

    def climb(level, got, own):
        return call(
            "climb_%d" % level, climb_kernel(level), "svvv", [block(eighth)],
            pos, got, own, w, flops=mac * eighth,
        )[0]

    keep2, send = call(
        "climb_1", climb_kernel(1), "svvv", [block(eighth), block(eighth)],
        pos, got1, own, w, flops=mac * quarter,
    )
    got2 = swap(send, 5)
    cleaf_shape = ((2, n, rank), BF)
    top_shape = block(eighth, F32)
    own, part_1, cleaf = call(
        "shadow_2", shadow_2, "ss" + "v" * 9, [top_shape, ((2, size, n), F32), cleaf_shape],
        pos, order, keep2, w, x, diag, b, bl, wl, q_mine, got0, flops=mac * n * 8,
    )
    base_shape = ((2, 2 * size, half), F32)
    q3 = climb(2, got2, own)
    got3 = swap(q3, 13)
    own, cleaf_other = call(
        "shadow_3", shadow_3, "s" + "v" * 7, [top_shape, cleaf_shape],
        pos, q3, w, b, bl, wl, q_other, got0_other, flops=mac * n * 4,
    )
    q4 = climb(3, got3, own)
    got4 = swap(q4, 17)
    own, top, base = call(
        "shadow_4", shadow_4, "ss" + "v" * 8,
        [top_shape, top_shape, base_shape],
        pos, order, q4, got3, w, b, row_basis, cleaf, part_0, part_1, flops=mac * n * 2,
    )
    q5 = climb(4, got4, own)
    got5 = swap(q5, 49)
    own, top, path, g0 = call(
        "shadow_5", shadow_5, "s" + "v" * 7,
        [top_shape, top_shape, block(rank), block(size)],
        pos, q5, got4, w, b, row_basis, paths, top, flops=mac * n * 3,
    )
    q6 = climb(5, got5, own)
    got6 = swap(q6, 65)
    own, top, path_6, path_8, g1 = call(
        "shadow_6", shadow_6, "s" + "v" * 8,
        [top_shape, top_shape, block(rank), block(rank), block(size)],
        pos, q6, got5, w, b, row_basis, paths, top, path, flops=mac * n * 4,
    )
    q7 = climb(6, got6, own)
    got7 = swap(q7, 193)
    const, const_oth, path, path_oth = call(
        "shadow_7", shadow_7, "s" + "v" * 8,
        [top_shape, top_shape, block(rank), block(rank)],
        pos, got6, w, b, top, path_6, path_8, keep2, got2, flops=mac * n * 3,
    )
    mine, send = call(
        "top", top_kernel, "s" + "v" * 5, [block(eighth), block(eighth)],
        pos, got7, const, const_oth, path, path_oth, flops=mac * eighth * 2,
    )
    got = swap(send, 5)
    c1, c1_oth = call(
        "shadow_8", shadow_8, "s" + "v" * 4, [block(quarter, F32), block(quarter, F32)],
        pos, mine, keep1, got1, b, flops=mac * half,
    )
    mine, send = call(
        "down", down_kernel, "s" + "v" * 5, [block(quarter), block(quarter)],
        pos, mine, got, c1, c1_oth, w, flops=mac * quarter * 2,
    )
    got = swap(send, 3)
    (base_other,) = call(
        "shadow_9", shadow_9, "ss" + "v" * 5, [base_shape],
        pos, order, mine, row_basis, cleaf_other, part_0, part_1, flops=mac * n * 2,
    )
    late, base_other = lax.optimization_barrier((mine, base_other))
    mine_other = swap(late, 1)
    got_other = swap(got, 1)
    piece = (2, 2, size, half)
    (done,) = call(
        "own_columns", own_kernel, "ss" + "v" * 5, [(piece, BF)],
        pos, order, mine, got, base, g0, g1, flops=mac * n * 2,
    )
    (out,) = call(
        "other_columns", last_kernel, "ss" + "v" * 6, [(rhs.shape, BF)],
        pos, order, mine_other, got_other, base_other, g0, g1, done,
        scratch=(pltpu.VMEM(piece, BF), pltpu.SemaphoreType.DMA((8,))),
        flops=mac * n * 2, out_spec=HBM,
    )
    return out


def solution(mesh):
    return jax.shard_map(
        shards,
        mesh=mesh,
        in_specs=(
            P(None, ("leaf", "top"), None),
            P(None, ("leaf", "top"), None, None),
            P(None, ("leaf", "top"), None, None),
            P(None, ("leaf", "top"), None, None),
            P(None, ("leaf", "top"), None, None, None),
            P(None, ("leaf", "top"), None, None),
            P(None, ("leaf", "top"), None, None, None, None),
            P(None, ("leaf", "top"), None, None, None),
            P(("leaf", "top"), None),
        ),
        out_specs=P(None, ("leaf", "top"), None),
        check_vma=False,
    )
```
